32 devices in a mesh: seq: 16 (over z, y, core), mlp: 2 (over x).
Axes of the slice: x: 2, y: 2, z: 4, core: 2. Of those that a mesh axis runs over, the one named last changes fastest.
Arguments:
- frames: bfloat16 [32768, 512], P(('seq', 'mlp')), may hold values from -6 to 6
- cotangent: bfloat16 [32768, 512], P(('seq', 'mlp')), may hold values from -6 to 6
- lengths: int32 [36], replicated, may hold values from 200 to 2304, as said below
- owners: int32 [16], replicated, may hold values from 0 to 15, as said below
- attn_master: float32 [32, 128, 512], P('seq')
- attn_first: float32 [32, 128, 512], P('seq'), may hold values from -64 to 64
- attn_second: float32 [32, 128, 512], P('seq'), may hold values from 8.192 to 32.768
- attn_average: float32 [32, 128, 512], P('seq'), may hold values from -1 to 1
- small_master: float32 [17, 512], replicated
- small_first: float32 [17, 512], replicated, may hold values from -128 to 128
- small_second: float32 [17, 512], replicated, may hold values from 32.768 to 131.072
- small_average: float32 [17, 512], replicated, may hold values from -3 to 3
- mlp_master: float32 [2, 512, 2048], P(None, None, 'mlp'), may hold values from -0.25 to 0.25
- mlp_first: float32 [2, 512, 2048], P(None, None, 'mlp'), may hold values from -48 to 48
- mlp_second: float32 [2, 512, 2048], P(None, None, 'mlp'), may hold values from 5.24288 to 20.97152
- mlp_average: float32 [2, 512, 2048], P(None, None, 'mlp'), may hold values from -0.25 to 0.25
- bias_master: float32 [2048], P('mlp'), may hold values from -3 to 3
- bias_first: float32 [2048], P('mlp'), may hold values from -32 to 32
- bias_second: float32 [2048], P('mlp'), may hold values from 2.94912 to 11.79648
- bias_average: float32 [2048], P('mlp'), may hold values from -3 to 3
Outputs:
- output: bfloat16 [32768, 512], P(('seq', 'mlp'))
- in_grad: bfloat16 [32768, 512], P(('seq', 'mlp'))
- attn_weights: float32 [32, 128, 512], P('seq')
- attn_moment: float32 [32, 128, 512], P('seq')
- attn_square: float32 [32, 128, 512], P('seq')
- attn_mean: float32 [32, 128, 512], P('seq')
- small_weights: float32 [17, 512], replicated
- small_moment: float32 [17, 512], replicated
- small_square: float32 [17, 512], replicated
- small_mean: float32 [17, 512], replicated
- mlp_weights: float32 [2, 512, 2048], P(None, None, 'mlp')
- mlp_moment: float32 [2, 512, 2048], P(None, None, 'mlp')
- mlp_square: float32 [2, 512, 2048], P(None, None, 'mlp')
- mlp_mean: float32 [2, 512, 2048], P(None, None, 'mlp')
- bias_weights: float32 [2048], P('mlp')
- bias_moment: float32 [2048], P('mlp')
- bias_square: float32 [2048], P('mlp')
- bias_mean: float32 [2048], P('mlp')
The draws below stay inside these ranges and needn't reach their ends.
Inputs may be any that keep to these rules, and one draw needn't show every extreme that they name: `lengths`: videos lie end to end from frame 0 in this order; their total falls within the last 1024 frames, at least 8 short of 32768. `owners`: no owner holds more than 2 tiles, and some owner holds exactly 2.
All inputs are finite; a program needn't handle non-finite values.
Results may differ from the reference program's by a relative error of at most 0.014.
Values may be sent and summed in bfloat16 or wider, within the bound.
No kernel may reach another device: no remote copies, remote signals or barrier semaphores. Data moves between devices by JAX's collectives and lax.ppermute only.
A program may use at most 192 MiB of HBM per device.

```python
import math
import jax
import jax.numpy as jnp
from jax import lax

D = 512
HEADS = 4
HEAD = 128
FF = 2048
HALF = 9
TOK_DEV = 1024
TOKENS = 32768
LMIN = 200
LMAX = 2304
NVID = 36
TILE = 128
TILES = 16
CAP = 2
NSMALL = 17
STEP = 7
N_SEQ = 16


def owner_list(key):
    first, second = jax.random.split(key)
    order = jax.random.permutation(first, N_SEQ * CAP) // CAP
    score = jnp.where(order == order[0], 0, N_SEQ * CAP) + jnp.arange(N_SEQ * CAP)
    ranked = order[jnp.argsort(score)]
    return jax.random.permutation(second, ranked[:TILES]).astype(jnp.int32)


def draw_owners(key, part):
    return owner_list(key)


def draw_attn_master(key, part):
    owners = owner_list(key)
    key = jax.random.fold_in(key, 5)
    tiles = jnp.arange(TILES, dtype=jnp.int32)
    earlier = (owners[None, :] == owners[:, None]) & (tiles[None, :] < tiles[:, None])
    slots = owners * CAP + jnp.sum(earlier.astype(jnp.int32), axis=1)
    hits = slots[None, :] == jnp.arange(N_SEQ * CAP, dtype=jnp.int32)[:, None]
    matrix = jnp.sum(jnp.where(hits, tiles[None, :] // (TILES // 4), 0), axis=1)
    factor = jnp.where(matrix == 3, 3.5, jnp.where(matrix == 2, 1.0, 1.4)) * D ** (-0.5)
    shape = (N_SEQ * CAP, TILE, D)
    base = jax.random.normal(key, shape, jnp.float32)
    return (base * factor[:, None, None]).astype(jnp.float32)


def draw_small_master(key, part):
    key = jax.random.fold_in(key, 7)
    index = jnp.arange(NSMALL)
    gains = (index == 0) | (index == 2)
    spread = jnp.where(gains, 0.15, jnp.where(index >= 8, 0.5, 0.3))
    centre = jnp.where(gains, 1.0, 0.0)
    base = jax.random.normal(key, (NSMALL, D), jnp.float32)
    return (centre[:, None] + spread[:, None] * base).astype(jnp.float32)


def draw_lengths(key, part):
    key = jax.random.fold_in(key, 11)
    first, second, third = jax.random.split(key, 3)
    index = jnp.arange(NVID, dtype=jnp.int32)
    used = TOKENS - jax.random.randint(first, (), 8, TOK_DEV // 2)
    chosen = jax.random.randint(second, (), 0, NVID)
    picks = jax.random.randint(third, (NVID,), 1, 9)
    weight = jnp.where(index == chosen, 0, picks * picks * picks)
    rest = used - NVID * (LMIN + 1) - (LMAX - LMIN - 1)
    share = jnp.minimum(rest * weight // jnp.sum(weight), LMAX - LMIN - 4)
    left = rest - jnp.sum(share)
    share = share + ((index < left) & (index != chosen)).astype(jnp.int32)
    lengths = jnp.where(index == chosen, LMAX, LMIN + 1 + share)
    ends = jnp.cumsum(lengths)
    before_big = jnp.concatenate([index[1:] == chosen, jnp.zeros((1,), bool)])
    broken = (ends % TOK_DEV == 0) & (index < NVID - 1) & ~(before_big & (index != chosen))
    delta = jnp.where(broken, jnp.where(index == chosen, -1, 1), 0)
    moved = jnp.concatenate([jnp.zeros((1,), jnp.int32), delta[:-1]])
    return (lengths + delta - moved).astype(jnp.int32)


def shard_levels(key, dims, cuts, low, high):
    def one(position, parts):
        draws = jax.random.uniform(jax.random.fold_in(jax.random.fold_in(key, 6), position), (parts,), jnp.float32, low / len(cuts), high / len(cuts))
        return jnp.repeat(jnp.exp(draws), dims[position] // parts).reshape((-1,) + (1,) * (len(dims) - position - 1))

    level = one(*cuts[0])
    for cut in cuts[1:]:
        level = level * one(*cut)
    return level


def scatter_about(stream_key, shape, deviation, most, cuts=(), kind=jnp.bfloat16):
    loudness = shard_levels(stream_key, shape, cuts, -0.22, 0.18) if cuts else 1.0
    drawn = jax.random.normal(stream_key, shape, jnp.float32) * deviation * loudness
    return jnp.minimum(jnp.maximum(drawn, -most), most).astype(kind)


def setup_inputs(seed: int = 0) -> dict:
    splits = jax.random.split(jax.random.key(seed), 21)
    frames = scatter_about(splits[0], (TOKENS, D), 1.0, 6.0, ((0, 32),))
    cotangent = scatter_about(splits[1], (TOKENS, D), 1.0, 6.0, ((0, 32),))
    lengths = draw_lengths(jax.random.fold_in(splits[20], 71), 0)
    owners = draw_owners(jax.random.fold_in(splits[20], 71), 0)
    attn_master = draw_attn_master(jax.random.fold_in(splits[20], 71), 0)
    attn_first = scatter_about(splits[5], (N_SEQ * CAP, TILE, D), (0.055 * TOKENS ** 0.5), 64.0, ((0, 16),), jnp.float32)
    attn_second = jnp.clip(jnp.exp(math.log(32.768) - 1.3862944 * jax.random.uniform(splits[6], (N_SEQ * CAP, TILE, D), jnp.float32) ** shard_levels(splits[6], (N_SEQ * CAP, TILE, D), ((0, 16),), -0.2, 0.2)), 8.192, 32.768)
    attn_average = scatter_about(splits[7], (N_SEQ * CAP, TILE, D), (1.5 * D ** -0.5), 1.0, ((0, 16),), jnp.float32)
    small_master = draw_small_master(jax.random.fold_in(splits[20], 71), 0)
    small_first = scatter_about(splits[9], (NSMALL, D), (0.11 * TOKENS ** 0.5), 128.0, (), jnp.float32)
    small_second = jnp.clip(jnp.exp(jax.random.uniform(splits[10], (NSMALL, D), jnp.float32, math.log(32.768), math.log(131.072))), 32.768, 131.072)
    small_average = scatter_about(splits[11], (NSMALL, D), 0.5, 3.0, (), jnp.float32)
    mlp_master = scatter_about(splits[12], (2, D, FF), D ** -0.5, 0.25, ((2, 2),), jnp.float32)
    mlp_first = scatter_about(splits[13], (2, D, FF), (0.044 * TOKENS ** 0.5), 48.0, ((2, 2),), jnp.float32)
    mlp_second = jnp.clip(jnp.exp(math.log(20.97152) - 1.3862944 * jax.random.uniform(splits[14], (2, D, FF), jnp.float32) ** shard_levels(splits[14], (2, D, FF), ((2, 2),), -0.2, 0.2)), 5.24288, 20.97152)
    mlp_average = scatter_about(splits[15], (2, D, FF), D ** -0.5, 0.25, ((2, 2),), jnp.float32)
    bias_master = scatter_about(splits[16], (FF,), 0.5, 3.0, ((0, 2),), jnp.float32)
    bias_first = scatter_about(splits[17], (FF,), (0.033 * TOKENS ** 0.5), 32.0, ((0, 2),), jnp.float32)
    bias_second = jnp.clip(jnp.exp(math.log(11.79648) - 1.3862944 * jax.random.uniform(splits[18], (FF,), jnp.float32) ** shard_levels(splits[18], (FF,), ((0, 2),), -0.2, 0.2)), 2.94912, 11.79648)
    bias_average = scatter_about(splits[19], (FF,), 0.5, 3.0, ((0, 2),), jnp.float32)
    return dict(frames=frames, cotangent=cotangent, lengths=lengths, owners=owners, attn_master=attn_master, attn_first=attn_first, attn_second=attn_second, attn_average=attn_average, small_master=small_master, small_first=small_first, small_second=small_second, small_average=small_average, mlp_master=mlp_master, mlp_first=mlp_first, mlp_second=mlp_second, mlp_average=mlp_average, bias_master=bias_master, bias_first=bias_first, bias_second=bias_second, bias_average=bias_average)


@jax.custom_vjp
def low(v):
    return lax.optimization_barrier(v.astype(jnp.bfloat16)).astype(jnp.float32)

@jax.custom_vjp
def low_back(v):
    return v

def low_keep(v):
    return (low(v), None)

def low_pass(kept, grad):
    return (grad,)

def back_keep(v):
    return (v, None)

def back_low(kept, grad):
    return (low(grad),)
low.defvjp(low_keep, low_pass)
low_back.defvjp(back_keep, back_low)
HIGH = lax.Precision.HIGHEST
NORM_EPS = 1e-05
MASKED = -1e+30
BETA_ONE = 0.9
BETA_TWO = 0.999
ADAM_EPS = 1e-08
MATRIX_RATE = 0.03
MATRIX_DECAY = 0.05
SMALL_RATE = 0.3
AVERAGE_RATE = 0.8

def both(v):
    return low(low_back(v))

def product(left, right):
    return jnp.dot(left, right, precision=HIGH, preferred_element_type=jnp.float32)

def frame_tables(lengths, positions):
    ends = jnp.cumsum(lengths)
    video = lax.optimization_barrier(jnp.sum((positions[:, None] >= ends[None, :]).astype(jnp.int32), axis=1))
    valid = (positions >= 0) & (positions < ends[-1])
    return (video, valid)

def conv_keeps(video, valid):
    keep_prev = valid[1:-1] & valid[:-2] & (video[1:-1] == video[:-2])
    keep_after = valid[1:-1] & valid[2:] & (video[1:-1] == video[2:])
    return (keep_prev.astype(jnp.float32), keep_after.astype(jnp.float32))

def norm_rows(values, gain, bias):
    mean = lax.optimization_barrier(jnp.mean(values, axis=-1, keepdims=True))
    centred = values - mean
    spread = lax.optimization_barrier(jnp.mean(centred * centred, axis=-1, keepdims=True))
    return centred * lax.rsqrt(spread + NORM_EPS) * gain + bias

def conv_three(padded, taps, keep_prev, keep_after):
    before = padded[:-2] * keep_prev[:, None]
    middle = padded[1:-1]
    after = padded[2:] * keep_after[:, None]
    return taps[:, 0, None, :] * before + taps[:, 1, None, :] * middle + taps[:, 2, None, :] * after

def window_mask(query_pos, key_pos, query_video, key_video, query_valid, key_valid):
    offset = query_pos[:, None] - key_pos[None, :]
    band = jnp.abs(offset) <= HALF
    same = (query_video[:, None] == key_video[None, :]) & query_valid[:, None] & key_valid[None, :]
    return band & (same | (offset == 0))

def tile_slots(owners):
    index = jnp.arange(owners.shape[0], dtype=jnp.int32)
    earlier = (owners[None, :] == owners[:, None]) & (index[None, :] < index[:, None])
    return owners * CAP + lax.optimization_barrier(jnp.sum(earlier.astype(jnp.int32), axis=1))

def adamw(weight, grad, first, second, average, rate, decay):
    first_new = BETA_ONE * first + (1.0 - BETA_ONE) * grad
    second_new = BETA_TWO * second + (1.0 - BETA_TWO) * grad * grad
    ratio = first_new / (1.0 - BETA_ONE ** STEP) / (jnp.sqrt(second_new / (1.0 - BETA_TWO ** STEP)) + ADAM_EPS)
    weight_new = weight - rate * (ratio + decay * weight)
    average_new = AVERAGE_RATE * average + (1.0 - AVERAGE_RATE) * weight_new
    return (weight_new, first_new, second_new, average_new)

def attend(query, keys, values, video, valid):
    block = min(512, TOK_DEV)
    span = block + 2 * HALF
    scale = HEAD ** (-0.5)
    pad_rows = jnp.zeros((HALF, D), jnp.float32)
    keys_pad = jnp.concatenate([pad_rows, keys, pad_rows]).reshape(-1, HEADS, HEAD)
    values_pad = jnp.concatenate([pad_rows, values, pad_rows]).reshape(-1, HEADS, HEAD)
    flags = jnp.zeros((HALF,), bool)
    marks = jnp.full((HALF,), -1, jnp.int32)
    video_pad = jnp.concatenate([marks, video, marks])
    valid_pad = jnp.concatenate([flags, valid, flags])
    query3 = query.reshape(-1, HEADS, HEAD)

    def one_block(start):
        query_part = lax.dynamic_slice_in_dim(query3, start, block, 0)
        key_part = lax.dynamic_slice_in_dim(keys_pad, start, span, 0)
        value_part = lax.dynamic_slice_in_dim(values_pad, start, span, 0)
        query_pos = start + jnp.arange(block, dtype=jnp.int32)
        key_pos = start - HALF + jnp.arange(span, dtype=jnp.int32)
        allowed = window_mask(query_pos, key_pos, lax.dynamic_slice_in_dim(video, start, block, 0), lax.dynamic_slice_in_dim(video_pad, start, span, 0), lax.dynamic_slice_in_dim(valid, start, block, 0), lax.dynamic_slice_in_dim(valid_pad, start, span, 0))
        scores = low_back(jnp.einsum('qhd,khd->hqk', query_part, key_part, precision=HIGH) * scale)
        masked = jnp.where(allowed[None], scores, MASKED)
        top = lax.optimization_barrier(jnp.max(masked, axis=-1, keepdims=True))
        expo = jnp.exp(masked - top)
        probs = low(expo / lax.optimization_barrier(jnp.sum(expo, axis=-1, keepdims=True)))
        mixed = jnp.einsum('hqk,khd->qhd', probs, value_part, precision=HIGH)
        return mixed.reshape(block, D)
    starts = jnp.arange(TOKENS // block, dtype=jnp.int32) * block
    return lax.map(jax.checkpoint(one_block), starts).reshape(TOKENS, D)

def reference(frames, cotangent, lengths, owners, attn_master, attn_first, attn_second, attn_average, small_master, small_first, small_second, small_average, mlp_master, mlp_first, mlp_second, mlp_average, bias_master, bias_first, bias_second, bias_average):
    positions = jnp.arange(-1, TOKENS + 1, dtype=jnp.int32)
    video_all, valid_all = frame_tables(lengths, positions)
    keep_prev, keep_after = conv_keeps(video_all, valid_all)
    video = video_all[1:-1]
    valid = valid_all[1:-1]
    valid_rows = valid.astype(jnp.float32)[:, None]
    slots = tile_slots(owners)
    matrices = attn_master[slots].reshape(4, D, D)

    def forward(inputs, weights, small, mlp_weights, hidden_bias):
        first = low(norm_rows(inputs, small[0], small[1]))
        padded = jnp.pad(first, ((1, 1), (0, 0)))
        convs = low(conv_three(padded, small[8:17].reshape(3, 3, D), keep_prev, keep_after))
        rounded = low(weights)
        query = both(product(convs[0], rounded[0]) + small[4])
        keys = both(product(convs[1], rounded[1]))
        values = both(product(convs[2], rounded[2]) + small[5])
        mixed = both(attend(query, keys, values, video, valid))
        branch = low_back(product(mixed, rounded[3]) + small[6])
        middle = inputs + valid_rows * branch
        second = low(norm_rows(middle, small[2], small[3]))
        mlp_low = low(mlp_weights)
        hidden = low_back(product(second, mlp_low[0]) + low(hidden_bias))
        active = low(jax.nn.gelu(hidden, approximate=False))
        result = low_back(lax.dot_general(active, mlp_low[1], (((1,), (1,)), ((), ())), precision=HIGH, preferred_element_type=jnp.float32) + small[7])
        return middle + valid_rows * result
    output, pull = jax.vjp(forward, frames.astype(jnp.float32), matrices, small_master, mlp_master, bias_master)
    grads = pull(cotangent.astype(jnp.float32))
    tile_grads = grads[1].reshape(TILES, TILE, D)
    slot_grads = jnp.zeros_like(attn_master).at[slots].set(tile_grads)
    filled = jnp.zeros((N_SEQ * CAP,), jnp.float32).at[slots].set(1.0)[:, None, None]
    attn_new = adamw(attn_master, slot_grads, attn_first, attn_second, attn_average, MATRIX_RATE, MATRIX_DECAY)
    small_new = adamw(small_master, grads[2], small_first, small_second, small_average, SMALL_RATE, 0.0)
    mlp_new = adamw(mlp_master, grads[3], mlp_first, mlp_second, mlp_average, MATRIX_RATE, MATRIX_DECAY)
    bias_new = adamw(bias_master, grads[4], bias_first, bias_second, bias_average, SMALL_RATE, 0.0)
    return (output.astype(jnp.bfloat16), grads[0].astype(jnp.bfloat16), attn_new[0] * filled, attn_new[1] * filled, attn_new[2] * filled, attn_new[3] * filled, small_new[0], small_new[1], small_new[2], small_new[3], mlp_new[0], mlp_new[1], mlp_new[2], mlp_new[3], bias_new[0], bias_new[1], bias_new[2], bias_new[3])
```

```python
import functools

import jax
import jax.numpy as jnp
from jax import lax
from jax.experimental import pallas as pl
from jax.experimental.pallas import tpu as pltpu
from jax.sharding import Mesh
from jax.sharding import PartitionSpec as P

HEADS = 4
HEAD = 128
HALF = 9
TILE = 128
TILES = 16
CAP = 2
STEP = 7
NSMALL = 17
NSMALL_ROWS = 32

NORM_EPS = 1e-05
MASKED = -1e30
BETA_ONE = 0.9
BETA_TWO = 0.999
ADAM_EPS = 1e-08
MATRIX_RATE = 0.03
MATRIX_DECAY = 0.05
SMALL_RATE = 0.3
AVERAGE_RATE = 0.8

F32 = jnp.float32
BF16 = jnp.bfloat16

KEY_RIM = 32
ROW_RIM = 16
QUERY_BLOCK = 96
KEY_SPAN = 128
FF_BLOCK = 512
FF_ROWS = 3
CHUNK = 128
NARROW = 64
SCALE = HEAD ** (-0.5)
GROUPS = ("z", "y", "core", "mlp")
SEATS = ("z", "y", "core")


def adamw(weight, grad, first, second, average, rate, decay):
    first_new = BETA_ONE * first + (1.0 - BETA_ONE) * grad
    second_new = BETA_TWO * second + (1.0 - BETA_TWO) * grad * grad
    scaled = second_new * (1.0 / (1.0 - BETA_TWO**STEP))
    root = scaled * lax.rsqrt(scaled)
    ratio = first_new * (1.0 / (1.0 - BETA_ONE**STEP)) / (root + ADAM_EPS)
    weight_new = weight - rate * (ratio + decay * weight)
    average_new = AVERAGE_RATE * average + (1.0 - AVERAGE_RATE) * weight_new
    return (weight_new, first_new, second_new, average_new)


def dot_nn(left, right):
    return lax.dot_general(left, right, (((1,), (0,)), ((), ())), preferred_element_type=F32)


def dot_nt(left, right):
    return lax.dot_general(left, right, (((1,), (1,)), ((), ())), preferred_element_type=F32)


def dot_tn(left, right):
    return lax.dot_general(left, right, (((0,), (0,)), ((), ())), preferred_element_type=F32)


def normal_parts(values):
    mean = jnp.mean(values, axis=-1, keepdims=True)
    centred = values - mean
    spread = jnp.mean(centred * centred, axis=-1, keepdims=True)
    inverse = lax.rsqrt(spread + NORM_EPS)
    return (centred * inverse, inverse)


def normal_back(unit, inverse, grad, gain):
    inner = grad * gain
    return inverse * (
        inner
        - jnp.mean(inner, axis=-1, keepdims=True)
        - unit * jnp.mean(inner * unit, axis=-1, keepdims=True)
    )


def fold_rows(values):
    return jnp.sum(values.reshape(-1, 8, values.shape[-1]), axis=0)


def conv_kernel(
    before, frames, after, cotangent, cols, small,
    conv_out, first_out, wide_out, cot_out, grad_rows_out, grad_t_out, rows,
):
    local = frames.shape[0]
    wide = local + 2 * KEY_RIM
    gain = small[0:1, :]
    bias = small[1:2, :]

    def norm_to(piece, start):
        unit, _ = normal_parts(piece.astype(F32))
        low = (unit * gain + bias).astype(BF16)
        first_out[pl.ds(start, piece.shape[0]), :] = low
        rows[pl.ds(start + 8, piece.shape[0]), :] = low.astype(F32)

    zero = jnp.zeros((8, rows.shape[1]), F32)
    rows[0:8, :] = zero
    rows[wide + 8 : wide + 16, :] = zero
    norm_to(before[0:KEY_RIM, :], 0)
    norm_to(after[0:KEY_RIM, :], KEY_RIM + local)

    def norm_step(step, carry):
        start = pl.multiple_of(step * CHUNK, CHUNK)
        norm_to(frames[pl.ds(start, CHUNK), :], pl.multiple_of(start + KEY_RIM, 32))
        return carry

    lax.fori_loop(0, local // CHUNK, norm_step, 0, unroll=2)
    wide_out[0:ROW_RIM, :] = before[KEY_RIM - ROW_RIM : KEY_RIM, :]
    wide_out[ROW_RIM : ROW_RIM + local, :] = frames[...]
    wide_out[ROW_RIM + local :, :] = after[0:ROW_RIM, :]
    cot_out[0:ROW_RIM, :] = before[KEY_RIM:, :]
    cot_out[ROW_RIM : ROW_RIM + local, :] = cotangent[...]
    cot_out[ROW_RIM + local :, :] = after[KEY_RIM:, :]

    def mask_step(step, carry):
        span = pl.ds(pl.multiple_of(step * QUERY_BLOCK, 32), QUERY_BLOCK)
        flags = cols[pl.ds(pl.multiple_of(step * QUERY_BLOCK + ROW_RIM, 16), QUERY_BLOCK), 2:3]
        grad_rows_out[span, :] = (cot_out[span, :].astype(F32) * flags).astype(BF16)
        return carry

    lax.fori_loop(0, cot_out.shape[0] // QUERY_BLOCK, mask_step, 0)
    grad_t_out[...] = grad_rows_out[ROW_RIM : ROW_RIM + local, :].T

    def conv_step(step, carry):
        start = pl.multiple_of(step * NARROW, NARROW)
        window = rows[pl.ds(start, NARROW + 16), :]
        flags = cols[pl.ds(start, NARROW), :]
        past = pltpu.roll(window, 1, 0)[8 : 8 + NARROW] * flags[:, 0:1]
        here = window[8 : 8 + NARROW]
        later = pltpu.roll(window, NARROW + 15, 0)[8 : 8 + NARROW] * flags[:, 1:2]
        for c in range(3):
            row = 8 + 3 * c
            mixed = (
                small[row : row + 1, :] * past
                + small[row + 1 : row + 2, :] * here
                + small[row + 2 : row + 3, :] * later
            )
            conv_out[c, pl.ds(start, NARROW), :] = mixed.astype(BF16)
        return carry

    lax.fori_loop(0, wide // NARROW, conv_step, 0)


def edges_kernel(tiles, head, tail, cot_head, cot_tail, first_out, second_out, up_out, down_out):
    first_out[...] = tiles[0].astype(BF16)
    second_out[...] = tiles[1].astype(BF16)
    up_out[0:KEY_RIM, :] = tail[...]
    up_out[KEY_RIM:, :] = cot_tail[...]
    down_out[0:KEY_RIM, :] = head[...]
    down_out[KEY_RIM:, :] = cot_head[...]


def matrices_kernel(master, low_out):
    size = master.shape[1]
    rows = pl.ds(pl.multiple_of(pl.program_id(0) * size, size), size)
    low_out[:, rows, :] = master[...].astype(BF16)


def half_kernel(place, master, bias, half_out):
    step = pl.program_id(0)
    size, units = master.shape[1:]
    half_out[pl.ds(pl.multiple_of(step * size, size), size), :] = master[0].astype(BF16)

    @pl.when(step == 0)
    def _():
        width = half_out.shape[0] - 16
        half_out[width:, :] = jnp.broadcast_to(bias[...], (16, units)).astype(BF16)


def tables_kernel(place, lengths, cols_out, codes_out):
    wide = cols_out.shape[0]
    blocks = (wide - KEY_SPAN) // QUERY_BLOCK + 1
    local = wide - 2 * KEY_RIM
    anchor = place[4] * local
    chunks = -(-wide // 128)
    height = -(-max(chunks, blocks) // 8) * 8
    row = lax.broadcasted_iota(jnp.int32, (height, 128), 0)
    lane = lax.broadcasted_iota(jnp.int32, (height, 128), 1)
    start = anchor - KEY_RIM + lane
    frame = start + row * 128
    key = start + row * QUERY_BLOCK
    zero = jnp.zeros((height, 128), jnp.int32)

    def count(j, carry):
        end, video, key_video, starts, stops = carry
        end = end + lengths[j]
        return (
            end,
            video + (frame >= end).astype(jnp.int32),
            key_video + (key >= end).astype(jnp.int32),
            starts + (frame == end).astype(jnp.int32),
            stops + (frame + 1 == end).astype(jnp.int32),
        )

    last, video, key_video, starts, stops = lax.fori_loop(
        0, lengths.shape[0], count, (jnp.int32(0), zero, zero, zero, zero)
    )
    valid = (frame >= 0) & (frame < last)
    key_valid = (key >= 0) & (key < last)
    prev = valid & (frame >= 1) & (starts == 0)
    after = valid & (frame + 1 < last) & (stops == 0)
    codes_out[...] = jnp.where(key_valid, key_video, -2).astype(F32)
    values = [prev.astype(F32), after.astype(F32), valid.astype(F32)]
    values.append(jnp.where(valid, video, -1).astype(F32))
    for c in range(chunks):
        size = min(128, wide - c * 128)
        columns = jnp.concatenate([value[c : c + 1] for value in values] * 2, axis=0).T
        cols_out[c * 128 : c * 128 + size, :] = columns[0:size]


def slots_of(owners):
    found = [owners[i] for i in range(TILES)]
    return [
        (found[i], sum([jnp.where(found[j] == found[i], 1, 0) for j in range(i)], jnp.int32(0)))
        for i in range(TILES)
    ]


def head_lanes(h):
    return slice(h * HEAD, (h + 1) * HEAD)


def head_rows(h):
    return slice(h * QUERY_BLOCK, (h + 1) * QUERY_BLOCK)


def attend_kernel(
    place, owners, *refs
):
    tiles, refs = (refs[:6], refs[6:])
    conv, cols, codes, small, *refs = refs
    weights_out, query_out, key_out, value_out, probs_out, mixed_out = refs
    rows, width = mixed_out.shape
    wide = conv.shape[1]
    depth = tiles[0].shape[0]
    for i, (owner, slot) in enumerate(slots_of(owners)):
        spot = pl.ds(i * TILE, TILE)
        core_away = (owner + place[2]) % 2
        y_away = (owner // 2 + place[1]) % 2
        z_away = place_of(place[0] ^ (owner // 4), depth)
        for r, source in enumerate(tiles[:4]):

            @pl.when((slot == 0) & (core_away * 2 + y_away == r))
            def _(source=source):
                weights_out[spot, :] = source[z_away]

        for r, source in enumerate(tiles[4:]):

            @pl.when((slot == 1) & (core_away == r))
            def _(source=source):
                weights_out[spot, :] = source[z_away, y_away]

    def matrix(c):
        return weights_out[c * width : (c + 1) * width, :]

    part = wide // 2
    for j in range(2):
        span = pl.ds(j * part, part)
        query_out[span, :] = (dot_nn(conv[0, span, :], matrix(0)) + small[4:5, :]).astype(BF16)
        key_out[span, :] = dot_nn(conv[1, span, :], matrix(1)).astype(BF16)
        value_out[span, :] = (dot_nn(conv[2, span, :], matrix(2)) + small[5:6, :]).astype(BF16)

    query_index = lax.broadcasted_iota(jnp.int32, (QUERY_BLOCK, KEY_SPAN), 0)
    key_index = lax.broadcasted_iota(jnp.int32, (QUERY_BLOCK, KEY_SPAN), 1)
    offset = query_index - key_index + (KEY_RIM - ROW_RIM)
    band = jnp.abs(offset) <= HALF
    same = offset == 0

    for step in range(rows // QUERY_BLOCK):
        start = step * QUERY_BLOCK
        query_start = start + ROW_RIM
        query_code = cols[pl.ds(query_start, QUERY_BLOCK), 3:4]
        key_code = codes[step : step + 1, :]
        allowed = band & (same | (query_code == key_code))
        scores = [
            jnp.where(
                allowed,
                dot_nt(
                    query_out[pl.ds(query_start, QUERY_BLOCK), head_lanes(h)],
                    key_out[pl.ds(start, KEY_SPAN), head_lanes(h)],
                )
                * SCALE,
                MASKED,
            )
            for h in range(HEADS)
        ]
        masked = jnp.concatenate(scores, axis=0)
        top = jnp.max(masked, axis=-1, keepdims=True)
        expo = jnp.exp(masked - top)
        probs = expo / jnp.sum(expo, axis=-1, keepdims=True)
        probs_out[step] = probs
        low = probs.astype(BF16)
        for h in range(HEADS):
            values = value_out[pl.ds(start, KEY_SPAN), head_lanes(h)]
            mixed = dot_nn(low[head_rows(h)], values)
            mixed_out[pl.ds(start, QUERY_BLOCK), head_lanes(h)] = mixed.astype(BF16)


def middle_kernel(mixed, weights, wide_rows, cols, small, middle_out, second_out, second_t_out):
    rows, width = wide_rows.shape
    part = rows // 3
    for j in range(3):
        span = pl.ds(j * part, part)
        branch = dot_nn(mixed[span, :], weights[3 * width : 4 * width, :]) + small[6:7, :]
        valid = cols[pl.ds(ROW_RIM + j * part, part), 2:3]
        middle = wide_rows[span, :].astype(F32) + valid * branch
        middle_out[span, :] = middle
        unit, _ = normal_parts(middle)
        second_out[span, :] = (unit * small[2:3, :] + small[3:4, :]).astype(BF16)
    second_t_out[...] = second_out[ROW_RIM : rows - ROW_RIM, :].T


def feed_kernel(first_call, *refs):
    place, first_matrix, second_matrix, hidden_bias, second, grad_rows, second_t, grad_t, *refs = refs
    if not first_call:
        result_in, second_grad_in, *refs = refs
    keep_out, send_out, bias_out, result, second_grad, up, down, active, hidden_grad = refs
    ways, _, units = first_matrix.shape
    width, block = up.shape
    per_piece = units // block
    rows = second.shape[0]
    local = rows - 2 * ROW_RIM
    own = slice(ROW_RIM, ROW_RIM + local)
    even = place[2] == 0
    straight = even if first_call else place[2] >= 0
    slabs, height = keep_out.shape[2:4]
    depth = slabs // 2
    if first_call:
        result[...] = jnp.zeros(result.shape, F32)
        second_grad[...] = jnp.zeros(second_grad.shape, F32)
    else:
        result[...] = result_in[...]
        second_grad[...] = second_grad_in[...]

    def block_step(step, carry):
        piece = step // per_piece
        lanes = pl.ds(pl.multiple_of((step % per_piece) * block, block), block)

        @pl.when(straight)
        def _():
            up[...] = first_matrix[piece, 0:width, lanes]
            down[...] = second_matrix[piece, 0:width, lanes]

        @pl.when(jnp.logical_not(straight))
        def _():
            up[...] = second_matrix[piece, 0:width, lanes]
            down[...] = first_matrix[piece, 0:width, lanes]

        if first_call:
            bias = first_matrix[piece, width : width + 16, lanes][0:1].astype(F32)
        else:
            bias = hidden_bias[0:1, lanes].astype(BF16).astype(F32)
        part = rows // FF_ROWS
        for j in range(FF_ROWS):
            span = pl.ds(j * part, part)
            value = dot_nn(second[span, :], up[...]) + bias
            active_grad = dot_nn(grad_rows[span, :], down[...])
            phi = 0.5 * (1.0 + lax.erf(value * (0.5**0.5)))
            density = jnp.exp(value * value * -0.5) * 0.3989422804014327
            active[span, :] = (value * phi).astype(BF16)
            hidden_grad[span, :] = (active_grad * (phi + value * density)).astype(BF16)
        result[...] += dot_nt(active[...], down[...])
        second_grad[...] += dot_nt(hidden_grad[...], up[...])
        up_grad = dot_nn(second_t[...], hidden_grad[own, :])
        down_grad = dot_nn(grad_t[...], active[own, :])
        bias_out[piece, :, lanes] = jnp.sum(
            hidden_grad[own, :].astype(F32), axis=0, keepdims=True
        )
        kept = jnp.where(even, up_grad, down_grad).astype(BF16)
        sent = jnp.where(even, down_grad, up_grad).astype(BF16)
        for slab in range(slabs):
            target = (slab // depth + place[1]) % 2 * depth + (slab % depth - place[0] + depth) % depth
            for half in range(2):
                start = (2 * slab + half) * height
                keep_out[piece, half, target, :, lanes] = kept[start : start + height]
                send_out[piece, half, target, :, lanes] = sent[start : start + height]
        return carry

    lax.fori_loop(0, ways * per_piece, block_step, 0)


def update_kernel(core_away, y_away, place, column, *refs):
    states, outs = refs[:4], refs[-8:-4]
    came, left, came_sems, left_sems = refs[-4:]
    depth, height, _ = column.shape
    matrix = (place[2] + core_away) % 2
    first_row = (place[1] + y_away) % 2 * (depth * height)

    def rows(j):
        return pl.ds(pl.multiple_of(first_row + j * height, height), height)

    def fetch(j, k):
        return pltpu.make_async_copy(
            states[k].at[matrix, rows(j)], came.at[j, k], came_sems.at[j, k]
        )

    def store(j, k):
        return pltpu.make_async_copy(
            left.at[j, k], outs[k].at[matrix, rows(j)], left_sems.at[j, k]
        )

    def start(j, carry):
        for k in range(4):
            fetch(j, k).start()
        return carry

    def update(j, carry):
        for k in range(4):
            fetch(j, k).wait()
        grad = column[(place[0] - j + depth) % depth].astype(F32)
        new = adamw(came[j, 0], grad, came[j, 1], came[j, 2], came[j, 3], MATRIX_RATE, MATRIX_DECAY)
        for k, value in enumerate(new):
            left[j, k] = value
            store(j, k).start()
        return carry

    def finish(j, carry):
        for k in range(4):
            store(j, k).wait()
        return carry

    lax.fori_loop(0, depth, start, 0)
    lax.fori_loop(0, depth, update, 0)
    lax.fori_loop(0, depth, finish, 0)


def middle_back_kernel(
    middle, cot, grad_rows, result_sum, second_sum, mixed, weights, cols, small,
    output_out, middle_grad_out, mixed_grad_out, out_grad_out, rows_out, branch,
):
    rows, width = middle.shape
    local = rows - 2 * ROW_RIM
    own = slice(ROW_RIM, ROW_RIM + local)
    rows_out[...] = jnp.zeros(rows_out.shape, F32)

    def finish(start, size, own_rows):
        span = pl.ds(start, size)
        here = middle[span, :]
        valid = cols[pl.ds(start + ROW_RIM, size), 2:3]
        unit, inverse = normal_parts(here)
        incoming = second_sum[span, :]
        back = normal_back(unit, inverse, incoming, small[2:3, :])
        middle_grad = cot[span, :].astype(F32) + back
        branch_grad = (valid * middle_grad).astype(BF16)
        branch[span, :] = branch_grad
        if own_rows:
            target = pl.ds(start - ROW_RIM, size)
            result = result_sum[span, :] + small[7:8, :]
            output_out[target, :] = (here + valid * result).astype(BF16)
            middle_grad_out[target, :] = middle_grad
            rows_out[0:8, :] += fold_rows(incoming * unit)
            rows_out[8:16, :] += fold_rows(incoming)
            rows_out[16:24, :] += fold_rows(branch_grad.astype(F32))
            rows_out[24:32, :] += fold_rows(grad_rows[span, :].astype(F32))

    finish(0, ROW_RIM, False)
    finish(ROW_RIM + local, ROW_RIM, False)

    def finish_step(j, carry):
        finish(pl.multiple_of(j * CHUNK + ROW_RIM, 16), CHUNK, True)
        return carry

    lax.fori_loop(0, local // CHUNK, finish_step, 0)
    mixed_grad_out[...] = dot_nt(branch[...], weights[3 * width : 4 * width, :]).astype(BF16)
    out_grad_out[...] = dot_tn(mixed[own, :], branch[own, :]).astype(BF16)


def scores_back_kernel(
    first_head, place, owners, query, keys, values, probs, mixed_grad, conv, out_grad,
    query_grad, key_grad, value_grad, keep_out, send_out,
    key_acc, value_acc, grads,
):
    rows, width = mixed_grad.shape
    columns = key_acc.shape[1]
    heads = columns // HEAD
    local = rows - 2 * ROW_RIM
    own = slice(ROW_RIM, ROW_RIM + local)
    wide_own = slice(KEY_RIM, KEY_RIM + local)
    key_acc[...] = jnp.zeros(key_acc.shape, F32)
    value_acc[...] = jnp.zeros(value_acc.shape, F32)
    keep_out[...] = jnp.zeros(keep_out.shape, BF16)
    send_out[...] = jnp.zeros(send_out.shape, BF16)

    for step in range(rows // QUERY_BLOCK):
        start = step * QUERY_BLOCK
        here = pl.ds(start, QUERY_BLOCK)
        span = pl.ds(start, KEY_SPAN)
        quest = pl.ds(start + ROW_RIM, QUERY_BLOCK)
        first_row = first_head * QUERY_BLOCK
        probs_here = probs[step, first_row : first_row + heads * QUERY_BLOCK, :]
        prob_grad = jnp.concatenate(
            [
                dot_nt(mixed_grad[here, head_lanes(h)], values[span, head_lanes(h)])
                for h in range(first_head, first_head + heads)
            ],
            axis=0,
        )
        inner = jnp.sum(probs_here * prob_grad, axis=-1, keepdims=True)
        score_grad = (probs_here * (prob_grad - inner)).astype(BF16)
        low = probs_here.astype(BF16)
        for h in range(heads):
            lanes, whole_lanes = head_lanes(h), head_lanes(first_head + h)
            score = score_grad[head_rows(h)]
            query_grad[here, lanes] = (dot_nn(score, keys[span, whole_lanes]) * SCALE).astype(BF16)
            key_acc[span, lanes] += dot_tn(score, query[quest, whole_lanes])
            value_acc[span, lanes] += dot_tn(low[head_rows(h)], mixed_grad[here, whole_lanes])

    inside = slice(ROW_RIM, ROW_RIM + rows)
    key_grad[...] = (key_acc[inside, :] * SCALE).astype(BF16)
    value_grad[...] = value_acc[inside, :].astype(BF16)

    for c, grad in enumerate((query_grad, key_grad, value_grad)):
        grads[c * width : (c + 1) * width, :] = dot_tn(conv[c, wide_own, :], grad[own, :]).astype(BF16)
    grads[3 * width :, :] = out_grad[:, first_head * HEAD : first_head * HEAD + columns]

    share = keep_out.shape[1]
    parts = TILE // share
    ways = CAP * parts
    depth = keep_out.shape[0] // (2 * ways)
    for i, (owner, slot) in enumerate(slots_of(owners)):
        away = (owner + place[2]) % 2
        y_away = (owner // 2 + place[1]) % 2
        z_away = (owner // 4) ^ place[0]
        for part in range(parts):
            way = (place[3] - slot * parts - part + ways) % ways
            target = (way * 2 + y_away) * depth + z_away
            here = pl.ds(i * TILE + part * share, share)

            @pl.when(away == 0)
            def _(target=target, here=here):
                keep_out[target] = grads[here, :]

            @pl.when(away == 1)
            def _(target=target, here=here):
                send_out[target] = grads[here, :]


def conv_grad_kernel(*refs):
    weights, conv_grad = refs[-2:]
    rows, columns = refs[0].shape
    width = weights.shape[1]
    part = rows // 2
    for j in range(2):
        span = pl.ds(j * part, part)
        for c in range(3):
            matrix = slice(c * width, (c + 1) * width)
            conv_grad[c, span, :] = dot_nt(refs[c][span, :], weights[matrix, 0:columns]) + dot_nt(
                refs[3 + c][span, :], weights[matrix, columns:]
            )


def conv_back_kernel(
    place, query_grad_0, value_grad_0, query_grad_1, value_grad_1, conv_grad, first, frames, feed_rows, near_bias, far_bias, cols, small,
    incoming_out, totals_out, sums,
):
    rows, columns = query_grad_0.shape
    width = frames.shape[1]
    local = rows - 2 * ROW_RIM
    sums[...] = jnp.zeros(sums.shape, F32)

    def conv_step(step, carry):
        start = pl.multiple_of(step * CHUNK, CHUNK)
        window = CHUNK + 16
        flags = cols[pl.ds(pl.multiple_of(start + KEY_RIM - 8, 8), window), :]
        span = pl.ds(pl.multiple_of(start + ROW_RIM - 8, 8), window)
        grads = [conv_grad[c, span, :] for c in range(3)]
        past = sum(small[8 + 3 * c : 9 + 3 * c, :] * grads[c] for c in range(3)) * flags[:, 0:1]
        later = sum(small[10 + 3 * c : 11 + 3 * c, :] * grads[c] for c in range(3)) * flags[:, 1:2]
        middle = slice(8, 8 + CHUNK)
        incoming = (
            sum(small[9 + 3 * c : 10 + 3 * c, :] * grads[c][middle] for c in range(3))
            + pltpu.roll(past, window - 1, 0)[middle]
            + pltpu.roll(later, 1, 0)[middle]
        )
        low = first[pl.ds(pl.multiple_of(start + KEY_RIM - 16, 16), window + 16), :].astype(F32)
        inner = slice(16, 16 + CHUNK)
        low_here = low[inner]
        low_past = pltpu.roll(low, 1, 0)[inner] * flags[middle, 0:1]
        low_later = pltpu.roll(low, window + 15, 0)[inner] * flags[middle, 1:2]
        for c in range(3):
            grad = grads[c][middle]
            base = 8 * (8 + 3 * c)
            sums[base : base + 8, :] += fold_rows(grad * low_past)
            sums[base + 8 : base + 16, :] += fold_rows(grad * low_here)
            sums[base + 16 : base + 24, :] += fold_rows(grad * low_later)
        unit, _ = normal_parts(frames[pl.ds(start, CHUNK), :].astype(F32))
        incoming_out[pl.ds(start, CHUNK), :] = incoming
        sums[0:8, :] += fold_rows(incoming * unit)
        sums[8:16, :] += fold_rows(incoming)
        here = pl.ds(pl.multiple_of(start + ROW_RIM, 16), CHUNK)
        for lanes, query_grad, value_grad in (
            (slice(0, columns), query_grad_0, value_grad_0),
            (slice(columns, width), query_grad_1, value_grad_1),
        ):
            sums[32:40, lanes] += fold_rows(query_grad[here, :].astype(F32))
            sums[40:48, lanes] += fold_rows(value_grad[here, :].astype(F32))
        return carry

    lax.fori_loop(0, local // CHUNK, conv_step, 0)
    sums[16:32, :] = feed_rows[0:16, :]
    sums[48:64, :] = feed_rows[16:32, :]
    totals_out[0:24, :] = jnp.sum(sums[...].reshape(24, 8, width), axis=1)
    totals_out[24:, :] = jnp.zeros((totals_out.shape[0] - 24, width), F32)
    units = near_bias.shape[2]
    ways = 1 + far_bias.shape[0]
    chunk = min(units, width)
    for piece in range(ways):
        source = near_bias if piece == 0 else far_bias
        for j in range(units // chunk):
            offset = (place[3] - piece + ways) % ways * units + j * chunk
            lanes = pl.ds(pl.multiple_of(offset % width, chunk), chunk)
            totals_out[pl.ds(24 + offset // width, 1), lanes] = source[
                max(piece - 1, 0), :, j * chunk : (j + 1) * chunk
            ]


def add_kernel(inputs, kinds, *refs):
    for out, parts in zip(refs[-len(kinds) :], inputs):
        count = out.shape[0]

        def step(j, carry, out=out, parts=parts, count=count):
            total = 0.0
            for index, start, *stride in parts:
                run = stride[0] // 2 if stride else count
                total = total + refs[index][start + j // run * 2 * run + j % run].astype(F32)
            out[j] = total.astype(out.dtype)
            return carry

        lax.fori_loop(0, count, step, 0)


def add_into(name, arrays, outputs, micros=0.1):
    outs = [in_place((count,) + arrays[0].shape[1:], BF16) for count, _ in outputs]
    kernel = functools.partial(add_kernel, [parts for _, parts in outputs], outs)
    return call(kernel, name, outs, micros, 8)(*arrays)


def join_kernel(first, second, out):
    count = first.shape[0]
    out[0:count] = first[...]
    out[count:] = second[...]


def joined(first, second):
    out = in_place((first.shape[0] + second.shape[0],) + first.shape[1:], first.dtype)
    return call(join_kernel, "joined", (out,), 0.1, 4)(first, second)[0]


def flipped(array, axis, bit):
    return lax.ppermute(array, axis, [(i, i ^ bit) for i in range(lax.axis_size(axis))])


def place_of(index, count):
    bits = count.bit_length() - 1
    return sum(((index >> k) & 1) << (bits - 1 - k) for k in range(bits))


def stack_kernel(*refs):
    for j, ref in enumerate(refs[:-1]):
        refs[-1][j] = ref[...]


def stacked(*arrays):
    out = in_place((len(arrays),) + arrays[0].shape, arrays[0].dtype)
    return call(stack_kernel, "stacked", (out,), 0.1, 4)(*arrays)[0]


def line_kernel(ways, *refs):
    first, second_got, totals, totals_got = refs[:ways], refs[ways : ways + 2], refs[ways + 2], refs[ways + 3]
    first_out, line_out, *second_out = refs[ways + 4 :]
    depth, piece, width = first_out.shape
    for j in range(depth):
        first_out[j] = sum(part[j].astype(F32) for part in first).astype(BF16)
        total = sum(part[depth + j].astype(F32) for part in first)
        line_out[j * piece : (j + 1) * piece, :] = total.astype(BF16)
        for d, out in enumerate(second_out):
            total = sum(part[d * depth + j].astype(F32) for part in second_got)
            out[j] = total.astype(BF16)
    low = (totals[...] + totals_got[...]).astype(BF16)
    edge = depth * piece
    line_out[edge : edge + NSMALL_ROWS, :] = low[:, 0:width]
    line_out[edge + NSMALL_ROWS :, :] = low[:, width:]


def flat_kernel(first, line, line_got, *refs):
    depth, share, width = first.shape
    second, (keep_out, send_out) = refs[:-2], refs[-2:]
    for j in range(depth):
        rows = slice(j * share, (j + 1) * share)
        left = first[j].astype(F32) + line_got[rows, :].astype(F32)
        right = sum(part[j].astype(F32) for part in second)
        if j % 2:
            out = slice(j // 2 * share, (j // 2 + 1) * share)
            send_out[out, 0:width] = left.astype(BF16)
            send_out[out, width:] = right.astype(BF16)
        else:
            keep_out[j // 2, :, 0:width] = left.astype(BF16)
            keep_out[j // 2, :, width:] = right.astype(BF16)
    edge, small = (depth * share, NSMALL_ROWS)
    low = (line[edge:, :].astype(F32) + line_got[edge:, :].astype(F32)).astype(BF16)
    send_out[depth // 2 * share :, 0:width] = low[0:small]
    send_out[depth // 2 * share :, width:] = low[small:]


def halve_kernel(keep, sent, got, keep_out, send_out):
    count, share, _ = keep.shape
    for j in range(count):
        rows = slice(j * share, (j + 1) * share)
        total = (keep[j].astype(F32) + got[rows, :].astype(F32)).astype(BF16)
        if j % 2:
            send_out[j // 2 * share : (j // 2 + 1) * share, :] = total
        else:
            keep_out[j // 2] = total
    low = sent[count * share :, :].astype(F32) + got[count * share :, :].astype(F32)
    send_out[count // 2 * share :, :] = low.astype(BF16)


def mine_kernel(keep, sent, got, out):
    share = keep.shape[1]
    out[0:share, :] = (keep[0].astype(F32) + got[0:share, :].astype(F32)).astype(BF16)
    out[share:, :] = (sent[share:, :].astype(F32) + got[share:, :].astype(F32)).astype(BF16)


def feed_line_kernel(*refs):
    depth = refs[0].shape[0]
    height = refs[0].shape[1]
    parts, outs = refs[:-depth], refs[-depth:]
    for j, out in enumerate(outs):
        out[0:height, :] = sum(part[j].astype(F32) for part in parts[:2]).astype(BF16)
        out[height:, :] = sum(part[j].astype(F32) for part in parts[2:]).astype(BF16)


def ordered_sum(parts, index):
    count = len(parts)
    total = 0.0
    for j in range(count):
        for d in range(count):
            total = total + jnp.where((index - d + count) % count == j, parts[d], 0.0)
    return total


def update_rest_kernel(place, owners, *refs):
    ways = len(refs) - 18
    shares = refs[:ways]
    attn, small = refs[ways : ways + 4], refs[ways + 4 : ways + 8]
    attn_out, small_out, bias_out, grads = refs[ways + 8 : ways + 12], refs[ways + 12 : ways + 16], refs[-2], refs[-1]
    share = shares[0].shape[0] - NSMALL_ROWS
    width = shares[0].shape[1]
    for d in range(ways):
        grads[(place[3] - d + ways) % ways] = shares[d][0:share, :]
    totals = ordered_sum([part[share:, :].astype(F32) for part in shares], place[3])
    new = adamw(*[small[0][...], totals[0:NSMALL]], *[ref[...] for ref in small[1:]], SMALL_RATE, 0.0)
    for out, value in zip(small_out, new):
        out[...] = value
    bias_out[...] = totals[24:]
    seat = (place[0] * 2 + place[1]) * 2 + place[2]
    parts = TILE // share
    held = sum(jnp.where(owners[i] == seat, 1, 0) for i in range(TILES))
    for k in range(CAP):
        for part in range(parts):
            rows = slice(part * share, (part + 1) * share)
            grad = grads[k * parts + part].astype(F32)
            old = [ref[k, rows, :] for ref in attn]
            new = adamw(old[0], grad, *old[1:], MATRIX_RATE, MATRIX_DECAY)
            for out, value in zip(attn_out, new):
                out[k, rows, :] = jnp.where(held > k, value, 0.0)


def in_grad_kernel(incoming, frames, middle_grad, small, in_grad_out):
    size = CHUNK

    def step_of(step, carry):
        rows = pl.ds(pl.multiple_of(step * size, size), size)
        unit, inverse = normal_parts(frames[rows, :].astype(F32))
        back = normal_back(unit, inverse, incoming[rows, :], small[0:1, :])
        in_grad_out[rows, :] = (middle_grad[rows, :] + back).astype(BF16)
        return carry

    lax.fori_loop(0, incoming.shape[0] // size, step_of, 0)


def in_vmem(count):
    return [pl.BlockSpec(memory_space=pltpu.VMEM)] * count


def in_smem(count):
    return [pl.BlockSpec(memory_space=pltpu.SMEM)] * count


def shape(dims, kind):
    return jax.ShapeDtypeStruct(dims, kind)


def swap(array, axis):
    return lax.ppermute(array, axis, [(0, 1), (1, 0)])


def shifted(array, axis, distance):
    count = lax.axis_size(axis)
    return lax.ppermute(array, axis, [(i, (i + distance) % count) for i in range(count)])


def added(*parts):
    return functools.reduce(jnp.add, [part.astype(F32) for part in parts])


def together(*arrays):
    return lax.optimization_barrier(arrays)


def cost(micros):
    return pl.CostEstimate(
        flops=int(micros * 1.1e9), bytes_accessed=int(micros * 3.6e6), transcendentals=0
    )


def far_away(array):
    return pltpu.with_memory_space_constraint(array, pltpu.HBM)


def call(kernel, name, outs, micros, limit, scratch=(), smem=0, fetched=()):
    def run(*arrays):
        arrays = list(arrays[:smem]) + [
            far_away(array) if index in fetched else kept(array)
            for index, array in enumerate(arrays[smem:])
        ]
        return pl.pallas_call(
            kernel,
            out_shape=tuple(outs),
            in_specs=in_smem(smem) + in_vmem(len(arrays) - smem),
            out_specs=tuple(in_vmem(len(outs))),
            scratch_shapes=list(scratch),
            compiler_params=pltpu.CompilerParams(vmem_limit_bytes=limit * 1024 * 1024),
            cost_estimate=cost(micros),
            name=name,
        )(*arrays)

    return run


def kept(array):
    return pltpu.with_memory_space_constraint(array, pltpu.VMEM)


def in_place(dims, kind):
    return pltpu.VMEM(dims, kind)


def feed(place, slabs, first_matrix, second_matrix, bias, second, grad_rows, second_t, grad_t, *sums):
    ways, _, units = first_matrix.shape
    rows, width = second.shape
    block = min(FF_BLOCK, units)
    grads = in_place((ways, 2, slabs, width // slabs // 2, units), BF16)
    return call(
        functools.partial(feed_kernel, not sums),
        "feed",
        (
            grads,
            grads,
            in_place((ways, 1, units), F32),
            in_place((rows, width), F32),
            in_place((rows, width), F32),
        ),
        14,
        8,
        (
            pltpu.VMEM((width, block), BF16),
            pltpu.VMEM((width, block), BF16),
            pltpu.VMEM((rows, block), BF16),
            pltpu.VMEM((rows, block), BF16),
        ),
        smem=1,
    )(place, first_matrix, second_matrix, bias, second, grad_rows, second_t, grad_t, *sums)


def update_feed(place, core_away, y_away, column, states, done=()):
    depth, height, units = column.shape
    anywhere = pl.BlockSpec(memory_space=pl.ANY)
    return pl.pallas_call(
        functools.partial(update_kernel, core_away, y_away),
        out_shape=tuple(shape(state.shape, F32) for state in states),
        in_specs=in_smem(1) + in_vmem(1) + [anywhere] * (4 + len(done)),
        out_specs=(anywhere,) * 4,
        input_output_aliases={6 + j: j for j in range(len(done))},
        scratch_shapes=[
            pltpu.VMEM((depth, 4, height, units), F32),
            pltpu.VMEM((depth, 4, height, units), F32),
            pltpu.SemaphoreType.DMA((depth, 4)),
            pltpu.SemaphoreType.DMA((depth, 4)),
        ],
        compiler_params=pltpu.CompilerParams(vmem_limit_bytes=12 * 1024 * 1024),
        cost_estimate=cost(0.3),
        name="update_feed",
    )(place, kept(column), *[far_away(state) for state in states], *done)


def shards(
    frames,
    cotangent,
    lengths,
    owners,
    attn_master,
    attn_first,
    attn_second,
    attn_average,
    small_master,
    small_first,
    small_second,
    small_average,
    mlp_master,
    mlp_first,
    mlp_second,
    mlp_average,
    bias_master,
    bias_first,
    bias_second,
    bias_average,
):
    local, width = frames.shape
    wide = local + 2 * KEY_RIM
    rows = local + 2 * ROW_RIM
    blocks = rows // QUERY_BLOCK
    assert blocks * QUERY_BLOCK == rows and local % CHUNK == 0
    units = mlp_master.shape[2]
    ways = lax.axis_size("mlp")
    depth = lax.axis_size("z")
    devices = lax.axis_size(GROUPS)
    share = CAP * TILE // ways
    way = lax.axis_index("mlp")
    place = jnp.stack([lax.axis_index(name) for name in GROUPS + (GROUPS,)]).astype(jnp.int32)

    last = local // KEY_RIM - 1
    last_cot = local // ROW_RIM - 1
    rim = KEY_RIM + ROW_RIM
    first_tile, second_tile, to_next, to_past = pl.pallas_call(
        edges_kernel,
        grid=(1,),
        out_shape=(
            in_place((TILE, width), BF16),
            in_place((TILE, width), BF16),
            in_place((rim, width), BF16),
            in_place((rim, width), BF16),
        ),
        in_specs=[
            pl.BlockSpec((CAP, TILE, width), lambda i: (0, 0, 0)),
            pl.BlockSpec((KEY_RIM, width), lambda i: (0, 0)),
            pl.BlockSpec((KEY_RIM, width), lambda i: (last, 0)),
            pl.BlockSpec((ROW_RIM, width), lambda i: (0, 0)),
            pl.BlockSpec((ROW_RIM, width), lambda i: (last_cot, 0)),
        ],
        out_specs=tuple(in_vmem(4)),
        compiler_params=pltpu.CompilerParams(vmem_limit_bytes=8 * 1024 * 1024),
        cost_estimate=cost(1),
        name="edges",
    )(*[far_away(array) for array in (attn_master, frames, frames, cotangent, cotangent)])
    second_tile_y = swap(second_tile, "y")
    pair_b = stacked(second_tile, second_tile_y)[None]
    bits = [1 << k for k in range(depth.bit_length() - 1)][::-1]
    column_a, column_b = (first_tile[None], pair_b)

    up = [(i, i + 1) for i in range(devices - 1)]
    down = [(i + 1, i) for i in range(devices - 1)]
    before = lax.ppermute(to_next, GROUPS, up)
    after = lax.ppermute(to_past, GROUPS, down)

    edges = (before, after)
    for bit in bits[:-1]:
        got_a, got_b = (flipped(column_a, "z", bit), flipped(column_b, "z", bit))
        column_a = joined(column_a, got_a)
        column_a, column_b, edges, place_late = together(column_a, column_b, edges, place)
        column_b = joined(column_b, got_b)
    before, after = edges

    bias_row = bias_master.reshape(1, units)
    cut_rows = width // 2
    half = pl.pallas_call(
        half_kernel,
        grid_spec=pltpu.PrefetchScalarGridSpec(
            num_scalar_prefetch=1,
            grid=(2,),
            in_specs=[
                pl.BlockSpec((1, cut_rows, units), lambda i, place: (place[2], i, 0)),
                pl.BlockSpec((1, units), lambda i, place: (0, 0)),
            ],
            out_specs=pl.BlockSpec(memory_space=pltpu.VMEM),
        ),
        out_shape=in_place((width + 16, units), BF16),
        compiler_params=pltpu.CompilerParams(vmem_limit_bytes=8 * 1024 * 1024),
        cost_estimate=cost(1),
        name="half",
    )(place_late, far_away(mlp_master), bias_row)
    half_got = [shifted(half, "mlp", d) for d in range(1, ways)]
    column_a = joined(column_a, flipped(column_a, "z", 1))
    column_a, mlp_late = together(column_a, mlp_master)
    column_a_y = swap(column_a, "y")
    low_mlp = pl.pallas_call(
        matrices_kernel,
        grid=(2,),
        out_shape=in_place((2, width, units), BF16),
        in_specs=[pl.BlockSpec((2, cut_rows, units), lambda i: (0, i, 0))],
        out_specs=pl.BlockSpec(memory_space=pltpu.VMEM),
        compiler_params=pltpu.CompilerParams(vmem_limit_bytes=12 * 1024 * 1024),
        cost_estimate=cost(0.5),
        name="matrices",
    )(far_away(mlp_late))

    height = -(-max(-(-wide // 128), blocks) // 8) * 8
    cols, codes = pl.pallas_call(
        tables_kernel,
        out_shape=(in_place((wide, 8), F32), in_place((height, 128), F32)),
        in_specs=in_smem(2),
        out_specs=tuple(in_vmem(2)),
        cost_estimate=cost(1),
        name="tables",
    )(place, lengths)

    column_b_z = flipped(column_b, "z", 1)
    conv, first, wide_rows, cot, grad_rows, grad_t = call(
        conv_kernel,
        "norm_conv",
        (
            in_place((3, wide, width), BF16),
            in_place((wide, width), BF16),
            in_place((rows, width), BF16),
            in_place((rows, width), BF16),
            in_place((rows, width), BF16),
            in_place((width, local), BF16),
        ),
        0.5,
        6,
        (pltpu.VMEM((wide + 16, width), F32),),
        fetched=(1, 3),
    )(before, frames, after, cotangent, cols, small_master)

    column_b, column_a_y, conv, half_got, low_mlp = together(
        column_b, column_a_y, conv, half_got, low_mlp
    )
    column_b = joined(column_b, column_b_z)
    columns = [column_a, column_a_y, column_b]
    away = [swap(column, "core") for column in columns]
    tiles = columns[:2] + away[:2] + columns[2:] + away[2:]

    weights, query, keys, values, probs, mixed = call(
        attend_kernel,
        "attend",
        (
            in_place((4 * width, width), BF16),
            in_place((wide, width), BF16),
            in_place((wide, width), BF16),
            in_place((wide, width), BF16),
            in_place((blocks, HEADS * QUERY_BLOCK, KEY_SPAN), F32),
            in_place((rows, width), BF16),
        ),
        0.5,
        8,
        smem=2,
    )(place, owners, *tiles, conv, cols, codes, small_master)
    half_got, mixed = together(half_got, mixed)
    halves = half_got[0][None] if ways == 2 else stacked(*half_got)
    others = swap(halves, "core")
    middle, second, second_t = call(
        middle_kernel,
        "middle",
        (
            in_place((rows, width), F32),
            in_place((rows, width), BF16),
            in_place((width, local), BF16),
        ),
        20,
        8,
    )(mixed, weights, wide_rows, cols, small_master)

    rest = (second, grad_rows, second_t, grad_t)
    far_keep, far_send, far_bias, *sums = feed(
        place, 2 * depth, halves, others, bias_row, *rest
    )
    far_got = swap(far_send, "core")
    near_keep, near_send, near_bias, *sums = feed(
        place, 2 * depth, low_mlp[0][None], low_mlp[1][None], bias_row, *rest, *sums
    )
    near_got = swap(near_send, "core")
    pieces = range(1, ways)
    height = width // (4 * depth)

    def halves_of(array):
        return array.reshape(-1, height, units)

    def row(piece, half, y_away=0):
        return ((piece * 2 + half) * 2 + y_away) * depth

    far = add_into(
        "far_sum",
        (halves_of(far_keep), halves_of(far_got)),
        [(2 * depth, [(i, row(d - 1, 0)) for i in range(2)]) for d in pieces]
        + [(depth, [(i, row(d - 1, 1)) for i in range(2)]) for d in pieces]
        + [(depth, [(i, row(d - 1, 1, 1)) for i in range(2)]) for d in pieces],
        0.1,
    )
    far, sums = together(far, sums)
    far_x = [shifted(far[d - 1], "mlp", -d) for d in pieces]
    far_y = [swap(far[2 * (ways - 1) + d - 1], "y") for d in pieces]

    output, middle_grad, mixed_grad, out_grad, feed_rows = call(
        middle_back_kernel,
        "middle_back",
        (
            shape((local, width), BF16),
            in_place((local, width), F32),
            in_place((rows, width), BF16),
            in_place((width, width), BF16),
            in_place((32, width), F32),
        ),
        0.5,
        8,
        (pltpu.VMEM((rows, width), BF16),),
    )(middle, cot, grad_rows, *sums, mixed, weights, cols, small_master)

    near_keep, mixed_grad, far_y = together(near_keep, mixed_grad, far_y)
    near = add_into(
        "near_sum",
        (halves_of(near_keep), halves_of(near_got)),
        [(2 * depth, [(i, row(0, 0)) for i in range(2)])]
        + [(depth, [(i, row(0, 1, j)) for i in range(2)]) for j in range(2)],
        0.1,
    )
    near, mixed_grad = together(near, mixed_grad)
    near_y = swap(near[2], "y")

    columns = width // 2
    slabs = in_place((2 * ways * depth, share, columns), BF16)

    def scores_back(first_head, mixed_grad):
        return call(
            functools.partial(scores_back_kernel, first_head),
            "scores_back",
            (
                in_place((rows, columns), BF16),
                in_place((rows, columns), BF16),
                in_place((rows, columns), BF16),
                slabs,
                slabs,
            ),
            8,
            10,
            (
                pltpu.VMEM((wide, columns), F32),
                pltpu.VMEM((wide, columns), F32),
                pltpu.VMEM((4 * width, columns), BF16),
            ),
            smem=2,
        )(place, owners, query, keys, values, probs, mixed_grad, conv, out_grad)

    *grads_0, keep_0, send_0 = scores_back(0, mixed_grad)
    got_0 = swap(send_0, "core")

    arrays = (near[0], *far_x, near[1], near_y, *far[ways - 1 : 2 * (ways - 1)], *far_y)
    first_parts = list(range(ways))
    feed_two = add_into(
        "feed_two",
        arrays,
        [(depth, [(i, j * depth) for i in first_parts]) for j in range(2)]
        + [(depth, [(ways, 0), (ways + 1, 0)])]
        + [(depth, [(ways + 1 + d, 0), (2 * ways + d, 0)]) for d in pieces],
        0.1,
    )
    feed_two, mixed_grad, grads_0 = together(feed_two, mixed_grad, grads_0)
    feed_y = swap(feed_two[1], "y")
    feed_x = [shifted(feed_two[2 + d], "mlp", -d) for d in pieces]

    *grads_1, keep_1, send_1 = scores_back(HEADS // 2, mixed_grad)
    got_1 = swap(send_1, "core")
    paired_0 = add_into(
        "paired",
        (keep_0, got_0),
        [(2 * depth, [(i, 2 * depth * d) for i in range(2)]) for d in range(ways)],
        20,
    )
    feed_line = call(
        feed_line_kernel,
        "feed_line",
        tuple(in_place((2 * height, units), BF16) for _ in range(depth)),
        0.1,
        8,
    )(feed_two[0], feed_y, feed_two[2], *feed_x)
    paired_0, feed_line, keep_1, grads_1 = together(paired_0, feed_line, keep_1, grads_1)
    first_got = [shifted(paired_0[d], "mlp", -d) for d in range(1, ways)]
    feed_got = [shifted(feed_line[d], "z", d) for d in range(1, depth)]

    paired_1 = add_into(
        "paired",
        (keep_1, got_1),
        [(ways * depth, [(i, depth * j, 2 * depth) for i in range(2)]) for j in range(2)],
        0.1,
    )
    paired_1, grads_1 = together(paired_1, grads_1)
    second_got = swap(paired_1[1], "y")

    conv_grad = call(
        conv_grad_kernel, "conv_grad", (in_place((3, rows, width), F32),), 20, 8
    )(*grads_0, *grads_1, weights)[0]
    incoming, totals = call(
        conv_back_kernel,
        "conv_back",
        (in_place((local, width), F32), in_place((NSMALL_ROWS, width), F32)),
        12,
        8,
        (pltpu.VMEM((192, width), F32),),
        smem=1,
    )(
        place, grads_0[0], grads_0[2], grads_1[0], grads_1[2], conv_grad, first, frames, feed_rows,
         near_bias, far_bias, cols, small_master,
    )

    totals_got = swap(totals, "core")
    feed_keep, totals = together(feed_line[0], totals)
    feed_own = add_into(
        "feed_own",
        [part[None] for part in (feed_keep, *feed_got)],
        [(1, [(d, 0) for d in range(depth)])],
    )[0]
    feed_own, first_keep = together(feed_own, paired_0[0])
    feed_all = [shifted(feed_own[0], "z", d) for d in range(1, depth)]
    lined, line, *second = call(
        functools.partial(line_kernel, ways),
        "line",
        (
            in_place((depth, share, columns), BF16),
            in_place((depth * share + 2 * NSMALL_ROWS, columns), BF16),
        )
        + (in_place((depth, share, columns), BF16),) * ways,
        0.1,
        8,
    )(first_keep, *first_got, paired_1[0], second_got, totals, totals_got)
    lined, line, second, incoming = together(lined, line, second, incoming)
    line_got = swap(line, "y")
    second_x = [shifted(second[d], "mlp", -d) for d in range(1, ways)]
    in_grad = call(
        in_grad_kernel, "in_grad", (shape((local, width), BF16),), 20, 8, fetched=(1,)
    )(incoming, frames, middle_grad, small_master)[0]
    lined, in_grad = together(lined, in_grad)

    def slabs(count, extra):
        if extra:
            return in_place((count * share + NSMALL_ROWS, width), BF16)
        return in_place((count, share, width), BF16)

    count = depth // 2
    z_keep, z_sent = call(flat_kernel, "flat", (slabs(count, 0), slabs(count, 1)), 0.1, 8)(
        lined, line, line_got, second[0], *second_x
    )
    feed_own, z_keep, z_sent = together(feed_own, z_keep, z_sent)
    z_got = flipped(z_sent, "z", 1)
    feed_sums = [stacked(feed_own[0], *feed_all)]
    feed_sums.append(swap(feed_sums[0], "y"))
    feed_sums.append(swap(feed_sums[0], "core"))
    states = (mlp_master, mlp_first, mlp_second, mlp_average)
    mlp_new = update_feed(place, 0, 0, feed_sums[0], states)
    mlp_new, z_keep = together(mlp_new, z_keep)
    for bit in bits[::-1][1:]:
        count //= 2
        z_keep, z_sent = call(halve_kernel, "halve", (slabs(count, 0), slabs(count, 1)), 0.1, 8)(
            z_keep, z_sent, z_got
        )
        mlp_new, z_keep, z_sent = together(mlp_new, z_keep, z_sent)
        z_got = flipped(z_sent, "z", bit)
    mlp_new = update_feed(place, 1, 0, feed_sums[2], states, mlp_new)
    mlp_new, z_keep = together(mlp_new, z_keep)
    mine = call(mine_kernel, "mine", (in_place((share + NSMALL_ROWS, width), BF16),), 0.1, 8)(
        z_keep, z_sent, z_got
    )[0]
    mine, own_y, mlp_new = together(mine, feed_sums[1], mlp_new)
    shares = [mine] + [shifted(mine, "mlp", d) for d in range(1, ways)]
    other_y = swap(own_y, "core")
    mlp_new = update_feed(place, 0, 1, own_y, states, mlp_new)
    mlp_new, other_y, shares[0] = together(mlp_new, other_y, shares[0])
    mlp_new = update_feed(place, 1, 1, other_y, states, mlp_new)
    attn_shape = shape(attn_master.shape, F32)
    small_shape = shape(small_master.shape, F32)
    rest_new = call(
        update_rest_kernel,
        "update_rest",
        (attn_shape,) * 4 + (small_shape,) * 4 + (in_place((8, width), F32),),
        3,
        12,
        (pltpu.VMEM((ways, share, width), BF16),),
        smem=2,
    )(
        place, owners, *shares, attn_master, attn_first, attn_second, attn_average,
        small_master, small_first, small_second, small_average,
    )

    bias_sum = lax.dynamic_slice_in_dim(rest_new[8].reshape(-1), way * units, units, 0)
    bias_new = adamw(
        bias_master, bias_sum, bias_first, bias_second, bias_average, SMALL_RATE, 0.0
    )
    return (
        output,
        in_grad,
        *rest_new[:8],
        *mlp_new,
        *bias_new,
    )


def solution(mesh):
    seq, mlp = mesh.devices.shape
    grid = Mesh(mesh.devices.reshape(seq // 4, 2, 2, mlp), GROUPS)
    rows = P(GROUPS, None)
    tiles = P(SEATS, None, None)
    units = P(None, None, "mlp")
    bias = P("mlp")
    in_specs = (
        (rows, rows, P(), P()) + (tiles,) * 4 + (P(),) * 4 + (units,) * 4 + (bias,) * 4
    )
    out_specs = (rows, rows) + (tiles,) * 4 + (P(),) * 4 + (units,) * 4 + (bias,) * 4
    return jax.shard_map(shards, mesh=grid, in_specs=in_specs, out_specs=out_specs, check_vma=False)
```

```python
import functools

import jax
import jax.numpy as jnp
from jax import lax
from jax.experimental import pallas as pl
from jax.experimental.pallas import tpu as pltpu
from jax.sharding import Mesh
from jax.sharding import PartitionSpec as P

HEADS = 4
HEAD = 128
HALF = 9
TILE = 128
TILES = 16
CAP = 2
STEP = 7
NSMALL = 17
NSMALL_ROWS = 32

NORM_EPS = 1e-05
MASKED = -1e30
BETA_ONE = 0.9
BETA_TWO = 0.999
ADAM_EPS = 1e-08
MATRIX_RATE = 0.03
MATRIX_DECAY = 0.05
SMALL_RATE = 0.3
AVERAGE_RATE = 0.8

F32 = jnp.float32
BF16 = jnp.bfloat16

KEY_RIM = 32
ROW_RIM = 16
QUERY_BLOCK = 96
KEY_SPAN = 128
FF_BLOCK = 512
FF_ROWS = 3
CHUNK = 128
NARROW = 64
SCALE = HEAD ** (-0.5)
GROUPS = ("z", "y", "core", "mlp")
SEATS = ("z", "y", "core")


def adamw(weight, grad, first, second, average, rate, decay):
    first_new = BETA_ONE * first + (1.0 - BETA_ONE) * grad
    second_new = BETA_TWO * second + (1.0 - BETA_TWO) * grad * grad
    scaled = second_new * (1.0 / (1.0 - BETA_TWO**STEP))
    root = scaled * lax.rsqrt(scaled)
    ratio = first_new * (1.0 / (1.0 - BETA_ONE**STEP)) / (root + ADAM_EPS)
    weight_new = weight - rate * (ratio + decay * weight)
    average_new = AVERAGE_RATE * average + (1.0 - AVERAGE_RATE) * weight_new
    return (weight_new, first_new, second_new, average_new)


def dot_nn(left, right):
    return lax.dot_general(left, right, (((1,), (0,)), ((), ())), preferred_element_type=F32)


def dot_nt(left, right):
    return lax.dot_general(left, right, (((1,), (1,)), ((), ())), preferred_element_type=F32)


def dot_tn(left, right):
    return lax.dot_general(left, right, (((0,), (0,)), ((), ())), preferred_element_type=F32)


def normal_parts(values):
    mean = jnp.mean(values, axis=-1, keepdims=True)
    centred = values - mean
    spread = jnp.mean(centred * centred, axis=-1, keepdims=True)
    inverse = lax.rsqrt(spread + NORM_EPS)
    return (centred * inverse, inverse)


def normal_back(unit, inverse, grad, gain):
    inner = grad * gain
    return inverse * (
        inner
        - jnp.mean(inner, axis=-1, keepdims=True)
        - unit * jnp.mean(inner * unit, axis=-1, keepdims=True)
    )


def fold_rows(values):
    return jnp.sum(values.reshape(-1, 8, values.shape[-1]), axis=0)


def conv_kernel(
    before, frames, after, cotangent, cols, small,
    conv_out, first_out, wide_out, cot_out, grad_rows_out, grad_t_out, rows,
):
    local = frames.shape[0]
    wide = local + 2 * KEY_RIM
    gain = small[0:1, :]
    bias = small[1:2, :]

    def norm_to(piece, start):
        unit, _ = normal_parts(piece.astype(F32))
        low = (unit * gain + bias).astype(BF16)
        first_out[pl.ds(start, piece.shape[0]), :] = low
        rows[pl.ds(start + 8, piece.shape[0]), :] = low.astype(F32)

    zero = jnp.zeros((8, rows.shape[1]), F32)
    rows[0:8, :] = zero
    rows[wide + 8 : wide + 16, :] = zero
    norm_to(before[0:KEY_RIM, :], 0)
    norm_to(after[0:KEY_RIM, :], KEY_RIM + local)

    def norm_step(step, carry):
        start = pl.multiple_of(step * CHUNK, CHUNK)
        norm_to(frames[pl.ds(start, CHUNK), :], pl.multiple_of(start + KEY_RIM, 32))
        return carry

    lax.fori_loop(0, local // CHUNK, norm_step, 0, unroll=2)
    wide_out[0:ROW_RIM, :] = before[KEY_RIM - ROW_RIM : KEY_RIM, :]
    wide_out[ROW_RIM : ROW_RIM + local, :] = frames[...]
    wide_out[ROW_RIM + local :, :] = after[0:ROW_RIM, :]
    cot_out[0:ROW_RIM, :] = before[KEY_RIM:, :]
    cot_out[ROW_RIM : ROW_RIM + local, :] = cotangent[...]
    cot_out[ROW_RIM + local :, :] = after[KEY_RIM:, :]

    def mask_step(step, carry):
        span = pl.ds(pl.multiple_of(step * QUERY_BLOCK, 32), QUERY_BLOCK)
        flags = cols[pl.ds(pl.multiple_of(step * QUERY_BLOCK + ROW_RIM, 16), QUERY_BLOCK), 2:3]
        grad_rows_out[span, :] = (cot_out[span, :].astype(F32) * flags).astype(BF16)
        return carry

    lax.fori_loop(0, cot_out.shape[0] // QUERY_BLOCK, mask_step, 0)
    grad_t_out[...] = grad_rows_out[ROW_RIM : ROW_RIM + local, :].T

    def conv_step(step, carry):
        start = pl.multiple_of(step * NARROW, NARROW)
        window = rows[pl.ds(start, NARROW + 16), :]
        flags = cols[pl.ds(start, NARROW), :]
        past = pltpu.roll(window, 1, 0)[8 : 8 + NARROW] * flags[:, 0:1]
        here = window[8 : 8 + NARROW]
        later = pltpu.roll(window, NARROW + 15, 0)[8 : 8 + NARROW] * flags[:, 1:2]
        for c in range(3):
            row = 8 + 3 * c
            mixed = (
                small[row : row + 1, :] * past
                + small[row + 1 : row + 2, :] * here
                + small[row + 2 : row + 3, :] * later
            )
            conv_out[c, pl.ds(start, NARROW), :] = mixed.astype(BF16)
        return carry

    lax.fori_loop(0, wide // NARROW, conv_step, 0)


def edges_kernel(tiles, head, tail, cot_head, cot_tail, first_out, second_out, up_out, down_out):
    first_out[...] = tiles[0].astype(BF16)
    second_out[...] = tiles[1].astype(BF16)
    up_out[0:KEY_RIM, :] = tail[...]
    up_out[KEY_RIM:, :] = cot_tail[...]
    down_out[0:KEY_RIM, :] = head[...]
    down_out[KEY_RIM:, :] = cot_head[...]


def matrices_kernel(master, low_out):
    size = master.shape[1]
    rows = pl.ds(pl.multiple_of(pl.program_id(0) * size, size), size)
    low_out[:, rows, :] = master[...].astype(BF16)


def half_kernel(place, master, bias, half_out):
    step = pl.program_id(0)
    size, units = master.shape[1:]
    half_out[pl.ds(pl.multiple_of(step * size, size), size), :] = master[0].astype(BF16)

    @pl.when(step == 0)
    def _():
        width = half_out.shape[0] - 16
        half_out[width:, :] = jnp.broadcast_to(bias[...], (16, units)).astype(BF16)


def tables_kernel(place, lengths, cols_out, codes_out):
    wide = cols_out.shape[0]
    blocks = (wide - KEY_SPAN) // QUERY_BLOCK + 1
    local = wide - 2 * KEY_RIM
    anchor = place[4] * local
    chunks = -(-wide // 128)
    height = -(-max(chunks, blocks) // 8) * 8
    row = lax.broadcasted_iota(jnp.int32, (height, 128), 0)
    lane = lax.broadcasted_iota(jnp.int32, (height, 128), 1)
    start = anchor - KEY_RIM + lane
    frame = start + row * 128
    key = start + row * QUERY_BLOCK
    zero = jnp.zeros((height, 128), jnp.int32)

    def count(j, carry):
        end, video, key_video, starts, stops = carry
        end = end + lengths[j]
        return (
            end,
            video + (frame >= end).astype(jnp.int32),
            key_video + (key >= end).astype(jnp.int32),
            starts + (frame == end).astype(jnp.int32),
            stops + (frame + 1 == end).astype(jnp.int32),
        )

    last, video, key_video, starts, stops = lax.fori_loop(
        0, lengths.shape[0], count, (jnp.int32(0), zero, zero, zero, zero)
    )
    valid = (frame >= 0) & (frame < last)
    key_valid = (key >= 0) & (key < last)
    prev = valid & (frame >= 1) & (starts == 0)
    after = valid & (frame + 1 < last) & (stops == 0)
    codes_out[...] = jnp.where(key_valid, key_video, -2).astype(F32)
    values = [prev.astype(F32), after.astype(F32), valid.astype(F32)]
    values.append(jnp.where(valid, video, -1).astype(F32))
    for c in range(chunks):
        size = min(128, wide - c * 128)
        columns = jnp.concatenate([value[c : c + 1] for value in values] * 2, axis=0).T
        cols_out[c * 128 : c * 128 + size, :] = columns[0:size]


def slots_of(owners):
    found = [owners[i] for i in range(TILES)]
    return [
        (found[i], sum([jnp.where(found[j] == found[i], 1, 0) for j in range(i)], jnp.int32(0)))
        for i in range(TILES)
    ]


def head_lanes(h):
    return slice(h * HEAD, (h + 1) * HEAD)


def head_rows(h):
    return slice(h * QUERY_BLOCK, (h + 1) * QUERY_BLOCK)


def attend_kernel(
    place, owners, *refs
):
    tiles, refs = (refs[:6], refs[6:])
    conv, cols, codes, small, *refs = refs
    weights_out, query_out, key_out, value_out, probs_out, mixed_out = refs
    rows, width = mixed_out.shape
    wide = conv.shape[1]
    depth = tiles[0].shape[0]
    for i, (owner, slot) in enumerate(slots_of(owners)):
        spot = pl.ds(i * TILE, TILE)
        core_away = (owner + place[2]) % 2
        y_away = (owner // 2 + place[1]) % 2
        z_away = place_of(place[0] ^ (owner // 4), depth)
        for r, source in enumerate(tiles[:4]):

            @pl.when((slot == 0) & (core_away * 2 + y_away == r))
            def _(source=source):
                weights_out[spot, :] = source[z_away]

        for r, source in enumerate(tiles[4:]):

            @pl.when((slot == 1) & (core_away == r))
            def _(source=source):
                weights_out[spot, :] = source[z_away, y_away]

    def matrix(c):
        return weights_out[c * width : (c + 1) * width, :]

    part = wide // 2
    for j in range(2):
        span = pl.ds(j * part, part)
        query_out[span, :] = (dot_nn(conv[0, span, :], matrix(0)) + small[4:5, :]).astype(BF16)
        key_out[span, :] = dot_nn(conv[1, span, :], matrix(1)).astype(BF16)
        value_out[span, :] = (dot_nn(conv[2, span, :], matrix(2)) + small[5:6, :]).astype(BF16)

    query_index = lax.broadcasted_iota(jnp.int32, (QUERY_BLOCK, KEY_SPAN), 0)
    key_index = lax.broadcasted_iota(jnp.int32, (QUERY_BLOCK, KEY_SPAN), 1)
    offset = query_index - key_index + (KEY_RIM - ROW_RIM)
    band = jnp.abs(offset) <= HALF
    same = offset == 0

    for step in range(rows // QUERY_BLOCK):
        start = step * QUERY_BLOCK
        query_start = start + ROW_RIM
        query_code = cols[pl.ds(query_start, QUERY_BLOCK), 3:4]
        key_code = codes[step : step + 1, :]
        allowed = band & (same | (query_code == key_code))
        scores = [
            jnp.where(
                allowed,
                dot_nt(
                    query_out[pl.ds(query_start, QUERY_BLOCK), head_lanes(h)],
                    key_out[pl.ds(start, KEY_SPAN), head_lanes(h)],
                )
                * SCALE,
                MASKED,
            )
            for h in range(HEADS)
        ]
        masked = jnp.concatenate(scores, axis=0)
        top = jnp.max(masked, axis=-1, keepdims=True)
        expo = jnp.exp(masked - top)
        probs = expo / jnp.sum(expo, axis=-1, keepdims=True)
        probs_out[step] = probs
        low = probs.astype(BF16)
        for h in range(HEADS):
            values = value_out[pl.ds(start, KEY_SPAN), head_lanes(h)]
            mixed = dot_nn(low[head_rows(h)], values)
            mixed_out[pl.ds(start, QUERY_BLOCK), head_lanes(h)] = mixed.astype(BF16)


def middle_kernel(mixed, weights, wide_rows, cols, small, middle_out, second_out, second_t_out):
    rows, width = wide_rows.shape
    part = rows // 3
    for j in range(3):
        span = pl.ds(j * part, part)
        branch = dot_nn(mixed[span, :], weights[3 * width : 4 * width, :]) + small[6:7, :]
        valid = cols[pl.ds(ROW_RIM + j * part, part), 2:3]
        middle = wide_rows[span, :].astype(F32) + valid * branch
        middle_out[span, :] = middle
        unit, _ = normal_parts(middle)
        second_out[span, :] = (unit * small[2:3, :] + small[3:4, :]).astype(BF16)
    second_t_out[...] = second_out[ROW_RIM : rows - ROW_RIM, :].T


def feed_kernel(first_call, *refs):
    place, first_matrix, second_matrix, hidden_bias, second, grad_rows, second_t, grad_t, *refs = refs
    if not first_call:
        result_in, second_grad_in, *refs = refs
    keep_out, send_out, bias_out, result, second_grad, up, down, active, hidden_grad = refs
    ways, _, units = first_matrix.shape
    width, block = up.shape
    per_piece = units // block
    rows = second.shape[0]
    local = rows - 2 * ROW_RIM
    own = slice(ROW_RIM, ROW_RIM + local)
    even = place[2] == 0
    straight = even if first_call else place[2] >= 0
    slabs, height = keep_out.shape[2:4]
    depth = slabs // 2
    if first_call:
        result[...] = jnp.zeros(result.shape, F32)
        second_grad[...] = jnp.zeros(second_grad.shape, F32)
    else:
        result[...] = result_in[...]
        second_grad[...] = second_grad_in[...]

    def block_step(step, carry):
        piece = step // per_piece
        lanes = pl.ds(pl.multiple_of((step % per_piece) * block, block), block)

        @pl.when(straight)
        def _():
            up[...] = first_matrix[piece, 0:width, lanes]
            down[...] = second_matrix[piece, 0:width, lanes]

        @pl.when(jnp.logical_not(straight))
        def _():
            up[...] = second_matrix[piece, 0:width, lanes]
            down[...] = first_matrix[piece, 0:width, lanes]

        if first_call:
            bias = first_matrix[piece, width : width + 16, lanes][0:1].astype(F32)
        else:
            bias = hidden_bias[0:1, lanes].astype(BF16).astype(F32)
        part = rows // FF_ROWS
        for j in range(FF_ROWS):
            span = pl.ds(j * part, part)
            value = dot_nn(second[span, :], up[...]) + bias
            active_grad = dot_nn(grad_rows[span, :], down[...])
            phi = 0.5 * (1.0 + lax.erf(value * (0.5**0.5)))
            density = jnp.exp(value * value * -0.5) * 0.3989422804014327
            active[span, :] = (value * phi).astype(BF16)
            hidden_grad[span, :] = (active_grad * (phi + value * density)).astype(BF16)
        result[...] += dot_nt(active[...], down[...])
        second_grad[...] += dot_nt(hidden_grad[...], up[...])
        up_grad = dot_nn(second_t[...], hidden_grad[own, :])
        down_grad = dot_nn(grad_t[...], active[own, :])
        bias_out[piece, :, lanes] = jnp.sum(
            hidden_grad[own, :].astype(F32), axis=0, keepdims=True
        )
        kept = jnp.where(even, up_grad, down_grad).astype(BF16)
        sent = jnp.where(even, down_grad, up_grad).astype(BF16)
        for slab in range(slabs):
            target = (slab // depth + place[1]) % 2 * depth + (slab % depth - place[0] + depth) % depth
            for half in range(2):
                start = (2 * slab + half) * height
                keep_out[piece, half, target, :, lanes] = kept[start : start + height]
                send_out[piece, half, target, :, lanes] = sent[start : start + height]
        return carry

    lax.fori_loop(0, ways * per_piece, block_step, 0)


def update_kernel(core_away, y_away, place, column, *refs):
    states, outs = refs[:4], refs[-8:-4]
    came, left, came_sems, left_sems = refs[-4:]
    depth, height, _ = column.shape
    matrix = (place[2] + core_away) % 2
    first_row = (place[1] + y_away) % 2 * (depth * height)

    def rows(j):
        return pl.ds(pl.multiple_of(first_row + j * height, height), height)

    def fetch(j, k):
        return pltpu.make_async_copy(
            states[k].at[matrix, rows(j)], came.at[j, k], came_sems.at[j, k]
        )

    def store(j, k):
        return pltpu.make_async_copy(
            left.at[j, k], outs[k].at[matrix, rows(j)], left_sems.at[j, k]
        )

    def start(j, carry):
        for k in range(4):
            fetch(j, k).start()
        return carry

    def update(j, carry):
        for k in range(4):
            fetch(j, k).wait()
        grad = column[(place[0] - j + depth) % depth].astype(F32)
        new = adamw(came[j, 0], grad, came[j, 1], came[j, 2], came[j, 3], MATRIX_RATE, MATRIX_DECAY)
        for k, value in enumerate(new):
            left[j, k] = value
            store(j, k).start()
        return carry

    def finish(j, carry):
        for k in range(4):
            store(j, k).wait()
        return carry

    lax.fori_loop(0, depth, start, 0)
    lax.fori_loop(0, depth, update, 0)
    lax.fori_loop(0, depth, finish, 0)


def middle_back_kernel(
    middle, cot, grad_rows, result_sum, second_sum, mixed, weights, cols, small,
    output_out, middle_grad_out, mixed_grad_out, out_grad_out, rows_out, branch,
):
    rows, width = middle.shape
    local = rows - 2 * ROW_RIM
    own = slice(ROW_RIM, ROW_RIM + local)
    rows_out[...] = jnp.zeros(rows_out.shape, F32)

    def finish(start, size, own_rows):
        span = pl.ds(start, size)
        here = middle[span, :]
        valid = cols[pl.ds(start + ROW_RIM, size), 2:3]
        unit, inverse = normal_parts(here)
        incoming = second_sum[span, :]
        back = normal_back(unit, inverse, incoming, small[2:3, :])
        middle_grad = cot[span, :].astype(F32) + back
        branch_grad = (valid * middle_grad).astype(BF16)
        branch[span, :] = branch_grad
        if own_rows:
            target = pl.ds(start - ROW_RIM, size)
            result = result_sum[span, :] + small[7:8, :]
            output_out[target, :] = (here + valid * result).astype(BF16)
            middle_grad_out[target, :] = middle_grad
            rows_out[0:8, :] += fold_rows(incoming * unit)
            rows_out[8:16, :] += fold_rows(incoming)
            rows_out[16:24, :] += fold_rows(branch_grad.astype(F32))
            rows_out[24:32, :] += fold_rows(grad_rows[span, :].astype(F32))

    finish(0, ROW_RIM, False)
    finish(ROW_RIM + local, ROW_RIM, False)

    def finish_step(j, carry):
        finish(pl.multiple_of(j * CHUNK + ROW_RIM, 16), CHUNK, True)
        return carry

    lax.fori_loop(0, local // CHUNK, finish_step, 0)
    mixed_grad_out[...] = dot_nt(branch[...], weights[3 * width : 4 * width, :]).astype(BF16)
    out_grad_out[...] = dot_tn(mixed[own, :], branch[own, :]).astype(BF16)


def scores_back_kernel(
    first_head, place, owners, query, keys, values, probs, mixed_grad, conv, out_grad,
    query_grad, key_grad, value_grad, keep_out, send_out,
    key_acc, value_acc, grads,
):
    rows, width = mixed_grad.shape
    columns = key_acc.shape[1]
    heads = columns // HEAD
    local = rows - 2 * ROW_RIM
    own = slice(ROW_RIM, ROW_RIM + local)
    wide_own = slice(KEY_RIM, KEY_RIM + local)
    key_acc[...] = jnp.zeros(key_acc.shape, F32)
    value_acc[...] = jnp.zeros(value_acc.shape, F32)
    keep_out[...] = jnp.zeros(keep_out.shape, BF16)
    send_out[...] = jnp.zeros(send_out.shape, BF16)

    for step in range(rows // QUERY_BLOCK):
        start = step * QUERY_BLOCK
        here = pl.ds(start, QUERY_BLOCK)
        span = pl.ds(start, KEY_SPAN)
        quest = pl.ds(start + ROW_RIM, QUERY_BLOCK)
        first_row = first_head * QUERY_BLOCK
        probs_here = probs[step, first_row : first_row + heads * QUERY_BLOCK, :]
        prob_grad = jnp.concatenate(
            [
                dot_nt(mixed_grad[here, head_lanes(h)], values[span, head_lanes(h)])
                for h in range(first_head, first_head + heads)
            ],
            axis=0,
        )
        inner = jnp.sum(probs_here * prob_grad, axis=-1, keepdims=True)
        score_grad = (probs_here * (prob_grad - inner)).astype(BF16)
        low = probs_here.astype(BF16)
        for h in range(heads):
            lanes, whole_lanes = head_lanes(h), head_lanes(first_head + h)
            score = score_grad[head_rows(h)]
            query_grad[here, lanes] = (dot_nn(score, keys[span, whole_lanes]) * SCALE).astype(BF16)
            key_acc[span, lanes] += dot_tn(score, query[quest, whole_lanes])
            value_acc[span, lanes] += dot_tn(low[head_rows(h)], mixed_grad[here, whole_lanes])

    inside = slice(ROW_RIM, ROW_RIM + rows)
    key_grad[...] = (key_acc[inside, :] * SCALE).astype(BF16)
    value_grad[...] = value_acc[inside, :].astype(BF16)

    for c, grad in enumerate((query_grad, key_grad, value_grad)):
        grads[c * width : (c + 1) * width, :] = dot_tn(conv[c, wide_own, :], grad[own, :]).astype(BF16)
    grads[3 * width :, :] = out_grad[:, first_head * HEAD : first_head * HEAD + columns]

    share = keep_out.shape[1]
    parts = TILE // share
    ways = CAP * parts
    depth = keep_out.shape[0] // (2 * ways)
    for i, (owner, slot) in enumerate(slots_of(owners)):
        away = (owner + place[2]) % 2
        y_away = (owner // 2 + place[1]) % 2
        z_away = (owner // 4) ^ place[0]
        for part in range(parts):
            way = (place[3] - slot * parts - part + ways) % ways
            target = (way * 2 + y_away) * depth + z_away
            here = pl.ds(i * TILE + part * share, share)

            @pl.when(away == 0)
            def _(target=target, here=here):
                keep_out[target] = grads[here, :]

            @pl.when(away == 1)
            def _(target=target, here=here):
                send_out[target] = grads[here, :]


def conv_grad_kernel(*refs):
    weights, conv_grad = refs[-2:]
    rows, columns = refs[0].shape
    width = weights.shape[1]
    part = rows // 2
    for j in range(2):
        span = pl.ds(j * part, part)
        for c in range(3):
            matrix = slice(c * width, (c + 1) * width)
            conv_grad[c, span, :] = dot_nt(refs[c][span, :], weights[matrix, 0:columns]) + dot_nt(
                refs[3 + c][span, :], weights[matrix, columns:]
            )


def conv_back_kernel(
    place, query_grad_0, value_grad_0, query_grad_1, value_grad_1, conv_grad, first, frames, feed_rows, near_bias, far_bias, cols, small,
    incoming_out, totals_out, sums,
):
    rows, columns = query_grad_0.shape
    width = frames.shape[1]
    local = rows - 2 * ROW_RIM
    sums[...] = jnp.zeros(sums.shape, F32)

    def conv_step(step, carry):
        start = pl.multiple_of(step * CHUNK, CHUNK)
        window = CHUNK + 16
        flags = cols[pl.ds(pl.multiple_of(start + KEY_RIM - 8, 8), window), :]
        span = pl.ds(pl.multiple_of(start + ROW_RIM - 8, 8), window)
        grads = [conv_grad[c, span, :] for c in range(3)]
        past = sum(small[8 + 3 * c : 9 + 3 * c, :] * grads[c] for c in range(3)) * flags[:, 0:1]
        later = sum(small[10 + 3 * c : 11 + 3 * c, :] * grads[c] for c in range(3)) * flags[:, 1:2]
        middle = slice(8, 8 + CHUNK)
        incoming = (
            sum(small[9 + 3 * c : 10 + 3 * c, :] * grads[c][middle] for c in range(3))
            + pltpu.roll(past, window - 1, 0)[middle]
            + pltpu.roll(later, 1, 0)[middle]
        )
        low = first[pl.ds(pl.multiple_of(start + KEY_RIM - 16, 16), window + 16), :].astype(F32)
        inner = slice(16, 16 + CHUNK)
        low_here = low[inner]
        low_past = pltpu.roll(low, 1, 0)[inner] * flags[middle, 0:1]
        low_later = pltpu.roll(low, window + 15, 0)[inner] * flags[middle, 1:2]
        for c in range(3):
            grad = grads[c][middle]
            base = 8 * (8 + 3 * c)
            sums[base : base + 8, :] += fold_rows(grad * low_past)
            sums[base + 8 : base + 16, :] += fold_rows(grad * low_here)
            sums[base + 16 : base + 24, :] += fold_rows(grad * low_later)
        unit, _ = normal_parts(frames[pl.ds(start, CHUNK), :].astype(F32))
        incoming_out[pl.ds(start, CHUNK), :] = incoming
        sums[0:8, :] += fold_rows(incoming * unit)
        sums[8:16, :] += fold_rows(incoming)
        here = pl.ds(pl.multiple_of(start + ROW_RIM, 16), CHUNK)
        for lanes, query_grad, value_grad in (
            (slice(0, columns), query_grad_0, value_grad_0),
            (slice(columns, width), query_grad_1, value_grad_1),
        ):
            sums[32:40, lanes] += fold_rows(query_grad[here, :].astype(F32))
            sums[40:48, lanes] += fold_rows(value_grad[here, :].astype(F32))
        return carry

    lax.fori_loop(0, local // CHUNK, conv_step, 0)
    sums[16:32, :] = feed_rows[0:16, :]
    sums[48:64, :] = feed_rows[16:32, :]
    totals_out[0:24, :] = jnp.sum(sums[...].reshape(24, 8, width), axis=1)
    totals_out[24:, :] = jnp.zeros((totals_out.shape[0] - 24, width), F32)
    units = near_bias.shape[2]
    ways = 1 + far_bias.shape[0]
    chunk = min(units, width)
    for piece in range(ways):
        source = near_bias if piece == 0 else far_bias
        for j in range(units // chunk):
            offset = (place[3] - piece + ways) % ways * units + j * chunk
            lanes = pl.ds(pl.multiple_of(offset % width, chunk), chunk)
            totals_out[pl.ds(24 + offset // width, 1), lanes] = source[
                max(piece - 1, 0), :, j * chunk : (j + 1) * chunk
            ]


def add_kernel(inputs, kinds, *refs):
    for out, parts in zip(refs[-len(kinds) :], inputs):
        count = out.shape[0]

        def step(j, carry, out=out, parts=parts, count=count):
            total = 0.0
            for index, start, *stride in parts:
                run = stride[0] // 2 if stride else count
                total = total + refs[index][start + j // run * 2 * run + j % run].astype(F32)
            out[j] = total.astype(out.dtype)
            return carry

        lax.fori_loop(0, count, step, 0)


def add_into(name, arrays, outputs, micros=0.1):
    outs = [in_place((count,) + arrays[0].shape[1:], BF16) for count, _ in outputs]
    kernel = functools.partial(add_kernel, [parts for _, parts in outputs], outs)
    return call(kernel, name, outs, micros, 8)(*arrays)


def join_kernel(first, second, out):
    count = first.shape[0]
    out[0:count] = first[...]
    out[count:] = second[...]


def joined(first, second):
    out = in_place((first.shape[0] + second.shape[0],) + first.shape[1:], first.dtype)
    return call(join_kernel, "joined", (out,), 0.1, 4)(first, second)[0]


def flipped(array, axis, bit):
    return lax.ppermute(array, axis, [(i, i ^ bit) for i in range(lax.axis_size(axis))])


def place_of(index, count):
    bits = count.bit_length() - 1
    return sum(((index >> k) & 1) << (bits - 1 - k) for k in range(bits))


def stack_kernel(*refs):
    for j, ref in enumerate(refs[:-1]):
        refs[-1][j] = ref[...]


def stacked(*arrays):
    out = in_place((len(arrays),) + arrays[0].shape, arrays[0].dtype)
    return call(stack_kernel, "stacked", (out,), 0.1, 4)(*arrays)[0]


def line_kernel(ways, *refs):
    first, second_got, totals, totals_got = refs[:ways], refs[ways : ways + 2], refs[ways + 2], refs[ways + 3]
    first_out, line_out, *second_out = refs[ways + 4 :]
    depth, piece, width = first_out.shape
    for j in range(depth):
        first_out[j] = sum(part[j].astype(F32) for part in first).astype(BF16)
        total = sum(part[depth + j].astype(F32) for part in first)
        line_out[j * piece : (j + 1) * piece, :] = total.astype(BF16)
        for d, out in enumerate(second_out):
            total = sum(part[d * depth + j].astype(F32) for part in second_got)
            out[j] = total.astype(BF16)
    low = (totals[...] + totals_got[...]).astype(BF16)
    edge = depth * piece
    line_out[edge : edge + NSMALL_ROWS, :] = low[:, 0:width]
    line_out[edge + NSMALL_ROWS :, :] = low[:, width:]


def flat_kernel(first, line, line_got, *refs):
    depth, share, width = first.shape
    second, (keep_out, send_out) = refs[:-2], refs[-2:]
    for j in range(depth):
        rows = slice(j * share, (j + 1) * share)
        left = first[j].astype(F32) + line_got[rows, :].astype(F32)
        right = sum(part[j].astype(F32) for part in second)
        if j % 2:
            out = slice(j // 2 * share, (j // 2 + 1) * share)
            send_out[out, 0:width] = left.astype(BF16)
            send_out[out, width:] = right.astype(BF16)
        else:
            keep_out[j // 2, :, 0:width] = left.astype(BF16)
            keep_out[j // 2, :, width:] = right.astype(BF16)
    edge, small = (depth * share, NSMALL_ROWS)
    low = (line[edge:, :].astype(F32) + line_got[edge:, :].astype(F32)).astype(BF16)
    send_out[depth // 2 * share :, 0:width] = low[0:small]
    send_out[depth // 2 * share :, width:] = low[small:]


def halve_kernel(keep, sent, got, keep_out, send_out):
    count, share, _ = keep.shape
    for j in range(count):
        rows = slice(j * share, (j + 1) * share)
        total = (keep[j].astype(F32) + got[rows, :].astype(F32)).astype(BF16)
        if j % 2:
            send_out[j // 2 * share : (j // 2 + 1) * share, :] = total
        else:
            keep_out[j // 2] = total
    low = sent[count * share :, :].astype(F32) + got[count * share :, :].astype(F32)
    send_out[count // 2 * share :, :] = low.astype(BF16)


def mine_kernel(keep, sent, got, out):
    share = keep.shape[1]
    out[0:share, :] = (keep[0].astype(F32) + got[0:share, :].astype(F32)).astype(BF16)
    out[share:, :] = (sent[share:, :].astype(F32) + got[share:, :].astype(F32)).astype(BF16)


def feed_line_kernel(*refs):
    depth = refs[0].shape[0]
    height = refs[0].shape[1]
    parts, outs = refs[:-depth], refs[-depth:]
    for j, out in enumerate(outs):
        out[0:height, :] = sum(part[j].astype(F32) for part in parts[:2]).astype(BF16)
        out[height:, :] = sum(part[j].astype(F32) for part in parts[2:]).astype(BF16)


def ordered_sum(parts, index):
    count = len(parts)
    total = 0.0
    for j in range(count):
        for d in range(count):
            total = total + jnp.where((index - d + count) % count == j, parts[d], 0.0)
    return total


def update_rest_kernel(place, owners, *refs):
    ways = len(refs) - 26
    shares = refs[:ways]
    attn, small, hidden = (refs[ways + k : ways + k + 4] for k in (0, 4, 8))
    attn_out, small_out, hidden_out = (refs[ways + k : ways + k + 4] for k in (12, 16, 20))
    grads, rows_held = refs[-2:]
    share = shares[0].shape[0] - NSMALL_ROWS
    width = shares[0].shape[1]
    for d in range(ways):
        grads[(place[3] - d + ways) % ways] = shares[d][0:share, :]
    totals = ordered_sum([part[share:, :].astype(F32) for part in shares], place[3])
    new = adamw(*[small[0][...], totals[0:NSMALL]], *[ref[...] for ref in small[1:]], SMALL_RATE, 0.0)
    for out, value in zip(small_out, new):
        out[...] = value
    rows_held[...] = totals[24:]
    units = hidden[0].shape[1]
    chunk = min(units, width)
    for j in range(units // chunk):
        offset = place[3] * units + j * chunk
        lanes = pl.ds(pl.multiple_of(offset % width, chunk), chunk)
        grad = rows_held[pl.ds(offset // width, 1), lanes]
        here = slice(j * chunk, (j + 1) * chunk)
        old = [ref[:, here] for ref in hidden]
        new = adamw(old[0], grad, *old[1:], SMALL_RATE, 0.0)
        for out, value in zip(hidden_out, new):
            out[:, here] = value
    seat = (place[0] * 2 + place[1]) * 2 + place[2]
    parts = TILE // share
    held = sum(jnp.where(owners[i] == seat, 1, 0) for i in range(TILES))
    for k in range(CAP):
        for part in range(parts):
            rows = slice(part * share, (part + 1) * share)
            grad = grads[k * parts + part].astype(F32)
            old = [ref[k, rows, :] for ref in attn]
            new = adamw(old[0], grad, *old[1:], MATRIX_RATE, MATRIX_DECAY)
            for out, value in zip(attn_out, new):
                out[k, rows, :] = jnp.where(held > k, value, 0.0)


def in_grad_kernel(incoming, frames, middle_grad, small, in_grad_out):
    size = CHUNK

    def step_of(step, carry):
        rows = pl.ds(pl.multiple_of(step * size, size), size)
        unit, inverse = normal_parts(frames[rows, :].astype(F32))
        back = normal_back(unit, inverse, incoming[rows, :], small[0:1, :])
        in_grad_out[rows, :] = (middle_grad[rows, :] + back).astype(BF16)
        return carry

    lax.fori_loop(0, incoming.shape[0] // size, step_of, 0)


def in_vmem(count):
    return [pl.BlockSpec(memory_space=pltpu.VMEM)] * count


def in_smem(count):
    return [pl.BlockSpec(memory_space=pltpu.SMEM)] * count


def shape(dims, kind):
    return jax.ShapeDtypeStruct(dims, kind)


def swap(array, axis):
    return lax.ppermute(array, axis, [(0, 1), (1, 0)])


def shifted(array, axis, distance):
    count = lax.axis_size(axis)
    return lax.ppermute(array, axis, [(i, (i + distance) % count) for i in range(count)])


def added(*parts):
    return functools.reduce(jnp.add, [part.astype(F32) for part in parts])


def together(*arrays):
    return lax.optimization_barrier(arrays)


def cost(micros):
    return pl.CostEstimate(
        flops=int(micros * 1.1e9), bytes_accessed=int(micros * 3.6e6), transcendentals=0
    )


def far_away(array):
    return pltpu.with_memory_space_constraint(array, pltpu.HBM)


def call(kernel, name, outs, micros, limit, scratch=(), smem=0, fetched=()):
    def run(*arrays):
        arrays = list(arrays[:smem]) + [
            far_away(array) if index in fetched else kept(array)
            for index, array in enumerate(arrays[smem:])
        ]
        return pl.pallas_call(
            kernel,
            out_shape=tuple(outs),
            in_specs=in_smem(smem) + in_vmem(len(arrays) - smem),
            out_specs=tuple(in_vmem(len(outs))),
            scratch_shapes=list(scratch),
            compiler_params=pltpu.CompilerParams(vmem_limit_bytes=limit * 1024 * 1024),
            cost_estimate=cost(micros),
            name=name,
        )(*arrays)

    return run


def kept(array):
    return pltpu.with_memory_space_constraint(array, pltpu.VMEM)


def in_place(dims, kind):
    return pltpu.VMEM(dims, kind)


def feed(place, slabs, first_matrix, second_matrix, bias, second, grad_rows, second_t, grad_t, *sums):
    ways, _, units = first_matrix.shape
    rows, width = second.shape
    block = min(FF_BLOCK, units)
    grads = in_place((ways, 2, slabs, width // slabs // 2, units), BF16)
    return call(
        functools.partial(feed_kernel, not sums),
        "feed",
        (
            grads,
            grads,
            in_place((ways, 1, units), F32),
            in_place((rows, width), F32),
            in_place((rows, width), F32),
        ),
        14,
        8,
        (
            pltpu.VMEM((width, block), BF16),
            pltpu.VMEM((width, block), BF16),
            pltpu.VMEM((rows, block), BF16),
            pltpu.VMEM((rows, block), BF16),
        ),
        smem=1,
    )(place, first_matrix, second_matrix, bias, second, grad_rows, second_t, grad_t, *sums)


def update_feed(place, core_away, y_away, column, states, done=()):
    depth, height, units = column.shape
    anywhere = pl.BlockSpec(memory_space=pl.ANY)
    return pl.pallas_call(
        functools.partial(update_kernel, core_away, y_away),
        out_shape=tuple(shape(state.shape, F32) for state in states),
        in_specs=in_smem(1) + in_vmem(1) + [anywhere] * (4 + len(done)),
        out_specs=(anywhere,) * 4,
        input_output_aliases={6 + j: j for j in range(len(done))},
        scratch_shapes=[
            pltpu.VMEM((depth, 4, height, units), F32),
            pltpu.VMEM((depth, 4, height, units), F32),
            pltpu.SemaphoreType.DMA((depth, 4)),
            pltpu.SemaphoreType.DMA((depth, 4)),
        ],
        compiler_params=pltpu.CompilerParams(vmem_limit_bytes=12 * 1024 * 1024),
        cost_estimate=cost(0.3),
        name="update_feed",
    )(place, kept(column), *[far_away(state) for state in states], *done)


def shards(
    frames,
    cotangent,
    lengths,
    owners,
    attn_master,
    attn_first,
    attn_second,
    attn_average,
    small_master,
    small_first,
    small_second,
    small_average,
    mlp_master,
    mlp_first,
    mlp_second,
    mlp_average,
    bias_master,
    bias_first,
    bias_second,
    bias_average,
):
    local, width = frames.shape
    wide = local + 2 * KEY_RIM
    rows = local + 2 * ROW_RIM
    blocks = rows // QUERY_BLOCK
    assert blocks * QUERY_BLOCK == rows and local % CHUNK == 0
    units = mlp_master.shape[2]
    ways = lax.axis_size("mlp")
    depth = lax.axis_size("z")
    devices = lax.axis_size(GROUPS)
    share = CAP * TILE // ways
    way = lax.axis_index("mlp")
    place = jnp.stack([lax.axis_index(name) for name in GROUPS + (GROUPS,)]).astype(jnp.int32)

    last = local // KEY_RIM - 1
    last_cot = local // ROW_RIM - 1
    rim = KEY_RIM + ROW_RIM
    first_tile, second_tile, to_next, to_past = pl.pallas_call(
        edges_kernel,
        grid=(1,),
        out_shape=(
            in_place((TILE, width), BF16),
            in_place((TILE, width), BF16),
            in_place((rim, width), BF16),
            in_place((rim, width), BF16),
        ),
        in_specs=[
            pl.BlockSpec((CAP, TILE, width), lambda i: (0, 0, 0)),
            pl.BlockSpec((KEY_RIM, width), lambda i: (0, 0)),
            pl.BlockSpec((KEY_RIM, width), lambda i: (last, 0)),
            pl.BlockSpec((ROW_RIM, width), lambda i: (0, 0)),
            pl.BlockSpec((ROW_RIM, width), lambda i: (last_cot, 0)),
        ],
        out_specs=tuple(in_vmem(4)),
        compiler_params=pltpu.CompilerParams(vmem_limit_bytes=8 * 1024 * 1024),
        cost_estimate=cost(1),
        name="edges",
    )(*[far_away(array) for array in (attn_master, frames, frames, cotangent, cotangent)])
    second_tile_y = swap(second_tile, "y")
    pair_b = stacked(second_tile, second_tile_y)[None]
    bits = [1 << k for k in range(depth.bit_length() - 1)][::-1]
    column_a, column_b = (first_tile[None], pair_b)

    up = [(i, i + 1) for i in range(devices - 1)]
    down = [(i + 1, i) for i in range(devices - 1)]
    before = lax.ppermute(to_next, GROUPS, up)
    after = lax.ppermute(to_past, GROUPS, down)

    edges = (before, after)
    for bit in bits[:-1]:
        got_a, got_b = (flipped(column_a, "z", bit), flipped(column_b, "z", bit))
        column_a = joined(column_a, got_a)
        column_a, column_b, edges, place_late = together(column_a, column_b, edges, place)
        column_b = joined(column_b, got_b)
    before, after = edges

    bias_row = bias_master.reshape(1, units)
    cut_rows = width // 2
    half = pl.pallas_call(
        half_kernel,
        grid_spec=pltpu.PrefetchScalarGridSpec(
            num_scalar_prefetch=1,
            grid=(2,),
            in_specs=[
                pl.BlockSpec((1, cut_rows, units), lambda i, place: (place[2], i, 0)),
                pl.BlockSpec((1, units), lambda i, place: (0, 0)),
            ],
            out_specs=pl.BlockSpec(memory_space=pltpu.VMEM),
        ),
        out_shape=in_place((width + 16, units), BF16),
        compiler_params=pltpu.CompilerParams(vmem_limit_bytes=8 * 1024 * 1024),
        cost_estimate=cost(1),
        name="half",
    )(place_late, far_away(mlp_master), bias_row)
    half_got = [shifted(half, "mlp", d) for d in range(1, ways)]
    column_a = joined(column_a, flipped(column_a, "z", 1))
    column_a, mlp_late = together(column_a, mlp_master)
    column_a_y = swap(column_a, "y")
    low_mlp = pl.pallas_call(
        matrices_kernel,
        grid=(2,),
        out_shape=in_place((2, width, units), BF16),
        in_specs=[pl.BlockSpec((2, cut_rows, units), lambda i: (0, i, 0))],
        out_specs=pl.BlockSpec(memory_space=pltpu.VMEM),
        compiler_params=pltpu.CompilerParams(vmem_limit_bytes=12 * 1024 * 1024),
        cost_estimate=cost(0.5),
        name="matrices",
    )(far_away(mlp_late))

    height = -(-max(-(-wide // 128), blocks) // 8) * 8
    cols, codes = pl.pallas_call(
        tables_kernel,
        out_shape=(in_place((wide, 8), F32), in_place((height, 128), F32)),
        in_specs=in_smem(2),
        out_specs=tuple(in_vmem(2)),
        cost_estimate=cost(1),
        name="tables",
    )(place, lengths)

    column_b_z = flipped(column_b, "z", 1)
    conv, first, wide_rows, cot, grad_rows, grad_t = call(
        conv_kernel,
        "norm_conv",
        (
            in_place((3, wide, width), BF16),
            in_place((wide, width), BF16),
            in_place((rows, width), BF16),
            in_place((rows, width), BF16),
            in_place((rows, width), BF16),
            in_place((width, local), BF16),
        ),
        0.5,
        6,
        (pltpu.VMEM((wide + 16, width), F32),),
        fetched=(1, 3),
    )(before, frames, after, cotangent, cols, small_master)

    column_b, column_a_y, conv, half_got, low_mlp = together(
        column_b, column_a_y, conv, half_got, low_mlp
    )
    column_b = joined(column_b, column_b_z)
    columns = [column_a, column_a_y, column_b]
    away = [swap(column, "core") for column in columns]
    tiles = columns[:2] + away[:2] + columns[2:] + away[2:]

    halves = half_got[0][None] if ways == 2 else stacked(*half_got)
    halves, tiles = together(halves, tiles)
    others = swap(halves, "core")
    weights, query, keys, values, probs, mixed = call(
        attend_kernel,
        "attend",
        (
            in_place((4 * width, width), BF16),
            in_place((wide, width), BF16),
            in_place((wide, width), BF16),
            in_place((wide, width), BF16),
            in_place((blocks, HEADS * QUERY_BLOCK, KEY_SPAN), F32),
            in_place((rows, width), BF16),
        ),
        0.5,
        8,
        smem=2,
    )(place, owners, *tiles, conv, cols, codes, small_master)
    others, mixed = together(others, mixed)
    middle, second, second_t = call(
        middle_kernel,
        "middle",
        (
            in_place((rows, width), F32),
            in_place((rows, width), BF16),
            in_place((width, local), BF16),
        ),
        20,
        8,
    )(mixed, weights, wide_rows, cols, small_master)

    rest = (second, grad_rows, second_t, grad_t)
    far_keep, far_send, far_bias, *sums = feed(
        place, 2 * depth, halves, others, bias_row, *rest
    )
    far_got = swap(far_send, "core")
    near_keep, near_send, near_bias, *sums = feed(
        place, 2 * depth, low_mlp[0][None], low_mlp[1][None], bias_row, *rest, *sums
    )
    near_got = swap(near_send, "core")
    pieces = range(1, ways)
    height = width // (4 * depth)

    def halves_of(array):
        return array.reshape(-1, height, units)

    def row(piece, half, y_away=0):
        return ((piece * 2 + half) * 2 + y_away) * depth

    far = add_into(
        "far_sum",
        (halves_of(far_keep), halves_of(far_got)),
        [(2 * depth, [(i, row(d - 1, 0)) for i in range(2)]) for d in pieces]
        + [(depth, [(i, row(d - 1, 1)) for i in range(2)]) for d in pieces]
        + [(depth, [(i, row(d - 1, 1, 1)) for i in range(2)]) for d in pieces],
        0.1,
    )
    far, sums = together(far, sums)
    far_x = [shifted(far[d - 1], "mlp", -d) for d in pieces]
    far_y = [swap(far[2 * (ways - 1) + d - 1], "y") for d in pieces]

    output, middle_grad, mixed_grad, out_grad, feed_rows = call(
        middle_back_kernel,
        "middle_back",
        (
            shape((local, width), BF16),
            in_place((local, width), F32),
            in_place((rows, width), BF16),
            in_place((width, width), BF16),
            in_place((32, width), F32),
        ),
        0.5,
        8,
        (pltpu.VMEM((rows, width), BF16),),
    )(middle, cot, grad_rows, *sums, mixed, weights, cols, small_master)

    near_keep, mixed_grad, far_y = together(near_keep, mixed_grad, far_y)
    near = add_into(
        "near_sum",
        (halves_of(near_keep), halves_of(near_got)),
        [(2 * depth, [(i, row(0, 0)) for i in range(2)])]
        + [(depth, [(i, row(0, 1, j)) for i in range(2)]) for j in range(2)],
        0.1,
    )
    near, mixed_grad = together(near, mixed_grad)
    near_y = swap(near[2], "y")

    columns = width // 2
    slabs = in_place((2 * ways * depth, share, columns), BF16)

    def scores_back(first_head, mixed_grad):
        return call(
            functools.partial(scores_back_kernel, first_head),
            "scores_back",
            (
                in_place((rows, columns), BF16),
                in_place((rows, columns), BF16),
                in_place((rows, columns), BF16),
                slabs,
                slabs,
            ),
            8,
            10,
            (
                pltpu.VMEM((wide, columns), F32),
                pltpu.VMEM((wide, columns), F32),
                pltpu.VMEM((4 * width, columns), BF16),
            ),
            smem=2,
        )(place, owners, query, keys, values, probs, mixed_grad, conv, out_grad)

    *grads_0, keep_0, send_0 = scores_back(0, mixed_grad)
    got_0 = swap(send_0, "core")

    arrays = (near[0], *far_x, near[1], near_y, *far[ways - 1 : 2 * (ways - 1)], *far_y)
    first_parts = list(range(ways))
    feed_two = add_into(
        "feed_two",
        arrays,
        [(depth, [(i, j * depth) for i in first_parts]) for j in range(2)]
        + [(depth, [(ways, 0), (ways + 1, 0)])]
        + [(depth, [(ways + 1 + d, 0), (2 * ways + d, 0)]) for d in pieces],
        0.1,
    )
    feed_two, mixed_grad, grads_0 = together(feed_two, mixed_grad, grads_0)
    feed_y = swap(feed_two[1], "y")
    feed_x = [shifted(feed_two[2 + d], "mlp", -d) for d in pieces]

    *grads_1, keep_1, send_1 = scores_back(HEADS // 2, mixed_grad)
    got_1 = swap(send_1, "core")
    paired_0 = add_into(
        "paired",
        (keep_0, got_0),
        [(2 * depth, [(i, 2 * depth * d) for i in range(2)]) for d in range(ways)],
        20,
    )
    feed_line = call(
        feed_line_kernel,
        "feed_line",
        tuple(in_place((2 * height, units), BF16) for _ in range(depth)),
        0.1,
        8,
    )(feed_two[0], feed_y, feed_two[2], *feed_x)
    paired_0, feed_line, keep_1, grads_1 = together(paired_0, feed_line, keep_1, grads_1)
    first_got = [shifted(paired_0[d], "mlp", -d) for d in range(1, ways)]
    feed_got = [shifted(feed_line[d], "z", d) for d in range(1, depth)]

    paired_1 = add_into(
        "paired",
        (keep_1, got_1),
        [(ways * depth, [(i, depth * j, 2 * depth) for i in range(2)]) for j in range(2)],
        0.1,
    )
    paired_1, grads_1 = together(paired_1, grads_1)
    second_got = swap(paired_1[1], "y")

    conv_grad = call(
        conv_grad_kernel, "conv_grad", (in_place((3, rows, width), F32),), 20, 8
    )(*grads_0, *grads_1, weights)[0]
    incoming, totals = call(
        conv_back_kernel,
        "conv_back",
        (in_place((local, width), F32), in_place((NSMALL_ROWS, width), F32)),
        12,
        8,
        (pltpu.VMEM((192, width), F32),),
        smem=1,
    )(
        place, grads_0[0], grads_0[2], grads_1[0], grads_1[2], conv_grad, first, frames, feed_rows,
         near_bias, far_bias, cols, small_master,
    )

    totals_got = swap(totals, "core")
    feed_keep, totals = together(feed_line[0], totals)
    feed_own = add_into(
        "feed_own",
        [part[None] for part in (feed_keep, *feed_got)],
        [(1, [(d, 0) for d in range(depth)])],
    )[0]
    feed_own, first_keep = together(feed_own, paired_0[0])
    feed_all = [shifted(feed_own[0], "z", d) for d in range(1, depth)]
    lined, line, *second = call(
        functools.partial(line_kernel, ways),
        "line",
        (
            in_place((depth, share, columns), BF16),
            in_place((depth * share + 2 * NSMALL_ROWS, columns), BF16),
        )
        + (in_place((depth, share, columns), BF16),) * ways,
        0.1,
        8,
    )(first_keep, *first_got, paired_1[0], second_got, totals, totals_got)
    lined, line, second, incoming = together(lined, line, second, incoming)
    line_got = swap(line, "y")
    second_x = [shifted(second[d], "mlp", -d) for d in range(1, ways)]
    in_grad = call(
        in_grad_kernel, "in_grad", (shape((local, width), BF16),), 20, 8, fetched=(1,)
    )(incoming, frames, middle_grad, small_master)[0]
    lined, in_grad = together(lined, in_grad)

    def slabs(count, extra):
        if extra:
            return in_place((count * share + NSMALL_ROWS, width), BF16)
        return in_place((count, share, width), BF16)

    count = depth // 2
    z_keep, z_sent = call(flat_kernel, "flat", (slabs(count, 0), slabs(count, 1)), 0.1, 8)(
        lined, line, line_got, second[0], *second_x
    )
    feed_own, z_keep, z_sent = together(feed_own, z_keep, z_sent)
    z_got = flipped(z_sent, "z", 1)
    feed_sums = [stacked(feed_own[0], *feed_all)]
    feed_sums.append(swap(feed_sums[0], "y"))
    feed_sums.append(swap(feed_sums[0], "core"))
    states = (mlp_master, mlp_first, mlp_second, mlp_average)
    mlp_new = update_feed(place, 0, 0, feed_sums[0], states)
    mlp_new, z_keep = together(mlp_new, z_keep)
    for bit in bits[::-1][1:]:
        count //= 2
        z_keep, z_sent = call(halve_kernel, "halve", (slabs(count, 0), slabs(count, 1)), 0.1, 8)(
            z_keep, z_sent, z_got
        )
        mlp_new, z_keep, z_sent = together(mlp_new, z_keep, z_sent)
        z_got = flipped(z_sent, "z", bit)
    mlp_new = update_feed(place, 1, 0, feed_sums[2], states, mlp_new)
    mlp_new, z_keep = together(mlp_new, z_keep)
    mine = call(mine_kernel, "mine", (in_place((share + NSMALL_ROWS, width), BF16),), 0.1, 8)(
        z_keep, z_sent, z_got
    )[0]
    mine, own_y, mlp_new = together(mine, feed_sums[1], mlp_new)
    shares = [mine] + [shifted(mine, "mlp", d) for d in range(1, ways)]
    other_y = swap(own_y, "core")
    mlp_new = update_feed(place, 0, 1, own_y, states, mlp_new)
    mlp_new, other_y, shares[0] = together(mlp_new, other_y, shares[0])
    mlp_new = update_feed(place, 1, 1, other_y, states, mlp_new)
    attn_shape = shape(attn_master.shape, F32)
    small_shape = shape(small_master.shape, F32)
    rest_new = call(
        update_rest_kernel,
        "update_rest",
        (attn_shape,) * 4 + (small_shape,) * 4 + (shape((1, units), F32),) * 4,
        3,
        12,
        (pltpu.VMEM((ways, share, width), BF16), pltpu.VMEM((8, width), F32)),
        smem=2,
    )(
        place, owners, *shares, attn_master, attn_first, attn_second, attn_average,
        small_master, small_first, small_second, small_average,
        *[state.reshape(1, units) for state in (bias_master, bias_first, bias_second, bias_average)],
    )

    bias_new = [part.reshape(units) for part in rest_new[8:]]
    return (
        output,
        in_grad,
        *rest_new[:8],
        *mlp_new,
        *bias_new,
    )


def solution(mesh):
    seq, mlp = mesh.devices.shape
    grid = Mesh(mesh.devices.reshape(seq // 4, 2, 2, mlp), GROUPS)
    rows = P(GROUPS, None)
    tiles = P(SEATS, None, None)
    units = P(None, None, "mlp")
    bias = P("mlp")
    in_specs = (
        (rows, rows, P(), P()) + (tiles,) * 4 + (P(),) * 4 + (units,) * 4 + (bias,) * 4
    )
    out_specs = (rows, rows) + (tiles,) * 4 + (P(),) * 4 + (units,) * 4 + (bias,) * 4
    return jax.shard_map(shards, mesh=grid, in_specs=in_specs, out_specs=out_specs, check_vma=False)
```

```python
import functools

import jax
import jax.numpy as jnp
from jax import lax
from jax.experimental import pallas as pl
from jax.experimental.pallas import tpu as pltpu
from jax.sharding import Mesh
from jax.sharding import PartitionSpec as P

HEADS = 4
HEAD = 128
HALF = 9
TILE = 128
TILES = 16
CAP = 2
STEP = 7
NSMALL = 17
NSMALL_ROWS = 32

NORM_EPS = 1e-05
MASKED = -1e30
BETA_ONE = 0.9
BETA_TWO = 0.999
ADAM_EPS = 1e-08
MATRIX_RATE = 0.03
MATRIX_DECAY = 0.05
SMALL_RATE = 0.3
AVERAGE_RATE = 0.8

F32 = jnp.float32
BF16 = jnp.bfloat16

KEY_RIM = 32
ROW_RIM = 16
QUERY_BLOCK = 96
KEY_SPAN = 128
FF_BLOCK = 512
FF_ROWS = 3
CHUNK = 128
NARROW = 64
SCALE = HEAD ** (-0.5)
GROUPS = ("z", "y", "core", "mlp")
SEATS = ("z", "y", "core")


def adamw(weight, grad, first, second, average, rate, decay):
    first_new = BETA_ONE * first + (1.0 - BETA_ONE) * grad
    second_new = BETA_TWO * second + (1.0 - BETA_TWO) * grad * grad
    scaled = second_new * (1.0 / (1.0 - BETA_TWO**STEP))
    root = scaled * lax.rsqrt(scaled)
    ratio = first_new * (1.0 / (1.0 - BETA_ONE**STEP)) / (root + ADAM_EPS)
    weight_new = weight - rate * (ratio + decay * weight)
    average_new = AVERAGE_RATE * average + (1.0 - AVERAGE_RATE) * weight_new
    return (weight_new, first_new, second_new, average_new)


def dot_nn(left, right):
    return lax.dot_general(left, right, (((1,), (0,)), ((), ())), preferred_element_type=F32)


def dot_nt(left, right):
    return lax.dot_general(left, right, (((1,), (1,)), ((), ())), preferred_element_type=F32)


def dot_tn(left, right):
    return lax.dot_general(left, right, (((0,), (0,)), ((), ())), preferred_element_type=F32)


def normal_parts(values):
    mean = jnp.mean(values, axis=-1, keepdims=True)
    centred = values - mean
    spread = jnp.mean(centred * centred, axis=-1, keepdims=True)
    inverse = lax.rsqrt(spread + NORM_EPS)
    return (centred * inverse, inverse)


def normal_back(unit, inverse, grad, gain):
    inner = grad * gain
    return inverse * (
        inner
        - jnp.mean(inner, axis=-1, keepdims=True)
        - unit * jnp.mean(inner * unit, axis=-1, keepdims=True)
    )


def fold_rows(values):
    return jnp.sum(values.reshape(-1, 8, values.shape[-1]), axis=0)


def conv_kernel(
    before, frames, after, cotangent, cols, small,
    conv_out, first_out, wide_out, cot_out, grad_rows_out, grad_t_out, rows,
):
    local = frames.shape[0]
    wide = local + 2 * KEY_RIM
    gain = small[0:1, :]
    bias = small[1:2, :]

    def norm_to(piece, start):
        unit, _ = normal_parts(piece.astype(F32))
        low = (unit * gain + bias).astype(BF16)
        first_out[pl.ds(start, piece.shape[0]), :] = low
        rows[pl.ds(start + 8, piece.shape[0]), :] = low.astype(F32)

    zero = jnp.zeros((8, rows.shape[1]), F32)
    rows[0:8, :] = zero
    rows[wide + 8 : wide + 16, :] = zero
    norm_to(before[0:KEY_RIM, :], 0)
    norm_to(after[0:KEY_RIM, :], KEY_RIM + local)

    def norm_step(step, carry):
        start = pl.multiple_of(step * CHUNK, CHUNK)
        norm_to(frames[pl.ds(start, CHUNK), :], pl.multiple_of(start + KEY_RIM, 32))
        return carry

    lax.fori_loop(0, local // CHUNK, norm_step, 0, unroll=2)
    wide_out[0:ROW_RIM, :] = before[KEY_RIM - ROW_RIM : KEY_RIM, :]
    wide_out[ROW_RIM : ROW_RIM + local, :] = frames[...]
    wide_out[ROW_RIM + local :, :] = after[0:ROW_RIM, :]
    cot_out[0:ROW_RIM, :] = before[KEY_RIM:, :]
    cot_out[ROW_RIM : ROW_RIM + local, :] = cotangent[...]
    cot_out[ROW_RIM + local :, :] = after[KEY_RIM:, :]

    def mask_step(step, carry):
        span = pl.ds(pl.multiple_of(step * QUERY_BLOCK, 32), QUERY_BLOCK)
        flags = cols[pl.ds(pl.multiple_of(step * QUERY_BLOCK + ROW_RIM, 16), QUERY_BLOCK), 2:3]
        grad_rows_out[span, :] = (cot_out[span, :].astype(F32) * flags).astype(BF16)
        return carry

    lax.fori_loop(0, cot_out.shape[0] // QUERY_BLOCK, mask_step, 0)
    grad_t_out[...] = grad_rows_out[ROW_RIM : ROW_RIM + local, :].T

    def conv_step(step, carry):
        start = pl.multiple_of(step * NARROW, NARROW)
        window = rows[pl.ds(start, NARROW + 16), :]
        flags = cols[pl.ds(start, NARROW), :]
        past = pltpu.roll(window, 1, 0)[8 : 8 + NARROW] * flags[:, 0:1]
        here = window[8 : 8 + NARROW]
        later = pltpu.roll(window, NARROW + 15, 0)[8 : 8 + NARROW] * flags[:, 1:2]
        for c in range(3):
            row = 8 + 3 * c
            mixed = (
                small[row : row + 1, :] * past
                + small[row + 1 : row + 2, :] * here
                + small[row + 2 : row + 3, :] * later
            )
            conv_out[c, pl.ds(start, NARROW), :] = mixed.astype(BF16)
        return carry

    lax.fori_loop(0, wide // NARROW, conv_step, 0)


def edges_kernel(tiles, head, tail, cot_head, cot_tail, first_out, second_out, up_out, down_out):
    first_out[...] = tiles[0].astype(BF16)
    second_out[...] = tiles[1].astype(BF16)
    up_out[0:KEY_RIM, :] = tail[...]
    up_out[KEY_RIM:, :] = cot_tail[...]
    down_out[0:KEY_RIM, :] = head[...]
    down_out[KEY_RIM:, :] = cot_head[...]


def matrices_kernel(master, low_out):
    size = master.shape[1]
    rows = pl.ds(pl.multiple_of(pl.program_id(0) * size, size), size)
    low_out[:, rows, :] = master[...].astype(BF16)


def half_kernel(place, master, bias, half_out):
    step = pl.program_id(0)
    size, units = master.shape[1:]
    half_out[pl.ds(pl.multiple_of(step * size, size), size), :] = master[0].astype(BF16)

    @pl.when(step == 0)
    def _():
        width = half_out.shape[0] - 16
        half_out[width:, :] = jnp.broadcast_to(bias[...], (16, units)).astype(BF16)


def tables_kernel(place, lengths, cols_out, codes_out):
    wide = cols_out.shape[0]
    blocks = (wide - KEY_SPAN) // QUERY_BLOCK + 1
    local = wide - 2 * KEY_RIM
    anchor = place[4] * local
    chunks = -(-wide // 128)
    height = -(-max(chunks, blocks) // 8) * 8
    row = lax.broadcasted_iota(jnp.int32, (height, 128), 0)
    lane = lax.broadcasted_iota(jnp.int32, (height, 128), 1)
    start = anchor - KEY_RIM + lane
    frame = start + row * 128
    key = start + row * QUERY_BLOCK
    zero = jnp.zeros((height, 128), jnp.int32)

    def count(j, carry):
        end, video, key_video, starts, stops = carry
        end = end + lengths[j]
        return (
            end,
            video + (frame >= end).astype(jnp.int32),
            key_video + (key >= end).astype(jnp.int32),
            starts + (frame == end).astype(jnp.int32),
            stops + (frame + 1 == end).astype(jnp.int32),
        )

    last, video, key_video, starts, stops = lax.fori_loop(
        0, lengths.shape[0], count, (jnp.int32(0), zero, zero, zero, zero)
    )
    valid = (frame >= 0) & (frame < last)
    key_valid = (key >= 0) & (key < last)
    prev = valid & (frame >= 1) & (starts == 0)
    after = valid & (frame + 1 < last) & (stops == 0)
    codes_out[...] = jnp.where(key_valid, key_video, -2).astype(F32)
    values = [prev.astype(F32), after.astype(F32), valid.astype(F32)]
    values.append(jnp.where(valid, video, -1).astype(F32))
    for c in range(chunks):
        size = min(128, wide - c * 128)
        columns = jnp.concatenate([value[c : c + 1] for value in values] * 2, axis=0).T
        cols_out[c * 128 : c * 128 + size, :] = columns[0:size]


def slot_of(owners, i):
    owner = owners[i]
    return owner, sum(jnp.where((owners[j] == owner) & (j < i), 1, 0) for j in range(TILES))


def slots_of(owners):
    found = [owners[i] for i in range(TILES)]
    return [
        (found[i], sum([jnp.where(found[j] == found[i], 1, 0) for j in range(i)], jnp.int32(0)))
        for i in range(TILES)
    ]


def head_lanes(h):
    return slice(h * HEAD, (h + 1) * HEAD)


def head_rows(h):
    return slice(h * QUERY_BLOCK, (h + 1) * QUERY_BLOCK)


def attend_kernel(
    place, owners, *refs
):
    tiles, refs = (refs[:8], refs[8:])
    conv, cols, codes, small, *refs = refs
    weights_out, query_out, key_out, value_out, probs_out, mixed_out = refs
    rows, width = mixed_out.shape
    wide = conv.shape[1]
    depth = tiles[0].shape[0]
    def tile_step(i, carry):
        owner, slot = slot_of(owners, i)
        spot = pl.ds(pl.multiple_of(i * TILE, TILE), TILE)
        core_away = (owner + place[2]) % 2
        y_away = (owner // 2 + place[1]) % 2
        z_away = place_of(place[0] ^ (owner // 4), depth)
        late = z_away // (depth // 2)
        for r, source in enumerate(tiles[:4]):

            @pl.when((slot == 0) & (core_away * 2 + y_away == r))
            def _(source=source):
                weights_out[spot, :] = source[z_away]

        for r, source in enumerate(tiles[4:]):

            @pl.when((slot == 1) & (core_away * 2 + late == r))
            def _(source=source):
                weights_out[spot, :] = source[z_away % (depth // 2), y_away]

        return carry

    lax.fori_loop(0, TILES, tile_step, 0)

    def matrix(c):
        return weights_out[c * width : (c + 1) * width, :]

    part = wide // 2
    for j in range(2):
        span = pl.ds(j * part, part)
        query_out[span, :] = (dot_nn(conv[0, span, :], matrix(0)) + small[4:5, :]).astype(BF16)
        key_out[span, :] = dot_nn(conv[1, span, :], matrix(1)).astype(BF16)
        value_out[span, :] = (dot_nn(conv[2, span, :], matrix(2)) + small[5:6, :]).astype(BF16)

    query_index = lax.broadcasted_iota(jnp.int32, (QUERY_BLOCK, KEY_SPAN), 0)
    key_index = lax.broadcasted_iota(jnp.int32, (QUERY_BLOCK, KEY_SPAN), 1)
    offset = query_index - key_index + (KEY_RIM - ROW_RIM)
    band = jnp.abs(offset) <= HALF
    same = offset == 0

    for step in range(rows // QUERY_BLOCK):
        start = step * QUERY_BLOCK
        query_start = start + ROW_RIM
        query_code = cols[pl.ds(query_start, QUERY_BLOCK), 3:4]
        key_code = codes[step : step + 1, :]
        allowed = band & (same | (query_code == key_code))
        scores = [
            jnp.where(
                allowed,
                dot_nt(
                    query_out[pl.ds(query_start, QUERY_BLOCK), head_lanes(h)],
                    key_out[pl.ds(start, KEY_SPAN), head_lanes(h)],
                )
                * SCALE,
                MASKED,
            )
            for h in range(HEADS)
        ]
        masked = jnp.concatenate(scores, axis=0)
        top = jnp.max(masked, axis=-1, keepdims=True)
        expo = jnp.exp(masked - top)
        probs = expo / jnp.sum(expo, axis=-1, keepdims=True)
        probs_out[step] = probs
        low = probs.astype(BF16)
        for h in range(HEADS):
            values = value_out[pl.ds(start, KEY_SPAN), head_lanes(h)]
            mixed = dot_nn(low[head_rows(h)], values)
            mixed_out[pl.ds(start, QUERY_BLOCK), head_lanes(h)] = mixed.astype(BF16)


def middle_kernel(mixed, weights, wide_rows, cols, small, middle_out, second_out, second_t_out):
    rows, width = wide_rows.shape
    part = rows // 3
    for j in range(3):
        span = pl.ds(j * part, part)
        branch = dot_nn(mixed[span, :], weights[3 * width : 4 * width, :]) + small[6:7, :]
        valid = cols[pl.ds(ROW_RIM + j * part, part), 2:3]
        middle = wide_rows[span, :].astype(F32) + valid * branch
        middle_out[span, :] = middle
        unit, _ = normal_parts(middle)
        second_out[span, :] = (unit * small[2:3, :] + small[3:4, :]).astype(BF16)
    second_t_out[...] = second_out[ROW_RIM : rows - ROW_RIM, :].T


def feed_kernel(first_call, *refs):
    place, first_matrix, second_matrix, hidden_bias, second, grad_rows, second_t, grad_t, *refs = refs
    if not first_call:
        result_in, second_grad_in, *refs = refs
    keep_out, send_out, bias_out, result, second_grad, up, down, active, hidden_grad = refs
    ways, _, units = first_matrix.shape
    width, block = up.shape
    per_piece = units // block
    rows = second.shape[0]
    local = rows - 2 * ROW_RIM
    own = slice(ROW_RIM, ROW_RIM + local)
    even = place[2] == 0
    straight = even if first_call else place[2] >= 0
    slabs, height = keep_out.shape[2:4]
    depth = slabs // 2
    if first_call:
        result[...] = jnp.zeros(result.shape, F32)
        second_grad[...] = jnp.zeros(second_grad.shape, F32)
    else:
        result[...] = result_in[...]
        second_grad[...] = second_grad_in[...]

    def block_step(step, carry):
        piece = step // per_piece
        lanes = pl.ds(pl.multiple_of((step % per_piece) * block, block), block)

        @pl.when(straight)
        def _():
            up[...] = first_matrix[piece, 0:width, lanes]
            down[...] = second_matrix[piece, 0:width, lanes]

        @pl.when(jnp.logical_not(straight))
        def _():
            up[...] = second_matrix[piece, 0:width, lanes]
            down[...] = first_matrix[piece, 0:width, lanes]

        if first_call:
            bias = first_matrix[piece, width : width + 16, lanes][0:1].astype(F32)
        else:
            bias = hidden_bias[0:1, lanes].astype(BF16).astype(F32)
        part = rows // FF_ROWS
        for j in range(FF_ROWS):
            span = pl.ds(j * part, part)
            value = dot_nn(second[span, :], up[...]) + bias
            active_grad = dot_nn(grad_rows[span, :], down[...])
            phi = 0.5 * (1.0 + lax.erf(value * (0.5**0.5)))
            density = jnp.exp(value * value * -0.5) * 0.3989422804014327
            active[span, :] = (value * phi).astype(BF16)
            hidden_grad[span, :] = (active_grad * (phi + value * density)).astype(BF16)
        result[...] += dot_nt(active[...], down[...])
        second_grad[...] += dot_nt(hidden_grad[...], up[...])
        up_grad = dot_nn(second_t[...], hidden_grad[own, :])
        down_grad = dot_nn(grad_t[...], active[own, :])
        bias_out[piece, :, lanes] = jnp.sum(
            hidden_grad[own, :].astype(F32), axis=0, keepdims=True
        )
        kept = jnp.where(even, up_grad, down_grad).astype(BF16)
        sent = jnp.where(even, down_grad, up_grad).astype(BF16)
        for slab in range(slabs):
            target = (slab // depth + place[1]) % 2 * depth + (slab % depth - place[0] + depth) % depth
            for half in range(2):
                start = (2 * slab + half) * height
                keep_out[piece, half, target, :, lanes] = kept[start : start + height]
                send_out[piece, half, target, :, lanes] = sent[start : start + height]
        return carry

    lax.fori_loop(0, ways * per_piece, block_step, 0)


def update_kernel(core_away, y_away, place, column, *refs):
    states, outs = refs[:4], refs[-8:-4]
    came, left, came_sems, left_sems = refs[-4:]
    depth, height, _ = column.shape
    matrix = (place[2] + core_away) % 2
    first_row = (place[1] + y_away) % 2 * (depth * height)

    def rows(j):
        return pl.ds(pl.multiple_of(first_row + j * height, height), height)

    def fetch(j, k):
        return pltpu.make_async_copy(
            states[k].at[matrix, rows(j)], came.at[j, k], came_sems.at[j, k]
        )

    def store(j, k):
        return pltpu.make_async_copy(
            left.at[j, k], outs[k].at[matrix, rows(j)], left_sems.at[j, k]
        )

    def start(j, carry):
        for k in range(4):
            fetch(j, k).start()
        return carry

    def update(j, carry):
        for k in range(4):
            fetch(j, k).wait()
        grad = column[(place[0] - j + depth) % depth].astype(F32)
        new = adamw(came[j, 0], grad, came[j, 1], came[j, 2], came[j, 3], MATRIX_RATE, MATRIX_DECAY)
        for k, value in enumerate(new):
            left[j, k] = value
            store(j, k).start()
        return carry

    def finish(j, carry):
        for k in range(4):
            store(j, k).wait()
        return carry

    lax.fori_loop(0, depth, start, 0)
    lax.fori_loop(0, depth, update, 0)
    lax.fori_loop(0, depth, finish, 0)


def middle_back_kernel(
    middle, cot, grad_rows, result_sum, second_sum, mixed, weights, cols, small,
    output_out, middle_grad_out, mixed_grad_out, out_grad_out, rows_out, branch,
):
    rows, width = middle.shape
    local = rows - 2 * ROW_RIM
    own = slice(ROW_RIM, ROW_RIM + local)
    rows_out[...] = jnp.zeros(rows_out.shape, F32)

    def finish(start, size, own_rows):
        span = pl.ds(start, size)
        here = middle[span, :]
        valid = cols[pl.ds(start + ROW_RIM, size), 2:3]
        unit, inverse = normal_parts(here)
        incoming = second_sum[span, :]
        back = normal_back(unit, inverse, incoming, small[2:3, :])
        middle_grad = cot[span, :].astype(F32) + back
        branch_grad = (valid * middle_grad).astype(BF16)
        branch[span, :] = branch_grad
        if own_rows:
            target = pl.ds(start - ROW_RIM, size)
            result = result_sum[span, :] + small[7:8, :]
            output_out[target, :] = (here + valid * result).astype(BF16)
            middle_grad_out[target, :] = middle_grad
            rows_out[0:8, :] += fold_rows(incoming * unit)
            rows_out[8:16, :] += fold_rows(incoming)
            rows_out[16:24, :] += fold_rows(branch_grad.astype(F32))
            rows_out[24:32, :] += fold_rows(grad_rows[span, :].astype(F32))

    finish(0, ROW_RIM, False)
    finish(ROW_RIM + local, ROW_RIM, False)

    def finish_step(j, carry):
        finish(pl.multiple_of(j * CHUNK + ROW_RIM, 16), CHUNK, True)
        return carry

    lax.fori_loop(0, local // CHUNK, finish_step, 0)
    mixed_grad_out[...] = dot_nt(branch[...], weights[3 * width : 4 * width, :]).astype(BF16)
    out_grad_out[...] = dot_tn(mixed[own, :], branch[own, :]).astype(BF16)


def scores_back_kernel(
    first_head, place, owners, query, keys, values, probs, mixed_grad, conv, out_grad,
    query_grad, key_grad, value_grad, keep_out, send_out,
    key_acc, value_acc, grads,
):
    rows, width = mixed_grad.shape
    columns = key_acc.shape[1]
    heads = columns // HEAD
    local = rows - 2 * ROW_RIM
    own = slice(ROW_RIM, ROW_RIM + local)
    wide_own = slice(KEY_RIM, KEY_RIM + local)
    key_acc[...] = jnp.zeros(key_acc.shape, F32)
    value_acc[...] = jnp.zeros(value_acc.shape, F32)
    keep_out[...] = jnp.zeros(keep_out.shape, BF16)
    send_out[...] = jnp.zeros(send_out.shape, BF16)

    for step in range(rows // QUERY_BLOCK):
        start = step * QUERY_BLOCK
        here = pl.ds(start, QUERY_BLOCK)
        span = pl.ds(start, KEY_SPAN)
        quest = pl.ds(start + ROW_RIM, QUERY_BLOCK)
        first_row = first_head * QUERY_BLOCK
        probs_here = probs[step, first_row : first_row + heads * QUERY_BLOCK, :]
        prob_grad = jnp.concatenate(
            [
                dot_nt(mixed_grad[here, head_lanes(h)], values[span, head_lanes(h)])
                for h in range(first_head, first_head + heads)
            ],
            axis=0,
        )
        inner = jnp.sum(probs_here * prob_grad, axis=-1, keepdims=True)
        score_grad = (probs_here * (prob_grad - inner)).astype(BF16)
        low = probs_here.astype(BF16)
        for h in range(heads):
            lanes, whole_lanes = head_lanes(h), head_lanes(first_head + h)
            score = score_grad[head_rows(h)]
            query_grad[here, lanes] = (dot_nn(score, keys[span, whole_lanes]) * SCALE).astype(BF16)
            key_acc[span, lanes] += dot_tn(score, query[quest, whole_lanes])
            value_acc[span, lanes] += dot_tn(low[head_rows(h)], mixed_grad[here, whole_lanes])

    inside = slice(ROW_RIM, ROW_RIM + rows)
    key_grad[...] = (key_acc[inside, :] * SCALE).astype(BF16)
    value_grad[...] = value_acc[inside, :].astype(BF16)

    for c, grad in enumerate((query_grad, key_grad, value_grad)):
        grads[c * width : (c + 1) * width, :] = dot_tn(conv[c, wide_own, :], grad[own, :]).astype(BF16)
    grads[3 * width :, :] = out_grad[:, first_head * HEAD : first_head * HEAD + columns]

    share = keep_out.shape[1]
    parts = TILE // share
    ways = CAP * parts
    depth = keep_out.shape[0] // (2 * ways)
    for i, (owner, slot) in enumerate(slots_of(owners)):
        away = (owner + place[2]) % 2
        y_away = (owner // 2 + place[1]) % 2
        z_away = (owner // 4) ^ place[0]
        for part in range(parts):
            way = (place[3] - slot * parts - part + ways) % ways
            target = (way * 2 + y_away) * depth + z_away
            here = pl.ds(i * TILE + part * share, share)

            @pl.when(away == 0)
            def _(target=target, here=here):
                keep_out[target] = grads[here, :]

            @pl.when(away == 1)
            def _(target=target, here=here):
                send_out[target] = grads[here, :]


def conv_grad_kernel(*refs):
    weights, conv_grad = refs[-2:]
    rows, columns = refs[0].shape
    width = weights.shape[1]
    part = rows // 2
    for j in range(2):
        span = pl.ds(j * part, part)
        for c in range(3):
            matrix = slice(c * width, (c + 1) * width)
            conv_grad[c, span, :] = dot_nt(refs[c][span, :], weights[matrix, 0:columns]) + dot_nt(
                refs[3 + c][span, :], weights[matrix, columns:]
            )


def conv_back_kernel(
    place, query_grad_0, value_grad_0, query_grad_1, value_grad_1, conv_grad, first, frames, feed_rows, near_bias, far_bias, cols, small,
    incoming_out, totals_out, sums,
):
    rows, columns = query_grad_0.shape
    width = frames.shape[1]
    local = rows - 2 * ROW_RIM
    sums[...] = jnp.zeros(sums.shape, F32)

    def conv_step(step, carry):
        start = pl.multiple_of(step * CHUNK, CHUNK)
        window = CHUNK + 16
        flags = cols[pl.ds(pl.multiple_of(start + KEY_RIM - 8, 8), window), :]
        span = pl.ds(pl.multiple_of(start + ROW_RIM - 8, 8), window)
        grads = [conv_grad[c, span, :] for c in range(3)]
        past = sum(small[8 + 3 * c : 9 + 3 * c, :] * grads[c] for c in range(3)) * flags[:, 0:1]
        later = sum(small[10 + 3 * c : 11 + 3 * c, :] * grads[c] for c in range(3)) * flags[:, 1:2]
        middle = slice(8, 8 + CHUNK)
        incoming = (
            sum(small[9 + 3 * c : 10 + 3 * c, :] * grads[c][middle] for c in range(3))
            + pltpu.roll(past, window - 1, 0)[middle]
            + pltpu.roll(later, 1, 0)[middle]
        )
        low = first[pl.ds(pl.multiple_of(start + KEY_RIM - 16, 16), window + 16), :].astype(F32)
        inner = slice(16, 16 + CHUNK)
        low_here = low[inner]
        low_past = pltpu.roll(low, 1, 0)[inner] * flags[middle, 0:1]
        low_later = pltpu.roll(low, window + 15, 0)[inner] * flags[middle, 1:2]
        for c in range(3):
            grad = grads[c][middle]
            base = 8 * (8 + 3 * c)
            sums[base : base + 8, :] += fold_rows(grad * low_past)
            sums[base + 8 : base + 16, :] += fold_rows(grad * low_here)
            sums[base + 16 : base + 24, :] += fold_rows(grad * low_later)
        unit, _ = normal_parts(frames[pl.ds(start, CHUNK), :].astype(F32))
        incoming_out[pl.ds(start, CHUNK), :] = incoming
        sums[0:8, :] += fold_rows(incoming * unit)
        sums[8:16, :] += fold_rows(incoming)
        here = pl.ds(pl.multiple_of(start + ROW_RIM, 16), CHUNK)
        for lanes, query_grad, value_grad in (
            (slice(0, columns), query_grad_0, value_grad_0),
            (slice(columns, width), query_grad_1, value_grad_1),
        ):
            sums[32:40, lanes] += fold_rows(query_grad[here, :].astype(F32))
            sums[40:48, lanes] += fold_rows(value_grad[here, :].astype(F32))
        return carry

    lax.fori_loop(0, local // CHUNK, conv_step, 0)
    sums[16:32, :] = feed_rows[0:16, :]
    sums[48:64, :] = feed_rows[16:32, :]
    totals_out[0:24, :] = jnp.sum(sums[...].reshape(24, 8, width), axis=1)
    totals_out[24:, :] = jnp.zeros((totals_out.shape[0] - 24, width), F32)
    units = near_bias.shape[2]
    ways = 1 + far_bias.shape[0]
    chunk = min(units, width)
    for piece in range(ways):
        source = near_bias if piece == 0 else far_bias
        for j in range(units // chunk):
            offset = (place[3] - piece + ways) % ways * units + j * chunk
            lanes = pl.ds(pl.multiple_of(offset % width, chunk), chunk)
            totals_out[pl.ds(24 + offset // width, 1), lanes] = source[
                max(piece - 1, 0), :, j * chunk : (j + 1) * chunk
            ]


def add_kernel(inputs, kinds, *refs):
    for out, parts in zip(refs[-len(kinds) :], inputs):
        count = out.shape[0]

        def step(j, carry, out=out, parts=parts, count=count):
            total = 0.0
            for index, start, *stride in parts:
                run = stride[0] // 2 if stride else count
                total = total + refs[index][start + j // run * 2 * run + j % run].astype(F32)
            out[j] = total.astype(out.dtype)
            return carry

        lax.fori_loop(0, count, step, 0)


def add_into(name, arrays, outputs, micros=0.1):
    outs = [in_place((count,) + arrays[0].shape[1:], BF16) for count, _ in outputs]
    kernel = functools.partial(add_kernel, [parts for _, parts in outputs], outs)
    return call(kernel, name, outs, micros, 8)(*arrays)


def join_kernel(first, second, out):
    count = first.shape[0]
    out[0:count] = first[...]
    out[count:] = second[...]


def joined(first, second):
    out = in_place((first.shape[0] + second.shape[0],) + first.shape[1:], first.dtype)
    return call(join_kernel, "joined", (out,), 0.1, 4)(first, second)[0]


def flipped(array, axis, bit):
    return lax.ppermute(array, axis, [(i, i ^ bit) for i in range(lax.axis_size(axis))])


def place_of(index, count):
    bits = count.bit_length() - 1
    return sum(((index >> k) & 1) << (bits - 1 - k) for k in range(bits))


def stack_kernel(*refs):
    for j, ref in enumerate(refs[:-1]):
        refs[-1][j] = ref[...]


def stacked(*arrays):
    out = in_place((len(arrays),) + arrays[0].shape, arrays[0].dtype)
    return call(stack_kernel, "stacked", (out,), 0.1, 4)(*arrays)[0]


def line_kernel(ways, *refs):
    first, second_got, totals, totals_got = refs[:ways], refs[ways : ways + 2], refs[ways + 2], refs[ways + 3]
    first_out, line_out, *second_out = refs[ways + 4 :]
    depth, piece, width = first_out.shape
    for j in range(depth):
        first_out[j] = sum(part[j].astype(F32) for part in first).astype(BF16)
        total = sum(part[depth + j].astype(F32) for part in first)
        line_out[j * piece : (j + 1) * piece, :] = total.astype(BF16)
        for d, out in enumerate(second_out):
            total = sum(part[d * depth + j].astype(F32) for part in second_got)
            out[j] = total.astype(BF16)
    low = (totals[...] + totals_got[...]).astype(BF16)
    edge = depth * piece
    line_out[edge : edge + NSMALL_ROWS, :] = low[:, 0:width]
    line_out[edge + NSMALL_ROWS :, :] = low[:, width:]


def flat_kernel(first, line, line_got, *refs):
    depth, share, width = first.shape
    second, (keep_out, send_out) = refs[:-2], refs[-2:]
    for j in range(depth):
        rows = slice(j * share, (j + 1) * share)
        left = first[j].astype(F32) + line_got[rows, :].astype(F32)
        right = sum(part[j].astype(F32) for part in second)
        if j % 2:
            out = slice(j // 2 * share, (j // 2 + 1) * share)
            send_out[out, 0:width] = left.astype(BF16)
            send_out[out, width:] = right.astype(BF16)
        else:
            keep_out[j // 2, :, 0:width] = left.astype(BF16)
            keep_out[j // 2, :, width:] = right.astype(BF16)
    edge, small = (depth * share, NSMALL_ROWS)
    low = (line[edge:, :].astype(F32) + line_got[edge:, :].astype(F32)).astype(BF16)
    send_out[depth // 2 * share :, 0:width] = low[0:small]
    send_out[depth // 2 * share :, width:] = low[small:]


def halve_kernel(keep, sent, got, keep_out, send_out):
    count, share, _ = keep.shape
    for j in range(count):
        rows = slice(j * share, (j + 1) * share)
        total = (keep[j].astype(F32) + got[rows, :].astype(F32)).astype(BF16)
        if j % 2:
            send_out[j // 2 * share : (j // 2 + 1) * share, :] = total
        else:
            keep_out[j // 2] = total
    low = sent[count * share :, :].astype(F32) + got[count * share :, :].astype(F32)
    send_out[count // 2 * share :, :] = low.astype(BF16)


def mine_kernel(keep, sent, got, out):
    share = keep.shape[1]
    out[0:share, :] = (keep[0].astype(F32) + got[0:share, :].astype(F32)).astype(BF16)
    out[share:, :] = (sent[share:, :].astype(F32) + got[share:, :].astype(F32)).astype(BF16)


def feed_line_kernel(*refs):
    depth = refs[0].shape[0]
    height = refs[0].shape[1]
    parts, outs = refs[:-depth], refs[-depth:]
    for j, out in enumerate(outs):
        out[0:height, :] = sum(part[j].astype(F32) for part in parts[:2]).astype(BF16)
        out[height:, :] = sum(part[j].astype(F32) for part in parts[2:]).astype(BF16)


def ordered_sum(parts, index):
    count = len(parts)
    total = 0.0
    for j in range(count):
        for d in range(count):
            total = total + jnp.where((index - d + count) % count == j, parts[d], 0.0)
    return total


def update_rest_kernel(place, owners, *refs):
    ways = len(refs) - 26
    shares = refs[:ways]
    attn, small, hidden = (refs[ways + k : ways + k + 4] for k in (0, 4, 8))
    attn_out, small_out, hidden_out = (refs[ways + k : ways + k + 4] for k in (12, 16, 20))
    grads, rows_held = refs[-2:]
    share = shares[0].shape[0] - NSMALL_ROWS
    width = shares[0].shape[1]
    for d in range(ways):
        grads[(place[3] - d + ways) % ways] = shares[d][0:share, :]
    totals = ordered_sum([part[share:, :].astype(F32) for part in shares], place[3])
    new = adamw(*[small[0][...], totals[0:NSMALL]], *[ref[...] for ref in small[1:]], SMALL_RATE, 0.0)
    for out, value in zip(small_out, new):
        out[...] = value
    rows_held[...] = totals[24:]
    units = hidden[0].shape[1]
    chunk = min(units, width)
    for j in range(units // chunk):
        offset = place[3] * units + j * chunk
        lanes = pl.ds(pl.multiple_of(offset % width, chunk), chunk)
        grad = rows_held[pl.ds(offset // width, 1), lanes]
        here = slice(j * chunk, (j + 1) * chunk)
        old = [ref[:, here] for ref in hidden]
        new = adamw(old[0], grad, *old[1:], SMALL_RATE, 0.0)
        for out, value in zip(hidden_out, new):
            out[:, here] = value
    seat = (place[0] * 2 + place[1]) * 2 + place[2]
    parts = TILE // share
    held = sum(jnp.where(owners[i] == seat, 1, 0) for i in range(TILES))
    for k in range(CAP):
        for part in range(parts):
            rows = slice(part * share, (part + 1) * share)
            grad = grads[k * parts + part].astype(F32)
            old = [ref[k, rows, :] for ref in attn]
            new = adamw(old[0], grad, *old[1:], MATRIX_RATE, MATRIX_DECAY)
            for out, value in zip(attn_out, new):
                out[k, rows, :] = jnp.where(held > k, value, 0.0)


def in_grad_kernel(incoming, frames, middle_grad, small, in_grad_out):
    size = CHUNK

    def step_of(step, carry):
        rows = pl.ds(pl.multiple_of(step * size, size), size)
        unit, inverse = normal_parts(frames[rows, :].astype(F32))
        back = normal_back(unit, inverse, incoming[rows, :], small[0:1, :])
        in_grad_out[rows, :] = (middle_grad[rows, :] + back).astype(BF16)
        return carry

    lax.fori_loop(0, incoming.shape[0] // size, step_of, 0)


def in_vmem(count):
    return [pl.BlockSpec(memory_space=pltpu.VMEM)] * count


def in_smem(count):
    return [pl.BlockSpec(memory_space=pltpu.SMEM)] * count


def shape(dims, kind):
    return jax.ShapeDtypeStruct(dims, kind)


def swap(array, axis):
    return lax.ppermute(array, axis, [(0, 1), (1, 0)])


def shifted(array, axis, distance):
    count = lax.axis_size(axis)
    return lax.ppermute(array, axis, [(i, (i + distance) % count) for i in range(count)])


def added(*parts):
    return functools.reduce(jnp.add, [part.astype(F32) for part in parts])


def together(*arrays):
    return lax.optimization_barrier(arrays)


def cost(micros):
    return pl.CostEstimate(
        flops=int(micros * 1.1e9), bytes_accessed=int(micros * 3.6e6), transcendentals=0
    )


def far_away(array):
    return pltpu.with_memory_space_constraint(array, pltpu.HBM)


def call(kernel, name, outs, micros, limit, scratch=(), smem=0, fetched=()):
    def run(*arrays):
        arrays = list(arrays[:smem]) + [
            far_away(array) if index in fetched else kept(array)
            for index, array in enumerate(arrays[smem:])
        ]
        return pl.pallas_call(
            kernel,
            out_shape=tuple(outs),
            in_specs=in_smem(smem) + in_vmem(len(arrays) - smem),
            out_specs=tuple(in_vmem(len(outs))),
            scratch_shapes=list(scratch),
            compiler_params=pltpu.CompilerParams(vmem_limit_bytes=limit * 1024 * 1024),
            cost_estimate=cost(micros),
            name=name,
        )(*arrays)

    return run


def kept(array):
    return pltpu.with_memory_space_constraint(array, pltpu.VMEM)


def in_place(dims, kind):
    return pltpu.VMEM(dims, kind)


def feed(place, slabs, first_matrix, second_matrix, bias, second, grad_rows, second_t, grad_t, *sums):
    ways, _, units = first_matrix.shape
    rows, width = second.shape
    block = min(FF_BLOCK, units)
    grads = in_place((ways, 2, slabs, width // slabs // 2, units), BF16)
    return call(
        functools.partial(feed_kernel, not sums),
        "feed",
        (
            grads,
            grads,
            in_place((ways, 1, units), F32),
            in_place((rows, width), F32),
            in_place((rows, width), F32),
        ),
        14,
        8,
        (
            pltpu.VMEM((width, block), BF16),
            pltpu.VMEM((width, block), BF16),
            pltpu.VMEM((rows, block), BF16),
            pltpu.VMEM((rows, block), BF16),
        ),
        smem=1,
    )(place, first_matrix, second_matrix, bias, second, grad_rows, second_t, grad_t, *sums)


def update_feed(place, core_away, y_away, column, states, done=()):
    depth, height, units = column.shape
    anywhere = pl.BlockSpec(memory_space=pl.ANY)
    return pl.pallas_call(
        functools.partial(update_kernel, core_away, y_away),
        out_shape=tuple(shape(state.shape, F32) for state in states),
        in_specs=in_smem(1) + in_vmem(1) + [anywhere] * (4 + len(done)),
        out_specs=(anywhere,) * 4,
        input_output_aliases={6 + j: j for j in range(len(done))},
        scratch_shapes=[
            pltpu.VMEM((depth, 4, height, units), F32),
            pltpu.VMEM((depth, 4, height, units), F32),
            pltpu.SemaphoreType.DMA((depth, 4)),
            pltpu.SemaphoreType.DMA((depth, 4)),
        ],
        compiler_params=pltpu.CompilerParams(vmem_limit_bytes=12 * 1024 * 1024),
        cost_estimate=cost(0.3),
        name="update_feed",
    )(place, kept(column), *[far_away(state) for state in states], *done)


def shards(
    frames,
    cotangent,
    lengths,
    owners,
    attn_master,
    attn_first,
    attn_second,
    attn_average,
    small_master,
    small_first,
    small_second,
    small_average,
    mlp_master,
    mlp_first,
    mlp_second,
    mlp_average,
    bias_master,
    bias_first,
    bias_second,
    bias_average,
):
    local, width = frames.shape
    wide = local + 2 * KEY_RIM
    rows = local + 2 * ROW_RIM
    blocks = rows // QUERY_BLOCK
    assert blocks * QUERY_BLOCK == rows and local % CHUNK == 0
    units = mlp_master.shape[2]
    ways = lax.axis_size("mlp")
    depth = lax.axis_size("z")
    devices = lax.axis_size(GROUPS)
    share = CAP * TILE // ways
    way = lax.axis_index("mlp")
    place = jnp.stack([lax.axis_index(name) for name in GROUPS + (GROUPS,)]).astype(jnp.int32)

    last = local // KEY_RIM - 1
    last_cot = local // ROW_RIM - 1
    rim = KEY_RIM + ROW_RIM
    first_tile, second_tile, to_next, to_past = pl.pallas_call(
        edges_kernel,
        grid=(1,),
        out_shape=(
            in_place((TILE, width), BF16),
            in_place((TILE, width), BF16),
            in_place((rim, width), BF16),
            in_place((rim, width), BF16),
        ),
        in_specs=[
            pl.BlockSpec((CAP, TILE, width), lambda i: (0, 0, 0)),
            pl.BlockSpec((KEY_RIM, width), lambda i: (0, 0)),
            pl.BlockSpec((KEY_RIM, width), lambda i: (last, 0)),
            pl.BlockSpec((ROW_RIM, width), lambda i: (0, 0)),
            pl.BlockSpec((ROW_RIM, width), lambda i: (last_cot, 0)),
        ],
        out_specs=tuple(in_vmem(4)),
        compiler_params=pltpu.CompilerParams(vmem_limit_bytes=8 * 1024 * 1024),
        cost_estimate=cost(1),
        name="edges",
    )(*[far_away(array) for array in (attn_master, frames, frames, cotangent, cotangent)])
    second_tile_y = swap(second_tile, "y")
    pair_b = stacked(second_tile, second_tile_y)[None]
    bits = [1 << k for k in range(depth.bit_length() - 1)][::-1]
    column_a, column_b = (first_tile[None], pair_b)

    up = [(i, i + 1) for i in range(devices - 1)]
    down = [(i + 1, i) for i in range(devices - 1)]
    before = lax.ppermute(to_next, GROUPS, up)
    after = lax.ppermute(to_past, GROUPS, down)

    edges = (before, after)
    for bit in bits[:-1]:
        got_a, got_b = (flipped(column_a, "z", bit), flipped(column_b, "z", bit))
        column_a = joined(column_a, got_a)
        column_a, column_b, edges, place_late = together(column_a, column_b, edges, place)
        column_b = joined(column_b, got_b)
    before, after = edges

    bias_row = bias_master.reshape(1, units)
    cut_rows = width // 2
    half = pl.pallas_call(
        half_kernel,
        grid_spec=pltpu.PrefetchScalarGridSpec(
            num_scalar_prefetch=1,
            grid=(2,),
            in_specs=[
                pl.BlockSpec((1, cut_rows, units), lambda i, place: (place[2], i, 0)),
                pl.BlockSpec((1, units), lambda i, place: (0, 0)),
            ],
            out_specs=pl.BlockSpec(memory_space=pltpu.VMEM),
        ),
        out_shape=in_place((width + 16, units), BF16),
        compiler_params=pltpu.CompilerParams(vmem_limit_bytes=8 * 1024 * 1024),
        cost_estimate=cost(1),
        name="half",
    )(place_late, far_away(mlp_master), bias_row)
    half_got = [shifted(half, "mlp", d) for d in range(1, ways)]
    column_a = joined(column_a, flipped(column_a, "z", 1))
    column_a, mlp_late = together(column_a, mlp_master)
    column_a_y = swap(column_a, "y")
    low_mlp = pl.pallas_call(
        matrices_kernel,
        grid=(2,),
        out_shape=in_place((2, width, units), BF16),
        in_specs=[pl.BlockSpec((2, cut_rows, units), lambda i: (0, i, 0))],
        out_specs=pl.BlockSpec(memory_space=pltpu.VMEM),
        compiler_params=pltpu.CompilerParams(vmem_limit_bytes=12 * 1024 * 1024),
        cost_estimate=cost(0.5),
        name="matrices",
    )(far_away(mlp_late))

    height = -(-max(-(-wide // 128), blocks) // 8) * 8
    cols, codes = pl.pallas_call(
        tables_kernel,
        out_shape=(in_place((wide, 8), F32), in_place((height, 128), F32)),
        in_specs=in_smem(2),
        out_specs=tuple(in_vmem(2)),
        cost_estimate=cost(1),
        name="tables",
    )(place, lengths)

    column_b_z = flipped(column_b, "z", 1)
    conv, first, wide_rows, cot, grad_rows, grad_t = call(
        conv_kernel,
        "norm_conv",
        (
            in_place((3, wide, width), BF16),
            in_place((wide, width), BF16),
            in_place((rows, width), BF16),
            in_place((rows, width), BF16),
            in_place((rows, width), BF16),
            in_place((width, local), BF16),
        ),
        0.5,
        6,
        (pltpu.VMEM((wide + 16, width), F32),),
        fetched=(1, 3),
    )(before, frames, after, cotangent, cols, small_master)

    column_b_z, column_a_y, conv, half_got, low_mlp = together(
        column_b_z, column_a_y, conv, half_got, low_mlp
    )
    away = [swap(column, "core") for column in (column_a, column_a_y, column_b, column_b_z)]
    tiles = [column_a, column_a_y] + away[:2] + [column_b, column_b_z] + away[2:]

    halves = half_got[0][None] if ways == 2 else stacked(*half_got)
    halves, tiles = together(halves, tiles)
    others = swap(halves, "core")
    weights, query, keys, values, probs, mixed = call(
        attend_kernel,
        "attend",
        (
            in_place((4 * width, width), BF16),
            in_place((wide, width), BF16),
            in_place((wide, width), BF16),
            in_place((wide, width), BF16),
            in_place((blocks, HEADS * QUERY_BLOCK, KEY_SPAN), F32),
            in_place((rows, width), BF16),
        ),
        0.5,
        8,
        smem=2,
    )(place, owners, *tiles, conv, cols, codes, small_master)
    others, mixed = together(others, mixed)
    middle, second, second_t = call(
        middle_kernel,
        "middle",
        (
            in_place((rows, width), F32),
            in_place((rows, width), BF16),
            in_place((width, local), BF16),
        ),
        20,
        8,
    )(mixed, weights, wide_rows, cols, small_master)

    rest = (second, grad_rows, second_t, grad_t)
    far_keep, far_send, far_bias, *sums = feed(
        place, 2 * depth, halves, others, bias_row, *rest
    )
    far_got = swap(far_send, "core")
    near_keep, near_send, near_bias, *sums = feed(
        place, 2 * depth, low_mlp[0][None], low_mlp[1][None], bias_row, *rest, *sums
    )
    near_got = swap(near_send, "core")
    pieces = range(1, ways)
    height = width // (4 * depth)

    def halves_of(array):
        return array.reshape(-1, height, units)

    def row(piece, half, y_away=0):
        return ((piece * 2 + half) * 2 + y_away) * depth

    far = add_into(
        "far_sum",
        (halves_of(far_keep), halves_of(far_got)),
        [(2 * depth, [(i, row(d - 1, 0)) for i in range(2)]) for d in pieces]
        + [(depth, [(i, row(d - 1, 1)) for i in range(2)]) for d in pieces]
        + [(depth, [(i, row(d - 1, 1, 1)) for i in range(2)]) for d in pieces],
        0.1,
    )
    far, sums = together(far, sums)
    far_x = [shifted(far[d - 1], "mlp", -d) for d in pieces]
    far_y = [swap(far[2 * (ways - 1) + d - 1], "y") for d in pieces]

    output, middle_grad, mixed_grad, out_grad, feed_rows = call(
        middle_back_kernel,
        "middle_back",
        (
            shape((local, width), BF16),
            in_place((local, width), F32),
            in_place((rows, width), BF16),
            in_place((width, width), BF16),
            in_place((32, width), F32),
        ),
        0.5,
        8,
        (pltpu.VMEM((rows, width), BF16),),
    )(middle, cot, grad_rows, *sums, mixed, weights, cols, small_master)

    near_keep, mixed_grad, far_y = together(near_keep, mixed_grad, far_y)
    near = add_into(
        "near_sum",
        (halves_of(near_keep), halves_of(near_got)),
        [(2 * depth, [(i, row(0, 0)) for i in range(2)])]
        + [(depth, [(i, row(0, 1, j)) for i in range(2)]) for j in range(2)],
        0.1,
    )
    near, mixed_grad = together(near, mixed_grad)
    near_y = swap(near[2], "y")

    columns = width // 2
    slabs = in_place((2 * ways * depth, share, columns), BF16)

    def scores_back(first_head, mixed_grad):
        return call(
            functools.partial(scores_back_kernel, first_head),
            "scores_back",
            (
                in_place((rows, columns), BF16),
                in_place((rows, columns), BF16),
                in_place((rows, columns), BF16),
                slabs,
                slabs,
            ),
            8,
            10,
            (
                pltpu.VMEM((wide, columns), F32),
                pltpu.VMEM((wide, columns), F32),
                pltpu.VMEM((4 * width, columns), BF16),
            ),
            smem=2,
        )(place, owners, query, keys, values, probs, mixed_grad, conv, out_grad)

    *grads_0, keep_0, send_0 = scores_back(0, mixed_grad)
    got_0 = swap(send_0, "core")

    arrays = (near[0], *far_x, near[1], near_y, *far[ways - 1 : 2 * (ways - 1)], *far_y)
    first_parts = list(range(ways))
    feed_two = add_into(
        "feed_two",
        arrays,
        [(depth, [(i, j * depth) for i in first_parts]) for j in range(2)]
        + [(depth, [(ways, 0), (ways + 1, 0)])]
        + [(depth, [(ways + 1 + d, 0), (2 * ways + d, 0)]) for d in pieces],
        0.1,
    )
    feed_two, mixed_grad, grads_0 = together(feed_two, mixed_grad, grads_0)
    feed_y = swap(feed_two[1], "y")
    feed_x = [shifted(feed_two[2 + d], "mlp", -d) for d in pieces]

    *grads_1, keep_1, send_1 = scores_back(HEADS // 2, mixed_grad)
    got_1 = swap(send_1, "core")
    paired_0 = add_into(
        "paired",
        (keep_0, got_0),
        [(2 * depth, [(i, 2 * depth * d) for i in range(2)]) for d in range(ways)],
        20,
    )
    feed_line = call(
        feed_line_kernel,
        "feed_line",
        tuple(in_place((2 * height, units), BF16) for _ in range(depth)),
        0.1,
        8,
    )(feed_two[0], feed_y, feed_two[2], *feed_x)
    paired_0, feed_line, keep_1, grads_1 = together(paired_0, feed_line, keep_1, grads_1)
    first_got = [shifted(paired_0[d], "mlp", -d) for d in range(1, ways)]
    feed_got = [shifted(feed_line[d], "z", d) for d in range(1, depth)]

    paired_1 = add_into(
        "paired",
        (keep_1, got_1),
        [(ways * depth, [(i, depth * j, 2 * depth) for i in range(2)]) for j in range(2)],
        0.1,
    )
    paired_1, grads_1 = together(paired_1, grads_1)
    second_got = swap(paired_1[1], "y")

    conv_grad = call(
        conv_grad_kernel, "conv_grad", (in_place((3, rows, width), F32),), 20, 8
    )(*grads_0, *grads_1, weights)[0]
    incoming, totals = call(
        conv_back_kernel,
        "conv_back",
        (in_place((local, width), F32), in_place((NSMALL_ROWS, width), F32)),
        12,
        8,
        (pltpu.VMEM((192, width), F32),),
        smem=1,
    )(
        place, grads_0[0], grads_0[2], grads_1[0], grads_1[2], conv_grad, first, frames, feed_rows,
         near_bias, far_bias, cols, small_master,
    )

    totals_got = swap(totals, "core")
    feed_keep, totals = together(feed_line[0], totals)
    feed_own = add_into(
        "feed_own",
        [part[None] for part in (feed_keep, *feed_got)],
        [(1, [(d, 0) for d in range(depth)])],
    )[0]
    feed_own, first_keep = together(feed_own, paired_0[0])
    feed_all = [shifted(feed_own[0], "z", d) for d in range(1, depth)]
    lined, line, *second = call(
        functools.partial(line_kernel, ways),
        "line",
        (
            in_place((depth, share, columns), BF16),
            in_place((depth * share + 2 * NSMALL_ROWS, columns), BF16),
        )
        + (in_place((depth, share, columns), BF16),) * ways,
        0.1,
        8,
    )(first_keep, *first_got, paired_1[0], second_got, totals, totals_got)
    lined, line, second, incoming = together(lined, line, second, incoming)
    line_got = swap(line, "y")
    second_x = [shifted(second[d], "mlp", -d) for d in range(1, ways)]
    in_grad = call(
        in_grad_kernel, "in_grad", (shape((local, width), BF16),), 20, 8, fetched=(1,)
    )(incoming, frames, middle_grad, small_master)[0]
    lined, in_grad = together(lined, in_grad)

    def slabs(count, extra):
        if extra:
            return in_place((count * share + NSMALL_ROWS, width), BF16)
        return in_place((count, share, width), BF16)

    count = depth // 2
    z_keep, z_sent = call(flat_kernel, "flat", (slabs(count, 0), slabs(count, 1)), 0.1, 8)(
        lined, line, line_got, second[0], *second_x
    )
    feed_own, z_keep, z_sent = together(feed_own, z_keep, z_sent)
    z_got = flipped(z_sent, "z", 1)
    feed_sums = [stacked(feed_own[0], *feed_all)]
    feed_sums.append(swap(feed_sums[0], "y"))
    feed_sums.append(swap(feed_sums[0], "core"))
    states = (mlp_master, mlp_first, mlp_second, mlp_average)
    mlp_new = update_feed(place, 0, 0, feed_sums[0], states)
    mlp_new, z_keep = together(mlp_new, z_keep)
    for bit in bits[::-1][1:]:
        count //= 2
        z_keep, z_sent = call(halve_kernel, "halve", (slabs(count, 0), slabs(count, 1)), 0.1, 8)(
            z_keep, z_sent, z_got
        )
        mlp_new, z_keep, z_sent = together(mlp_new, z_keep, z_sent)
        z_got = flipped(z_sent, "z", bit)
    mlp_new = update_feed(place, 1, 0, feed_sums[2], states, mlp_new)
    mlp_new, z_keep = together(mlp_new, z_keep)
    mine = call(mine_kernel, "mine", (in_place((share + NSMALL_ROWS, width), BF16),), 0.1, 8)(
        z_keep, z_sent, z_got
    )[0]
    mine, own_y, mlp_new = together(mine, feed_sums[1], mlp_new)
    shares = [mine] + [shifted(mine, "mlp", d) for d in range(1, ways)]
    other_y = swap(own_y, "core")
    mlp_new = update_feed(place, 0, 1, own_y, states, mlp_new)
    mlp_new, other_y, shares[0] = together(mlp_new, other_y, shares[0])
    mlp_new = update_feed(place, 1, 1, other_y, states, mlp_new)
    attn_shape = shape(attn_master.shape, F32)
    small_shape = shape(small_master.shape, F32)
    rest_new = call(
        update_rest_kernel,
        "update_rest",
        (attn_shape,) * 4 + (small_shape,) * 4 + (shape((1, units), F32),) * 4,
        3,
        12,
        (pltpu.VMEM((ways, share, width), BF16), pltpu.VMEM((8, width), F32)),
        smem=2,
    )(
        place, owners, *shares, attn_master, attn_first, attn_second, attn_average,
        small_master, small_first, small_second, small_average,
        *[state.reshape(1, units) for state in (bias_master, bias_first, bias_second, bias_average)],
    )

    bias_new = [part.reshape(units) for part in rest_new[8:]]
    return (
        output,
        in_grad,
        *rest_new[:8],
        *mlp_new,
        *bias_new,
    )


def solution(mesh):
    seq, mlp = mesh.devices.shape
    grid = Mesh(mesh.devices.reshape(seq // 4, 2, 2, mlp), GROUPS)
    rows = P(GROUPS, None)
    tiles = P(SEATS, None, None)
    units = P(None, None, "mlp")
    bias = P("mlp")
    in_specs = (
        (rows, rows, P(), P()) + (tiles,) * 4 + (P(),) * 4 + (units,) * 4 + (bias,) * 4
    )
    out_specs = (rows, rows) + (tiles,) * 4 + (P(),) * 4 + (units,) * 4 + (bias,) * 4
    return jax.shard_map(shards, mesh=grid, in_specs=in_specs, out_specs=out_specs, check_vma=False)
```

```python
import functools

import jax
import jax.numpy as jnp
from jax import lax
from jax.experimental import pallas as pl
from jax.experimental.pallas import tpu as pltpu
from jax.sharding import Mesh
from jax.sharding import PartitionSpec as P

HEADS = 4
HEAD = 128
HALF = 9
TILE = 128
TILES = 16
CAP = 2
STEP = 7
NSMALL = 17
NSMALL_ROWS = 32

NORM_EPS = 1e-05
MASKED = -1e30
BETA_ONE = 0.9
BETA_TWO = 0.999
ADAM_EPS = 1e-08
MATRIX_RATE = 0.03
MATRIX_DECAY = 0.05
SMALL_RATE = 0.3
AVERAGE_RATE = 0.8

F32 = jnp.float32
BF16 = jnp.bfloat16

KEY_RIM = 32
ROW_RIM = 16
QUERY_BLOCK = 96
KEY_SPAN = 128
FF_BLOCK = 512
FF_ROWS = 3
CHUNK = 128
NARROW = 64
SCALE = HEAD ** (-0.5)
GROUPS = ("z", "y", "core", "mlp")
SEATS = ("z", "y", "core")


def adamw(weight, grad, first, second, average, rate, decay):
    first_new = BETA_ONE * first + (1.0 - BETA_ONE) * grad
    second_new = BETA_TWO * second + (1.0 - BETA_TWO) * grad * grad
    scaled = second_new * (1.0 / (1.0 - BETA_TWO**STEP))
    root = scaled * lax.rsqrt(scaled)
    ratio = first_new * (1.0 / (1.0 - BETA_ONE**STEP)) / (root + ADAM_EPS)
    weight_new = weight - rate * (ratio + decay * weight)
    average_new = AVERAGE_RATE * average + (1.0 - AVERAGE_RATE) * weight_new
    return (weight_new, first_new, second_new, average_new)


def dot_nn(left, right):
    return lax.dot_general(left, right, (((1,), (0,)), ((), ())), preferred_element_type=F32)


def dot_nt(left, right):
    return lax.dot_general(left, right, (((1,), (1,)), ((), ())), preferred_element_type=F32)


def dot_tn(left, right):
    return lax.dot_general(left, right, (((0,), (0,)), ((), ())), preferred_element_type=F32)


def normal_parts(values):
    mean = jnp.mean(values, axis=-1, keepdims=True)
    centred = values - mean
    spread = jnp.mean(centred * centred, axis=-1, keepdims=True)
    inverse = lax.rsqrt(spread + NORM_EPS)
    return (centred * inverse, inverse)


def normal_back(unit, inverse, grad, gain):
    inner = grad * gain
    return inverse * (
        inner
        - jnp.mean(inner, axis=-1, keepdims=True)
        - unit * jnp.mean(inner * unit, axis=-1, keepdims=True)
    )


def fold_rows(values):
    return jnp.sum(values.reshape(-1, 8, values.shape[-1]), axis=0)


def conv_kernel(
    before, frames, after, cotangent, cols, small,
    conv_out, first_out, wide_out, cot_out, grad_rows_out, grad_t_out, rows,
):
    local = frames.shape[0]
    wide = local + 2 * KEY_RIM
    gain = small[0:1, :]
    bias = small[1:2, :]

    def norm_to(piece, start):
        unit, _ = normal_parts(piece.astype(F32))
        low = (unit * gain + bias).astype(BF16)
        first_out[pl.ds(start, piece.shape[0]), :] = low
        rows[pl.ds(start + 8, piece.shape[0]), :] = low.astype(F32)

    zero = jnp.zeros((8, rows.shape[1]), F32)
    rows[0:8, :] = zero
    rows[wide + 8 : wide + 16, :] = zero
    norm_to(before[0:KEY_RIM, :], 0)
    norm_to(after[0:KEY_RIM, :], KEY_RIM + local)

    def norm_step(step, carry):
        start = pl.multiple_of(step * CHUNK, CHUNK)
        norm_to(frames[pl.ds(start, CHUNK), :], pl.multiple_of(start + KEY_RIM, 32))
        return carry

    lax.fori_loop(0, local // CHUNK, norm_step, 0, unroll=2)
    wide_out[0:ROW_RIM, :] = before[KEY_RIM - ROW_RIM : KEY_RIM, :]
    wide_out[ROW_RIM : ROW_RIM + local, :] = frames[...]
    wide_out[ROW_RIM + local :, :] = after[0:ROW_RIM, :]
    cot_out[0:ROW_RIM, :] = before[KEY_RIM:, :]
    cot_out[ROW_RIM : ROW_RIM + local, :] = cotangent[...]
    cot_out[ROW_RIM + local :, :] = after[KEY_RIM:, :]

    def mask_step(step, carry):
        span = pl.ds(pl.multiple_of(step * QUERY_BLOCK, 32), QUERY_BLOCK)
        flags = cols[pl.ds(pl.multiple_of(step * QUERY_BLOCK + ROW_RIM, 16), QUERY_BLOCK), 2:3]
        grad_rows_out[span, :] = (cot_out[span, :].astype(F32) * flags).astype(BF16)
        return carry

    lax.fori_loop(0, cot_out.shape[0] // QUERY_BLOCK, mask_step, 0)
    grad_t_out[...] = grad_rows_out[ROW_RIM : ROW_RIM + local, :].T

    def conv_step(step, carry):
        start = pl.multiple_of(step * NARROW, NARROW)
        window = rows[pl.ds(start, NARROW + 16), :]
        flags = cols[pl.ds(start, NARROW), :]
        past = pltpu.roll(window, 1, 0)[8 : 8 + NARROW] * flags[:, 0:1]
        here = window[8 : 8 + NARROW]
        later = pltpu.roll(window, NARROW + 15, 0)[8 : 8 + NARROW] * flags[:, 1:2]
        for c in range(3):
            row = 8 + 3 * c
            mixed = (
                small[row : row + 1, :] * past
                + small[row + 1 : row + 2, :] * here
                + small[row + 2 : row + 3, :] * later
            )
            conv_out[c, pl.ds(start, NARROW), :] = mixed.astype(BF16)
        return carry

    lax.fori_loop(0, wide // NARROW, conv_step, 0)


def edges_kernel(tiles, head, tail, cot_head, cot_tail, first_out, second_out, up_out, down_out):
    first_out[...] = tiles[0].astype(BF16)
    second_out[...] = tiles[1].astype(BF16)
    up_out[0:KEY_RIM, :] = tail[...]
    up_out[KEY_RIM:, :] = cot_tail[...]
    down_out[0:KEY_RIM, :] = head[...]
    down_out[KEY_RIM:, :] = cot_head[...]


def matrices_kernel(master, low_out):
    size = master.shape[1]
    rows = pl.ds(pl.multiple_of(pl.program_id(0) * size, size), size)
    low_out[:, rows, :] = master[...].astype(BF16)


def half_kernel(place, master, bias, half_out):
    step = pl.program_id(0)
    size, units = master.shape[1:]
    half_out[pl.ds(pl.multiple_of(step * size, size), size), :] = master[0].astype(BF16)

    @pl.when(step == 0)
    def _():
        width = half_out.shape[0] - 16
        half_out[width:, :] = jnp.broadcast_to(bias[...], (16, units)).astype(BF16)


def tables_kernel(place, lengths, cols_out, codes_out):
    wide = cols_out.shape[0]
    blocks = (wide - KEY_SPAN) // QUERY_BLOCK + 1
    local = wide - 2 * KEY_RIM
    anchor = place[4] * local
    chunks = -(-wide // 128)
    height = -(-max(chunks, blocks) // 8) * 8
    row = lax.broadcasted_iota(jnp.int32, (height, 128), 0)
    lane = lax.broadcasted_iota(jnp.int32, (height, 128), 1)
    start = anchor - KEY_RIM + lane
    frame = start + row * 128
    key = start + row * QUERY_BLOCK
    zero = jnp.zeros((height, 128), jnp.int32)

    def count(j, carry):
        end, video, key_video, starts, stops = carry
        end = end + lengths[j]
        return (
            end,
            video + (frame >= end).astype(jnp.int32),
            key_video + (key >= end).astype(jnp.int32),
            starts + (frame == end).astype(jnp.int32),
            stops + (frame + 1 == end).astype(jnp.int32),
        )

    last, video, key_video, starts, stops = lax.fori_loop(
        0, lengths.shape[0], count, (jnp.int32(0), zero, zero, zero, zero)
    )
    valid = (frame >= 0) & (frame < last)
    key_valid = (key >= 0) & (key < last)
    prev = valid & (frame >= 1) & (starts == 0)
    after = valid & (frame + 1 < last) & (stops == 0)
    codes_out[...] = jnp.where(key_valid, key_video, -2).astype(F32)
    values = [prev.astype(F32), after.astype(F32), valid.astype(F32)]
    values.append(jnp.where(valid, video, -1).astype(F32))
    for c in range(chunks):
        size = min(128, wide - c * 128)
        columns = jnp.concatenate([value[c : c + 1] for value in values] * 2, axis=0).T
        cols_out[c * 128 : c * 128 + size, :] = columns[0:size]


def slot_of(owners, i):
    owner = owners[i]
    return owner, sum(jnp.where((owners[j] == owner) & (j < i), 1, 0) for j in range(TILES))


def slots_of(owners):
    found = [owners[i] for i in range(TILES)]
    return [
        (found[i], sum([jnp.where(found[j] == found[i], 1, 0) for j in range(i)], jnp.int32(0)))
        for i in range(TILES)
    ]


def head_lanes(h):
    return slice(h * HEAD, (h + 1) * HEAD)


def head_rows(h):
    return slice(h * QUERY_BLOCK, (h + 1) * QUERY_BLOCK)


def attend_kernel(
    place, owners, *refs
):
    tiles, refs = (refs[:8], refs[8:])
    conv, cols, codes, small, *refs = refs
    weights_out, query_out, key_out, value_out, probs_out, mixed_out = refs
    rows, width = mixed_out.shape
    wide = conv.shape[1]
    depth = tiles[0].shape[0]
    def tile_step(i, carry):
        owner, slot = slot_of(owners, i)
        spot = pl.ds(pl.multiple_of(i * TILE, TILE), TILE)
        core_away = (owner + place[2]) % 2
        y_away = (owner // 2 + place[1]) % 2
        z_away = place_of(place[0] ^ (owner // 4), depth)
        late = z_away // (depth // 2)
        for r, source in enumerate(tiles[:4]):

            @pl.when((slot == 0) & (core_away * 2 + y_away == r))
            def _(source=source):
                weights_out[spot, :] = source[z_away]

        for r, source in enumerate(tiles[4:]):

            @pl.when((slot == 1) & (core_away * 2 + late == r))
            def _(source=source):
                weights_out[spot, :] = source[z_away % (depth // 2), y_away]

        return carry

    lax.fori_loop(0, TILES, tile_step, 0, unroll=4)

    def matrix(c):
        return weights_out[c * width : (c + 1) * width, :]

    part = wide // 2
    for j in range(2):
        span = pl.ds(j * part, part)
        query_out[span, :] = (dot_nn(conv[0, span, :], matrix(0)) + small[4:5, :]).astype(BF16)
        key_out[span, :] = dot_nn(conv[1, span, :], matrix(1)).astype(BF16)
        value_out[span, :] = (dot_nn(conv[2, span, :], matrix(2)) + small[5:6, :]).astype(BF16)

    query_index = lax.broadcasted_iota(jnp.int32, (QUERY_BLOCK, KEY_SPAN), 0)
    key_index = lax.broadcasted_iota(jnp.int32, (QUERY_BLOCK, KEY_SPAN), 1)
    offset = query_index - key_index + (KEY_RIM - ROW_RIM)
    band = jnp.abs(offset) <= HALF
    same = offset == 0

    for step in range(rows // QUERY_BLOCK):
        start = step * QUERY_BLOCK
        query_start = start + ROW_RIM
        query_code = cols[pl.ds(query_start, QUERY_BLOCK), 3:4]
        key_code = codes[step : step + 1, :]
        allowed = band & (same | (query_code == key_code))
        scores = [
            jnp.where(
                allowed,
                dot_nt(
                    query_out[pl.ds(query_start, QUERY_BLOCK), head_lanes(h)],
                    key_out[pl.ds(start, KEY_SPAN), head_lanes(h)],
                )
                * SCALE,
                MASKED,
            )
            for h in range(HEADS)
        ]
        masked = jnp.concatenate(scores, axis=0)
        top = jnp.max(masked, axis=-1, keepdims=True)
        expo = jnp.exp(masked - top)
        probs = expo / jnp.sum(expo, axis=-1, keepdims=True)
        probs_out[step] = probs
        low = probs.astype(BF16)
        for h in range(HEADS):
            values = value_out[pl.ds(start, KEY_SPAN), head_lanes(h)]
            mixed = dot_nn(low[head_rows(h)], values)
            mixed_out[pl.ds(start, QUERY_BLOCK), head_lanes(h)] = mixed.astype(BF16)


def middle_kernel(mixed, weights, wide_rows, cols, small, middle_out, second_out, second_t_out):
    rows, width = wide_rows.shape
    part = rows // 3
    for j in range(3):
        span = pl.ds(j * part, part)
        branch = dot_nn(mixed[span, :], weights[3 * width : 4 * width, :]) + small[6:7, :]
        valid = cols[pl.ds(ROW_RIM + j * part, part), 2:3]
        middle = wide_rows[span, :].astype(F32) + valid * branch
        middle_out[span, :] = middle
        unit, _ = normal_parts(middle)
        second_out[span, :] = (unit * small[2:3, :] + small[3:4, :]).astype(BF16)
    second_t_out[...] = second_out[ROW_RIM : rows - ROW_RIM, :].T


def feed_kernel(first_call, *refs):
    place, first_matrix, second_matrix, hidden_bias, second, grad_rows, second_t, grad_t, *refs = refs
    if not first_call:
        result_in, second_grad_in, *refs = refs
    keep_out, send_out, bias_out, result, second_grad, up, down, active, hidden_grad = refs
    ways, _, units = first_matrix.shape
    width, block = up.shape
    per_piece = units // block
    rows = second.shape[0]
    local = rows - 2 * ROW_RIM
    own = slice(ROW_RIM, ROW_RIM + local)
    even = place[2] == 0
    straight = even if first_call else place[2] >= 0
    slabs, height = keep_out.shape[2:4]
    depth = slabs // 2
    if first_call:
        result[...] = jnp.zeros(result.shape, F32)
        second_grad[...] = jnp.zeros(second_grad.shape, F32)
    else:
        result[...] = result_in[...]
        second_grad[...] = second_grad_in[...]

    def block_step(step, carry):
        piece = step // per_piece
        lanes = pl.ds(pl.multiple_of((step % per_piece) * block, block), block)

        @pl.when(straight)
        def _():
            up[...] = first_matrix[piece, 0:width, lanes]
            down[...] = second_matrix[piece, 0:width, lanes]

        @pl.when(jnp.logical_not(straight))
        def _():
            up[...] = second_matrix[piece, 0:width, lanes]
            down[...] = first_matrix[piece, 0:width, lanes]

        if first_call:
            bias = first_matrix[piece, width : width + 16, lanes][0:1].astype(F32)
        else:
            bias = hidden_bias[0:1, lanes].astype(BF16).astype(F32)
        part = rows // FF_ROWS
        for j in range(FF_ROWS):
            span = pl.ds(j * part, part)
            value = dot_nn(second[span, :], up[...]) + bias
            active_grad = dot_nn(grad_rows[span, :], down[...])
            phi = 0.5 * (1.0 + lax.erf(value * (0.5**0.5)))
            density = jnp.exp(value * value * -0.5) * 0.3989422804014327
            active[span, :] = (value * phi).astype(BF16)
            hidden_grad[span, :] = (active_grad * (phi + value * density)).astype(BF16)
        result[...] += dot_nt(active[...], down[...])
        second_grad[...] += dot_nt(hidden_grad[...], up[...])
        up_grad = dot_nn(second_t[...], hidden_grad[own, :])
        down_grad = dot_nn(grad_t[...], active[own, :])
        bias_out[piece, :, lanes] = jnp.sum(
            hidden_grad[own, :].astype(F32), axis=0, keepdims=True
        )
        kept = jnp.where(even, up_grad, down_grad).astype(BF16)
        sent = jnp.where(even, down_grad, up_grad).astype(BF16)
        for slab in range(slabs):
            target = (slab // depth + place[1]) % 2 * depth + (slab % depth - place[0] + depth) % depth
            for half in range(2):
                start = (2 * slab + half) * height
                keep_out[piece, half, target, :, lanes] = kept[start : start + height]
                send_out[piece, half, target, :, lanes] = sent[start : start + height]
        return carry

    lax.fori_loop(0, ways * per_piece, block_step, 0)


def update_kernel(core_away, y_away, place, column, *refs):
    states, outs = refs[:4], refs[-8:-4]
    came, left, came_sems, left_sems = refs[-4:]
    depth, height, _ = column.shape
    matrix = (place[2] + core_away) % 2
    first_row = (place[1] + y_away) % 2 * (depth * height)

    def rows(j):
        return pl.ds(pl.multiple_of(first_row + j * height, height), height)

    def fetch(j, k):
        return pltpu.make_async_copy(
            states[k].at[matrix, rows(j)], came.at[j, k], came_sems.at[j, k]
        )

    def store(j, k):
        return pltpu.make_async_copy(
            left.at[j, k], outs[k].at[matrix, rows(j)], left_sems.at[j, k]
        )

    def start(j, carry):
        for k in range(4):
            fetch(j, k).start()
        return carry

    def update(j, carry):
        for k in range(4):
            fetch(j, k).wait()
        grad = column[(place[0] - j + depth) % depth].astype(F32)
        new = adamw(came[j, 0], grad, came[j, 1], came[j, 2], came[j, 3], MATRIX_RATE, MATRIX_DECAY)
        for k, value in enumerate(new):
            left[j, k] = value
            store(j, k).start()
        return carry

    def finish(j, carry):
        for k in range(4):
            store(j, k).wait()
        return carry

    lax.fori_loop(0, depth, start, 0)
    lax.fori_loop(0, depth, update, 0)
    lax.fori_loop(0, depth, finish, 0)


def middle_back_kernel(
    middle, cot, grad_rows, result_sum, second_sum, mixed, weights, cols, small,
    output_out, middle_grad_out, mixed_grad_out, out_grad_out, rows_out, branch,
):
    rows, width = middle.shape
    local = rows - 2 * ROW_RIM
    own = slice(ROW_RIM, ROW_RIM + local)
    rows_out[...] = jnp.zeros(rows_out.shape, F32)

    def finish(start, size, own_rows):
        span = pl.ds(start, size)
        here = middle[span, :]
        valid = cols[pl.ds(start + ROW_RIM, size), 2:3]
        unit, inverse = normal_parts(here)
        incoming = second_sum[span, :]
        back = normal_back(unit, inverse, incoming, small[2:3, :])
        middle_grad = cot[span, :].astype(F32) + back
        branch_grad = (valid * middle_grad).astype(BF16)
        branch[span, :] = branch_grad
        if own_rows:
            target = pl.ds(start - ROW_RIM, size)
            result = result_sum[span, :] + small[7:8, :]
            output_out[target, :] = (here + valid * result).astype(BF16)
            middle_grad_out[target, :] = middle_grad
            rows_out[0:8, :] += fold_rows(incoming * unit)
            rows_out[8:16, :] += fold_rows(incoming)
            rows_out[16:24, :] += fold_rows(branch_grad.astype(F32))
            rows_out[24:32, :] += fold_rows(grad_rows[span, :].astype(F32))

    finish(0, ROW_RIM, False)
    finish(ROW_RIM + local, ROW_RIM, False)

    def finish_step(j, carry):
        finish(pl.multiple_of(j * CHUNK + ROW_RIM, 16), CHUNK, True)
        return carry

    lax.fori_loop(0, local // CHUNK, finish_step, 0)
    mixed_grad_out[...] = dot_nt(branch[...], weights[3 * width : 4 * width, :]).astype(BF16)
    out_grad_out[...] = dot_tn(mixed[own, :], branch[own, :]).astype(BF16)


def scores_back_kernel(
    first_head, place, owners, query, keys, values, probs, mixed_grad, conv, out_grad,
    query_grad, key_grad, value_grad, keep_out, send_out,
    key_acc, value_acc, grads,
):
    rows, width = mixed_grad.shape
    columns = key_acc.shape[1]
    heads = columns // HEAD
    local = rows - 2 * ROW_RIM
    own = slice(ROW_RIM, ROW_RIM + local)
    wide_own = slice(KEY_RIM, KEY_RIM + local)
    key_acc[...] = jnp.zeros(key_acc.shape, F32)
    value_acc[...] = jnp.zeros(value_acc.shape, F32)
    keep_out[...] = jnp.zeros(keep_out.shape, BF16)
    send_out[...] = jnp.zeros(send_out.shape, BF16)

    for step in range(rows // QUERY_BLOCK):
        start = step * QUERY_BLOCK
        here = pl.ds(start, QUERY_BLOCK)
        span = pl.ds(start, KEY_SPAN)
        quest = pl.ds(start + ROW_RIM, QUERY_BLOCK)
        first_row = first_head * QUERY_BLOCK
        probs_here = probs[step, first_row : first_row + heads * QUERY_BLOCK, :]
        prob_grad = jnp.concatenate(
            [
                dot_nt(mixed_grad[here, head_lanes(h)], values[span, head_lanes(h)])
                for h in range(first_head, first_head + heads)
            ],
            axis=0,
        )
        inner = jnp.sum(probs_here * prob_grad, axis=-1, keepdims=True)
        score_grad = (probs_here * (prob_grad - inner)).astype(BF16)
        low = probs_here.astype(BF16)
        for h in range(heads):
            lanes, whole_lanes = head_lanes(h), head_lanes(first_head + h)
            score = score_grad[head_rows(h)]
            query_grad[here, lanes] = (dot_nn(score, keys[span, whole_lanes]) * SCALE).astype(BF16)
            key_acc[span, lanes] += dot_tn(score, query[quest, whole_lanes])
            value_acc[span, lanes] += dot_tn(low[head_rows(h)], mixed_grad[here, whole_lanes])

    inside = slice(ROW_RIM, ROW_RIM + rows)
    key_grad[...] = (key_acc[inside, :] * SCALE).astype(BF16)
    value_grad[...] = value_acc[inside, :].astype(BF16)

    for c, grad in enumerate((query_grad, key_grad, value_grad)):
        grads[c * width : (c + 1) * width, :] = dot_tn(conv[c, wide_own, :], grad[own, :]).astype(BF16)
    grads[3 * width :, :] = out_grad[:, first_head * HEAD : first_head * HEAD + columns]

    share = keep_out.shape[1]
    parts = TILE // share
    ways = CAP * parts
    depth = keep_out.shape[0] // (2 * ways)
    for i, (owner, slot) in enumerate(slots_of(owners)):
        away = (owner + place[2]) % 2
        y_away = (owner // 2 + place[1]) % 2
        z_away = (owner // 4) ^ place[0]
        for part in range(parts):
            way = (place[3] - slot * parts - part + ways) % ways
            target = (way * 2 + y_away) * depth + z_away
            here = pl.ds(i * TILE + part * share, share)

            @pl.when(away == 0)
            def _(target=target, here=here):
                keep_out[target] = grads[here, :]

            @pl.when(away == 1)
            def _(target=target, here=here):
                send_out[target] = grads[here, :]


def conv_grad_kernel(*refs):
    weights, conv_grad = refs[-2:]
    rows, columns = refs[0].shape
    width = weights.shape[1]
    part = rows // 2
    for j in range(2):
        span = pl.ds(j * part, part)
        for c in range(3):
            matrix = slice(c * width, (c + 1) * width)
            conv_grad[c, span, :] = dot_nt(refs[c][span, :], weights[matrix, 0:columns]) + dot_nt(
                refs[3 + c][span, :], weights[matrix, columns:]
            )


def conv_back_kernel(
    place, query_grad_0, value_grad_0, query_grad_1, value_grad_1, conv_grad, first, frames, feed_rows, near_bias, far_bias, cols, small,
    incoming_out, totals_out, sums,
):
    rows, columns = query_grad_0.shape
    width = frames.shape[1]
    local = rows - 2 * ROW_RIM
    sums[...] = jnp.zeros(sums.shape, F32)

    def conv_step(step, carry):
        start = pl.multiple_of(step * CHUNK, CHUNK)
        window = CHUNK + 16
        flags = cols[pl.ds(pl.multiple_of(start + KEY_RIM - 8, 8), window), :]
        span = pl.ds(pl.multiple_of(start + ROW_RIM - 8, 8), window)
        grads = [conv_grad[c, span, :] for c in range(3)]
        past = sum(small[8 + 3 * c : 9 + 3 * c, :] * grads[c] for c in range(3)) * flags[:, 0:1]
        later = sum(small[10 + 3 * c : 11 + 3 * c, :] * grads[c] for c in range(3)) * flags[:, 1:2]
        middle = slice(8, 8 + CHUNK)
        incoming = (
            sum(small[9 + 3 * c : 10 + 3 * c, :] * grads[c][middle] for c in range(3))
            + pltpu.roll(past, window - 1, 0)[middle]
            + pltpu.roll(later, 1, 0)[middle]
        )
        low = first[pl.ds(pl.multiple_of(start + KEY_RIM - 16, 16), window + 16), :].astype(F32)
        inner = slice(16, 16 + CHUNK)
        low_here = low[inner]
        low_past = pltpu.roll(low, 1, 0)[inner] * flags[middle, 0:1]
        low_later = pltpu.roll(low, window + 15, 0)[inner] * flags[middle, 1:2]
        for c in range(3):
            grad = grads[c][middle]
            base = 8 * (8 + 3 * c)
            sums[base : base + 8, :] += fold_rows(grad * low_past)
            sums[base + 8 : base + 16, :] += fold_rows(grad * low_here)
            sums[base + 16 : base + 24, :] += fold_rows(grad * low_later)
        unit, _ = normal_parts(frames[pl.ds(start, CHUNK), :].astype(F32))
        incoming_out[pl.ds(start, CHUNK), :] = incoming
        sums[0:8, :] += fold_rows(incoming * unit)
        sums[8:16, :] += fold_rows(incoming)
        here = pl.ds(pl.multiple_of(start + ROW_RIM, 16), CHUNK)
        for lanes, query_grad, value_grad in (
            (slice(0, columns), query_grad_0, value_grad_0),
            (slice(columns, width), query_grad_1, value_grad_1),
        ):
            sums[32:40, lanes] += fold_rows(query_grad[here, :].astype(F32))
            sums[40:48, lanes] += fold_rows(value_grad[here, :].astype(F32))
        return carry

    lax.fori_loop(0, local // CHUNK, conv_step, 0)
    sums[16:32, :] = feed_rows[0:16, :]
    sums[48:64, :] = feed_rows[16:32, :]
    totals_out[0:24, :] = jnp.sum(sums[...].reshape(24, 8, width), axis=1)
    totals_out[24:, :] = jnp.zeros((totals_out.shape[0] - 24, width), F32)
    units = near_bias.shape[2]
    ways = 1 + far_bias.shape[0]
    chunk = min(units, width)
    for piece in range(ways):
        source = near_bias if piece == 0 else far_bias
        for j in range(units // chunk):
            offset = (place[3] - piece + ways) % ways * units + j * chunk
            lanes = pl.ds(pl.multiple_of(offset % width, chunk), chunk)
            totals_out[pl.ds(24 + offset // width, 1), lanes] = source[
                max(piece - 1, 0), :, j * chunk : (j + 1) * chunk
            ]


def add_kernel(inputs, kinds, *refs):
    for out, parts in zip(refs[-len(kinds) :], inputs):
        count = out.shape[0]

        def step(j, carry, out=out, parts=parts, count=count):
            total = 0.0
            for index, start, *stride in parts:
                run = stride[0] // 2 if stride else count
                total = total + refs[index][start + j // run * 2 * run + j % run].astype(F32)
            out[j] = total.astype(out.dtype)
            return carry

        lax.fori_loop(0, count, step, 0)


def add_into(name, arrays, outputs, micros=0.1):
    outs = [in_place((count,) + arrays[0].shape[1:], BF16) for count, _ in outputs]
    kernel = functools.partial(add_kernel, [parts for _, parts in outputs], outs)
    return call(kernel, name, outs, micros, 8)(*arrays)


def join_kernel(first, second, out):
    count = first.shape[0]
    out[0:count] = first[...]
    out[count:] = second[...]


def joined(first, second):
    out = in_place((first.shape[0] + second.shape[0],) + first.shape[1:], first.dtype)
    return call(join_kernel, "joined", (out,), 0.1, 4)(first, second)[0]


def flipped(array, axis, bit):
    return lax.ppermute(array, axis, [(i, i ^ bit) for i in range(lax.axis_size(axis))])


def place_of(index, count):
    bits = count.bit_length() - 1
    return sum(((index >> k) & 1) << (bits - 1 - k) for k in range(bits))


def stack_kernel(*refs):
    for j, ref in enumerate(refs[:-1]):
        refs[-1][j] = ref[...]


def stacked(*arrays):
    out = in_place((len(arrays),) + arrays[0].shape, arrays[0].dtype)
    return call(stack_kernel, "stacked", (out,), 0.1, 4)(*arrays)[0]


def line_kernel(ways, *refs):
    first, second_got, totals, totals_got = refs[:ways], refs[ways : ways + 2], refs[ways + 2], refs[ways + 3]
    first_out, line_out, *second_out = refs[ways + 4 :]
    depth, piece, width = first_out.shape
    for j in range(depth):
        first_out[j] = sum(part[j].astype(F32) for part in first).astype(BF16)
        total = sum(part[depth + j].astype(F32) for part in first)
        line_out[j * piece : (j + 1) * piece, :] = total.astype(BF16)
        for d, out in enumerate(second_out):
            total = sum(part[d * depth + j].astype(F32) for part in second_got)
            out[j] = total.astype(BF16)
    low = (totals[...] + totals_got[...]).astype(BF16)
    edge = depth * piece
    line_out[edge : edge + NSMALL_ROWS, :] = low[:, 0:width]
    line_out[edge + NSMALL_ROWS :, :] = low[:, width:]


def flat_kernel(first, line, line_got, *refs):
    depth, share, width = first.shape
    second, (keep_out, send_out) = refs[:-2], refs[-2:]
    for j in range(depth):
        rows = slice(j * share, (j + 1) * share)
        left = first[j].astype(F32) + line_got[rows, :].astype(F32)
        right = sum(part[j].astype(F32) for part in second)
        if j % 2:
            out = slice(j // 2 * share, (j // 2 + 1) * share)
            send_out[out, 0:width] = left.astype(BF16)
            send_out[out, width:] = right.astype(BF16)
        else:
            keep_out[j // 2, :, 0:width] = left.astype(BF16)
            keep_out[j // 2, :, width:] = right.astype(BF16)
    edge, small = (depth * share, NSMALL_ROWS)
    low = (line[edge:, :].astype(F32) + line_got[edge:, :].astype(F32)).astype(BF16)
    send_out[depth // 2 * share :, 0:width] = low[0:small]
    send_out[depth // 2 * share :, width:] = low[small:]


def halve_kernel(keep, sent, got, keep_out, send_out):
    count, share, _ = keep.shape
    for j in range(count):
        rows = slice(j * share, (j + 1) * share)
        total = (keep[j].astype(F32) + got[rows, :].astype(F32)).astype(BF16)
        if j % 2:
            send_out[j // 2 * share : (j // 2 + 1) * share, :] = total
        else:
            keep_out[j // 2] = total
    low = sent[count * share :, :].astype(F32) + got[count * share :, :].astype(F32)
    send_out[count // 2 * share :, :] = low.astype(BF16)


def mine_kernel(keep, sent, got, out):
    share = keep.shape[1]
    out[0:share, :] = (keep[0].astype(F32) + got[0:share, :].astype(F32)).astype(BF16)
    out[share:, :] = (sent[share:, :].astype(F32) + got[share:, :].astype(F32)).astype(BF16)


def feed_line_kernel(*refs):
    depth = refs[0].shape[0]
    height = refs[0].shape[1]
    parts, outs = refs[:-depth], refs[-depth:]
    for j, out in enumerate(outs):
        out[0:height, :] = sum(part[j].astype(F32) for part in parts[:2]).astype(BF16)
        out[height:, :] = sum(part[j].astype(F32) for part in parts[2:]).astype(BF16)


def ordered_sum(parts, index):
    count = len(parts)
    total = 0.0
    for j in range(count):
        for d in range(count):
            total = total + jnp.where((index - d + count) % count == j, parts[d], 0.0)
    return total


def update_rest_kernel(place, owners, *refs):
    ways = len(refs) - 26
    shares = refs[:ways]
    attn, small, hidden = (refs[ways + k : ways + k + 4] for k in (0, 4, 8))
    attn_out, small_out, hidden_out = (refs[ways + k : ways + k + 4] for k in (12, 16, 20))
    grads, rows_held = refs[-2:]
    share = shares[0].shape[0] - NSMALL_ROWS
    width = shares[0].shape[1]
    for d in range(ways):
        grads[(place[3] - d + ways) % ways] = shares[d][0:share, :]
    totals = ordered_sum([part[share:, :].astype(F32) for part in shares], place[3])
    new = adamw(*[small[0][...], totals[0:NSMALL]], *[ref[...] for ref in small[1:]], SMALL_RATE, 0.0)
    for out, value in zip(small_out, new):
        out[...] = value
    rows_held[...] = totals[24:]
    units = hidden[0].shape[1]
    chunk = min(units, width)
    for j in range(units // chunk):
        offset = place[3] * units + j * chunk
        lanes = pl.ds(pl.multiple_of(offset % width, chunk), chunk)
        grad = rows_held[pl.ds(offset // width, 1), lanes]
        here = slice(j * chunk, (j + 1) * chunk)
        old = [ref[:, here] for ref in hidden]
        new = adamw(old[0], grad, *old[1:], SMALL_RATE, 0.0)
        for out, value in zip(hidden_out, new):
            out[:, here] = value
    seat = (place[0] * 2 + place[1]) * 2 + place[2]
    parts = TILE // share
    held = sum(jnp.where(owners[i] == seat, 1, 0) for i in range(TILES))
    for k in range(CAP):
        for part in range(parts):
            rows = slice(part * share, (part + 1) * share)
            grad = grads[k * parts + part].astype(F32)
            old = [ref[k, rows, :] for ref in attn]
            new = adamw(old[0], grad, *old[1:], MATRIX_RATE, MATRIX_DECAY)
            for out, value in zip(attn_out, new):
                out[k, rows, :] = jnp.where(held > k, value, 0.0)


def in_grad_kernel(incoming, frames, middle_grad, small, in_grad_out):
    size = CHUNK

    def step_of(step, carry):
        rows = pl.ds(pl.multiple_of(step * size, size), size)
        unit, inverse = normal_parts(frames[rows, :].astype(F32))
        back = normal_back(unit, inverse, incoming[rows, :], small[0:1, :])
        in_grad_out[rows, :] = (middle_grad[rows, :] + back).astype(BF16)
        return carry

    lax.fori_loop(0, incoming.shape[0] // size, step_of, 0)


def in_vmem(count):
    return [pl.BlockSpec(memory_space=pltpu.VMEM)] * count


def in_smem(count):
    return [pl.BlockSpec(memory_space=pltpu.SMEM)] * count


def shape(dims, kind):
    return jax.ShapeDtypeStruct(dims, kind)


def swap(array, axis):
    return lax.ppermute(array, axis, [(0, 1), (1, 0)])


def shifted(array, axis, distance):
    count = lax.axis_size(axis)
    return lax.ppermute(array, axis, [(i, (i + distance) % count) for i in range(count)])


def added(*parts):
    return functools.reduce(jnp.add, [part.astype(F32) for part in parts])


def together(*arrays):
    return lax.optimization_barrier(arrays)


def cost(micros):
    return pl.CostEstimate(
        flops=int(micros * 1.1e9), bytes_accessed=int(micros * 3.6e6), transcendentals=0
    )


def far_away(array):
    return pltpu.with_memory_space_constraint(array, pltpu.HBM)


def call(kernel, name, outs, micros, limit, scratch=(), smem=0, fetched=()):
    def run(*arrays):
        arrays = list(arrays[:smem]) + [
            far_away(array) if index in fetched else kept(array)
            for index, array in enumerate(arrays[smem:])
        ]
        return pl.pallas_call(
            kernel,
            out_shape=tuple(outs),
            in_specs=in_smem(smem) + in_vmem(len(arrays) - smem),
            out_specs=tuple(in_vmem(len(outs))),
            scratch_shapes=list(scratch),
            compiler_params=pltpu.CompilerParams(vmem_limit_bytes=limit * 1024 * 1024),
            cost_estimate=cost(micros),
            name=name,
        )(*arrays)

    return run


def kept(array):
    return pltpu.with_memory_space_constraint(array, pltpu.VMEM)


def in_place(dims, kind):
    return pltpu.VMEM(dims, kind)


def feed(place, slabs, first_matrix, second_matrix, bias, second, grad_rows, second_t, grad_t, *sums):
    ways, _, units = first_matrix.shape
    rows, width = second.shape
    block = min(FF_BLOCK, units)
    grads = in_place((ways, 2, slabs, width // slabs // 2, units), BF16)
    return call(
        functools.partial(feed_kernel, not sums),
        "feed",
        (
            grads,
            grads,
            in_place((ways, 1, units), F32),
            in_place((rows, width), F32),
            in_place((rows, width), F32),
        ),
        14,
        8,
        (
            pltpu.VMEM((width, block), BF16),
            pltpu.VMEM((width, block), BF16),
            pltpu.VMEM((rows, block), BF16),
            pltpu.VMEM((rows, block), BF16),
        ),
        smem=1,
    )(place, first_matrix, second_matrix, bias, second, grad_rows, second_t, grad_t, *sums)


def update_feed(place, core_away, y_away, column, states, done=()):
    depth, height, units = column.shape
    anywhere = pl.BlockSpec(memory_space=pl.ANY)
    return pl.pallas_call(
        functools.partial(update_kernel, core_away, y_away),
        out_shape=tuple(shape(state.shape, F32) for state in states),
        in_specs=in_smem(1) + in_vmem(1) + [anywhere] * (4 + len(done)),
        out_specs=(anywhere,) * 4,
        input_output_aliases={6 + j: j for j in range(len(done))},
        scratch_shapes=[
            pltpu.VMEM((depth, 4, height, units), F32),
            pltpu.VMEM((depth, 4, height, units), F32),
            pltpu.SemaphoreType.DMA((depth, 4)),
            pltpu.SemaphoreType.DMA((depth, 4)),
        ],
        compiler_params=pltpu.CompilerParams(vmem_limit_bytes=12 * 1024 * 1024),
        cost_estimate=cost(0.3),
        name="update_feed",
    )(place, kept(column), *[far_away(state) for state in states], *done)


def shards(
    frames,
    cotangent,
    lengths,
    owners,
    attn_master,
    attn_first,
    attn_second,
    attn_average,
    small_master,
    small_first,
    small_second,
    small_average,
    mlp_master,
    mlp_first,
    mlp_second,
    mlp_average,
    bias_master,
    bias_first,
    bias_second,
    bias_average,
):
    local, width = frames.shape
    wide = local + 2 * KEY_RIM
    rows = local + 2 * ROW_RIM
    blocks = rows // QUERY_BLOCK
    assert blocks * QUERY_BLOCK == rows and local % CHUNK == 0
    units = mlp_master.shape[2]
    ways = lax.axis_size("mlp")
    depth = lax.axis_size("z")
    devices = lax.axis_size(GROUPS)
    share = CAP * TILE // ways
    way = lax.axis_index("mlp")
    place = jnp.stack([lax.axis_index(name) for name in GROUPS + (GROUPS,)]).astype(jnp.int32)

    last = local // KEY_RIM - 1
    last_cot = local // ROW_RIM - 1
    rim = KEY_RIM + ROW_RIM
    first_tile, second_tile, to_next, to_past = pl.pallas_call(
        edges_kernel,
        grid=(1,),
        out_shape=(
            in_place((TILE, width), BF16),
            in_place((TILE, width), BF16),
            in_place((rim, width), BF16),
            in_place((rim, width), BF16),
        ),
        in_specs=[
            pl.BlockSpec((CAP, TILE, width), lambda i: (0, 0, 0)),
            pl.BlockSpec((KEY_RIM, width), lambda i: (0, 0)),
            pl.BlockSpec((KEY_RIM, width), lambda i: (last, 0)),
            pl.BlockSpec((ROW_RIM, width), lambda i: (0, 0)),
            pl.BlockSpec((ROW_RIM, width), lambda i: (last_cot, 0)),
        ],
        out_specs=tuple(in_vmem(4)),
        compiler_params=pltpu.CompilerParams(vmem_limit_bytes=8 * 1024 * 1024),
        cost_estimate=cost(1),
        name="edges",
    )(*[far_away(array) for array in (attn_master, frames, frames, cotangent, cotangent)])
    second_tile_y = swap(second_tile, "y")
    pair_b = stacked(second_tile, second_tile_y)[None]
    bits = [1 << k for k in range(depth.bit_length() - 1)][::-1]
    column_a, column_b = (first_tile[None], pair_b)

    up = [(i, i + 1) for i in range(devices - 1)]
    down = [(i + 1, i) for i in range(devices - 1)]
    before = lax.ppermute(to_next, GROUPS, up)
    after = lax.ppermute(to_past, GROUPS, down)

    edges = (before, after)
    for bit in bits[:-1]:
        got_a, got_b = (flipped(column_a, "z", bit), flipped(column_b, "z", bit))
        column_a = joined(column_a, got_a)
        column_a, column_b, edges, place_late = together(column_a, column_b, edges, place)
        column_b = joined(column_b, got_b)
    before, after = edges

    bias_row = bias_master.reshape(1, units)
    cut_rows = width // 2
    half = pl.pallas_call(
        half_kernel,
        grid_spec=pltpu.PrefetchScalarGridSpec(
            num_scalar_prefetch=1,
            grid=(2,),
            in_specs=[
                pl.BlockSpec((1, cut_rows, units), lambda i, place: (place[2], i, 0)),
                pl.BlockSpec((1, units), lambda i, place: (0, 0)),
            ],
            out_specs=pl.BlockSpec(memory_space=pltpu.VMEM),
        ),
        out_shape=in_place((width + 16, units), BF16),
        compiler_params=pltpu.CompilerParams(vmem_limit_bytes=8 * 1024 * 1024),
        cost_estimate=cost(1),
        name="half",
    )(place_late, far_away(mlp_master), bias_row)
    half_got = [shifted(half, "mlp", d) for d in range(1, ways)]
    column_a = joined(column_a, flipped(column_a, "z", 1))
    column_a, mlp_late = together(column_a, mlp_master)
    column_a_y = swap(column_a, "y")
    low_mlp = pl.pallas_call(
        matrices_kernel,
        grid=(2,),
        out_shape=in_place((2, width, units), BF16),
        in_specs=[pl.BlockSpec((2, cut_rows, units), lambda i: (0, i, 0))],
        out_specs=pl.BlockSpec(memory_space=pltpu.VMEM),
        compiler_params=pltpu.CompilerParams(vmem_limit_bytes=12 * 1024 * 1024),
        cost_estimate=cost(0.5),
        name="matrices",
    )(far_away(mlp_late))

    height = -(-max(-(-wide // 128), blocks) // 8) * 8
    cols, codes = pl.pallas_call(
        tables_kernel,
        out_shape=(in_place((wide, 8), F32), in_place((height, 128), F32)),
        in_specs=in_smem(2),
        out_specs=tuple(in_vmem(2)),
        cost_estimate=cost(1),
        name="tables",
    )(place, lengths)

    column_b_z = flipped(column_b, "z", 1)
    conv, first, wide_rows, cot, grad_rows, grad_t = call(
        conv_kernel,
        "norm_conv",
        (
            in_place((3, wide, width), BF16),
            in_place((wide, width), BF16),
            in_place((rows, width), BF16),
            in_place((rows, width), BF16),
            in_place((rows, width), BF16),
            in_place((width, local), BF16),
        ),
        0.5,
        6,
        (pltpu.VMEM((wide + 16, width), F32),),
        fetched=(1, 3),
    )(before, frames, after, cotangent, cols, small_master)

    column_b_z, column_a_y, conv, half_got, low_mlp = together(
        column_b_z, column_a_y, conv, half_got, low_mlp
    )
    away = [swap(column, "core") for column in (column_a, column_a_y, column_b, column_b_z)]
    tiles = [column_a, column_a_y] + away[:2] + [column_b, column_b_z] + away[2:]

    halves = half_got[0][None] if ways == 2 else stacked(*half_got)
    halves, tiles = together(halves, tiles)
    others = swap(halves, "core")
    weights, query, keys, values, probs, mixed = call(
        attend_kernel,
        "attend",
        (
            in_place((4 * width, width), BF16),
            in_place((wide, width), BF16),
            in_place((wide, width), BF16),
            in_place((wide, width), BF16),
            in_place((blocks, HEADS * QUERY_BLOCK, KEY_SPAN), F32),
            in_place((rows, width), BF16),
        ),
        0.5,
        8,
        smem=2,
    )(place, owners, *tiles, conv, cols, codes, small_master)
    others, mixed = together(others, mixed)
    middle, second, second_t = call(
        middle_kernel,
        "middle",
        (
            in_place((rows, width), F32),
            in_place((rows, width), BF16),
            in_place((width, local), BF16),
        ),
        20,
        8,
    )(mixed, weights, wide_rows, cols, small_master)

    rest = (second, grad_rows, second_t, grad_t)
    far_keep, far_send, far_bias, *sums = feed(
        place, 2 * depth, halves, others, bias_row, *rest
    )
    far_got = swap(far_send, "core")
    near_keep, near_send, near_bias, *sums = feed(
        place, 2 * depth, low_mlp[0][None], low_mlp[1][None], bias_row, *rest, *sums
    )
    near_got = swap(near_send, "core")
    pieces = range(1, ways)
    height = width // (4 * depth)

    def halves_of(array):
        return array.reshape(-1, height, units)

    def row(piece, half, y_away=0):
        return ((piece * 2 + half) * 2 + y_away) * depth

    far = add_into(
        "far_sum",
        (halves_of(far_keep), halves_of(far_got)),
        [(2 * depth, [(i, row(d - 1, 0)) for i in range(2)]) for d in pieces]
        + [(depth, [(i, row(d - 1, 1)) for i in range(2)]) for d in pieces]
        + [(depth, [(i, row(d - 1, 1, 1)) for i in range(2)]) for d in pieces],
        0.1,
    )
    far, sums = together(far, sums)
    far_x = [shifted(far[d - 1], "mlp", -d) for d in pieces]
    far_y = [swap(far[2 * (ways - 1) + d - 1], "y") for d in pieces]

    output, middle_grad, mixed_grad, out_grad, feed_rows = call(
        middle_back_kernel,
        "middle_back",
        (
            shape((local, width), BF16),
            in_place((local, width), F32),
            in_place((rows, width), BF16),
            in_place((width, width), BF16),
            in_place((32, width), F32),
        ),
        0.5,
        8,
        (pltpu.VMEM((rows, width), BF16),),
    )(middle, cot, grad_rows, *sums, mixed, weights, cols, small_master)

    near_keep, mixed_grad, far_y = together(near_keep, mixed_grad, far_y)
    near = add_into(
        "near_sum",
        (halves_of(near_keep), halves_of(near_got)),
        [(2 * depth, [(i, row(0, 0)) for i in range(2)])]
        + [(depth, [(i, row(0, 1, j)) for i in range(2)]) for j in range(2)],
        0.1,
    )
    near, mixed_grad = together(near, mixed_grad)
    near_y = swap(near[2], "y")

    columns = width // 2
    slabs = in_place((2 * ways * depth, share, columns), BF16)

    def scores_back(first_head, mixed_grad):
        return call(
            functools.partial(scores_back_kernel, first_head),
            "scores_back",
            (
                in_place((rows, columns), BF16),
                in_place((rows, columns), BF16),
                in_place((rows, columns), BF16),
                slabs,
                slabs,
            ),
            8,
            10,
            (
                pltpu.VMEM((wide, columns), F32),
                pltpu.VMEM((wide, columns), F32),
                pltpu.VMEM((4 * width, columns), BF16),
            ),
            smem=2,
        )(place, owners, query, keys, values, probs, mixed_grad, conv, out_grad)

    *grads_0, keep_0, send_0 = scores_back(0, mixed_grad)
    got_0 = swap(send_0, "core")

    arrays = (near[0], *far_x, near[1], near_y, *far[ways - 1 : 2 * (ways - 1)], *far_y)
    first_parts = list(range(ways))
    feed_two = add_into(
        "feed_two",
        arrays,
        [(depth, [(i, j * depth) for i in first_parts]) for j in range(2)]
        + [(depth, [(ways, 0), (ways + 1, 0)])]
        + [(depth, [(ways + 1 + d, 0), (2 * ways + d, 0)]) for d in pieces],
        0.1,
    )
    feed_two, mixed_grad, grads_0 = together(feed_two, mixed_grad, grads_0)
    feed_y = swap(feed_two[1], "y")
    feed_x = [shifted(feed_two[2 + d], "mlp", -d) for d in pieces]

    *grads_1, keep_1, send_1 = scores_back(HEADS // 2, mixed_grad)
    got_1 = swap(send_1, "core")
    paired_0 = add_into(
        "paired",
        (keep_0, got_0),
        [(2 * depth, [(i, 2 * depth * d) for i in range(2)]) for d in range(ways)],
        20,
    )
    feed_line = call(
        feed_line_kernel,
        "feed_line",
        tuple(in_place((2 * height, units), BF16) for _ in range(depth)),
        0.1,
        8,
    )(feed_two[0], feed_y, feed_two[2], *feed_x)
    paired_0, feed_line, keep_1, grads_1 = together(paired_0, feed_line, keep_1, grads_1)
    first_got = [shifted(paired_0[d], "mlp", -d) for d in range(1, ways)]
    feed_got = [shifted(feed_line[d], "z", d) for d in range(1, depth)]

    paired_1 = add_into(
        "paired",
        (keep_1, got_1),
        [(ways * depth, [(i, depth * j, 2 * depth) for i in range(2)]) for j in range(2)],
        0.1,
    )
    paired_1, grads_1 = together(paired_1, grads_1)
    second_got = swap(paired_1[1], "y")

    conv_grad = call(
        conv_grad_kernel, "conv_grad", (in_place((3, rows, width), F32),), 20, 8
    )(*grads_0, *grads_1, weights)[0]
    incoming, totals = call(
        conv_back_kernel,
        "conv_back",
        (in_place((local, width), F32), in_place((NSMALL_ROWS, width), F32)),
        12,
        8,
        (pltpu.VMEM((192, width), F32),),
        smem=1,
    )(
        place, grads_0[0], grads_0[2], grads_1[0], grads_1[2], conv_grad, first, frames, feed_rows,
         near_bias, far_bias, cols, small_master,
    )

    totals_got = swap(totals, "core")
    feed_keep, totals = together(feed_line[0], totals)
    feed_own = add_into(
        "feed_own",
        [part[None] for part in (feed_keep, *feed_got)],
        [(1, [(d, 0) for d in range(depth)])],
    )[0]
    feed_own, first_keep = together(feed_own, paired_0[0])
    feed_all = [shifted(feed_own[0], "z", d) for d in range(1, depth)]
    lined, line, *second = call(
        functools.partial(line_kernel, ways),
        "line",
        (
            in_place((depth, share, columns), BF16),
            in_place((depth * share + 2 * NSMALL_ROWS, columns), BF16),
        )
        + (in_place((depth, share, columns), BF16),) * ways,
        0.1,
        8,
    )(first_keep, *first_got, paired_1[0], second_got, totals, totals_got)
    lined, line, second, incoming = together(lined, line, second, incoming)
    line_got = swap(line, "y")
    second_x = [shifted(second[d], "mlp", -d) for d in range(1, ways)]
    in_grad = call(
        in_grad_kernel, "in_grad", (shape((local, width), BF16),), 20, 8, fetched=(1,)
    )(incoming, frames, middle_grad, small_master)[0]
    lined, in_grad = together(lined, in_grad)

    def slabs(count, extra):
        if extra:
            return in_place((count * share + NSMALL_ROWS, width), BF16)
        return in_place((count, share, width), BF16)

    count = depth // 2
    z_keep, z_sent = call(flat_kernel, "flat", (slabs(count, 0), slabs(count, 1)), 0.1, 8)(
        lined, line, line_got, second[0], *second_x
    )
    feed_own, z_keep, z_sent = together(feed_own, z_keep, z_sent)
    z_got = flipped(z_sent, "z", 1)
    feed_sums = [stacked(feed_own[0], *feed_all)]
    feed_sums.append(swap(feed_sums[0], "y"))
    feed_sums.append(swap(feed_sums[0], "core"))
    states = (mlp_master, mlp_first, mlp_second, mlp_average)
    mlp_new = update_feed(place, 0, 0, feed_sums[0], states)
    mlp_new, z_keep = together(mlp_new, z_keep)
    for bit in bits[::-1][1:]:
        count //= 2
        z_keep, z_sent = call(halve_kernel, "halve", (slabs(count, 0), slabs(count, 1)), 0.1, 8)(
            z_keep, z_sent, z_got
        )
        mlp_new, z_keep, z_sent = together(mlp_new, z_keep, z_sent)
        z_got = flipped(z_sent, "z", bit)
    mlp_new = update_feed(place, 1, 0, feed_sums[2], states, mlp_new)
    mlp_new, z_keep = together(mlp_new, z_keep)
    mine = call(mine_kernel, "mine", (in_place((share + NSMALL_ROWS, width), BF16),), 0.1, 8)(
        z_keep, z_sent, z_got
    )[0]
    mine, own_y, mlp_new = together(mine, feed_sums[1], mlp_new)
    shares = [mine] + [shifted(mine, "mlp", d) for d in range(1, ways)]
    other_y = swap(own_y, "core")
    mlp_new = update_feed(place, 0, 1, own_y, states, mlp_new)
    mlp_new, other_y, shares[0] = together(mlp_new, other_y, shares[0])
    mlp_new = update_feed(place, 1, 1, other_y, states, mlp_new)
    attn_shape = shape(attn_master.shape, F32)
    small_shape = shape(small_master.shape, F32)
    rest_new = call(
        update_rest_kernel,
        "update_rest",
        (attn_shape,) * 4 + (small_shape,) * 4 + (shape((1, units), F32),) * 4,
        3,
        12,
        (pltpu.VMEM((ways, share, width), BF16), pltpu.VMEM((8, width), F32)),
        smem=2,
    )(
        place, owners, *shares, attn_master, attn_first, attn_second, attn_average,
        small_master, small_first, small_second, small_average,
        *[state.reshape(1, units) for state in (bias_master, bias_first, bias_second, bias_average)],
    )

    bias_new = [part.reshape(units) for part in rest_new[8:]]
    return (
        output,
        in_grad,
        *rest_new[:8],
        *mlp_new,
        *bias_new,
    )


def solution(mesh):
    seq, mlp = mesh.devices.shape
    grid = Mesh(mesh.devices.reshape(seq // 4, 2, 2, mlp), GROUPS)
    rows = P(GROUPS, None)
    tiles = P(SEATS, None, None)
    units = P(None, None, "mlp")
    bias = P("mlp")
    in_specs = (
        (rows, rows, P(), P()) + (tiles,) * 4 + (P(),) * 4 + (units,) * 4 + (bias,) * 4
    )
    out_specs = (rows, rows) + (tiles,) * 4 + (P(),) * 4 + (units,) * 4 + (bias,) * 4
    return jax.shard_map(shards, mesh=grid, in_specs=in_specs, out_specs=out_specs, check_vma=False)
```
